768 devices in a mesh: mesh: 96 (over z, x, core), sub: 8 (over y).
Axes of the slice: x: 4, y: 8, z: 12, core: 2. Of those that a mesh axis runs over, the one named last changes fastest.
Arguments:
- state: float32 [56, 9, 98304], P(None, None, ('mesh', 'sub')), may hold values from -6 to 6
- scales: float32 [98304], P(('mesh', 'sub')), may hold values from 0.5 to 2
- stiffness: float32 [3, 56, 56], replicated, may hold values from -0.75 to 0.75
- jacobians: float32 [3, 9, 9], replicated, may hold values from -2 to 2
- projection: float32 [4, 21, 56], replicated, may hold values from -0.75 to 0.75
- lifting: float32 [4, 56, 21], replicated, may hold values from -1.25 to 1.25
- flux_matrix: float32 [9, 9], replicated, may hold values from -2 to 2
- peer_send: int32 [768, 8, 8], P(('mesh', 'sub')), may hold values from -1 to 511, as said below
- peer_recv: int32 [768, 8, 8], P(('mesh', 'sub')), may hold values from -1 to 511, as said below
- edge_send: int32 [768, 2, 32], P(('mesh', 'sub')), may hold values from -1 to 511, as said below
- edge_recv: int32 [768, 2, 32], P(('mesh', 'sub')), may hold values from -1 to 511, as said below
- uplift_map: float32 [504, 256], replicated, may hold values from -0.25 to 0.25
- fault_elem: int32 [49152], P(('mesh', 'sub')), may hold values from 0 to 127
- fault_dest: int32 [49152, 1], P(('mesh', 'sub')), may hold values from 0 to 7; in each aligned block of 64 rows (0 to 63, 64 to 127, ...) at most 16 rows name the same one
- fault_row: int32 [49152], P(('mesh', 'sub')), may hold values from 0 to 63
- fault_slip: int32 [49152], P(('mesh', 'sub')), may hold values 0 or 1
- sea_level: float32 [6144, 2048], P('mesh', 'sub'), may hold values from -6 to 6
- velocity: float32 [2, 6144, 2048], P(None, 'mesh', 'sub'), may hold values from -4 to 4
- depth: float32 [6144, 2048], P('mesh', 'sub'), may hold values from 0.5 to 2
Outputs:
- new_state: float32 [56, 9, 98304], P(None, None, ('mesh', 'sub'))
- sea_out: float32 [6144, 2048], P('mesh', 'sub')
- flow_out: float32 [2, 6144, 2048], P(None, 'mesh', 'sub')
The draws below stay inside these ranges and needn't reach their ends.
Inputs may be any that keep to these rules, and one draw needn't show every extreme that they name: `peer_send`: entry [d, p, j] is a face code of device d, or -1 for a padded slot; live slots come first in each block. Block [(m, s), p] holds as many live slots as block [(m, p), s] of peer_recv, and the block with p = s is full. `peer_recv`: entry [d, p, j] is a face code of device d, or -1 for a padded slot; live slots come first in each block, as many as in block [(m, p), s] of peer_send for d = (m, s). `edge_send`: entry [d, side, j] is a face code of device d, or -1 for a padded slot; live slots come first. Block [(m, s), 1] holds as many live slots as block [(m + 1, s), 0] of edge_recv, block [(m, s), 0] as many as block [(m - 1, s), 1] of edge_recv; blocks towards a missing neighbour are all -1. Block [(0, s), 1] is full. `edge_recv`: entry [d, side, j] is a face code of device d, or -1 for a padded slot; live slots come first, as many as in the matching block of edge_send. `fault_dest`: among the 64 fault faces of one device, at most 16 name the same column.
All inputs are finite; a program needn't handle non-finite values. No bound on the sum of `fault_slip` on one device may be relied on, other than what follows from the above.
Results may differ from the reference program's by a relative error of at most 0.0003.
Values sent between devices are 32-bit elements; how exact they have to be, the bound alone decides.
A program may use at most 64 MiB of HBM per device.

```python
import math
import jax
import jax.numpy as jnp
import numpy as np
from jax import lax

NBASIS = 56
NQ = 9
NFACEB = 21
ORDER = 5
ELEM_DEV = 128
SUB_SLOTS = 8
EDGE_SLOTS = 32
FAULT_DEV = 64
CAP = 16
TX = 64
TY = 256
SEA_STEPS = 2
ELEMS = 98304
FAULTS = 49152
NX = 6144
NY = 2048
N_MESH = 96
N_SUB = 8
DEVICES = 768


def peer_counts(key):
    counts = jax.random.randint(jax.random.fold_in(key, 11), (N_MESH, N_SUB, N_SUB), 1, SUB_SLOTS + 1)
    diagonal_mask = jnp.eye(N_SUB, dtype=jnp.int32)[None] > 0
    return jnp.where(diagonal_mask, SUB_SLOTS, counts).astype(jnp.int32)


def peer_codes(key, counts):
    face_codes = jax.random.randint(key, (N_MESH, N_SUB, N_SUB, SUB_SLOTS), 0, 4 * ELEM_DEV)
    slot_index = jnp.arange(SUB_SLOTS, dtype=jnp.int32)[None, None, None, :]
    live_slot = slot_index < counts[..., None]
    return jnp.where(live_slot, face_codes, -1).astype(jnp.int32).reshape(N_MESH * N_SUB, N_SUB, SUB_SLOTS)


def draw_peer_send(key, part):
    counts = peer_counts(key)
    key = jax.random.fold_in(key, 1)
    return peer_codes(key, counts)


def draw_peer_recv(key, part):
    counts = jnp.transpose(peer_counts(key), (0, 2, 1))
    key = jax.random.fold_in(key, 2)
    return peer_codes(key, counts)


def edge_counts(key):
    lowest = EDGE_SLOTS // 2
    upward = jax.random.randint(jax.random.fold_in(key, 21), (N_MESH, N_SUB), lowest, EDGE_SLOTS + 1)
    downward = jax.random.randint(jax.random.fold_in(key, 22), (N_MESH, N_SUB), lowest, EDGE_SLOTS + 1)
    upward = upward.at[0].set(EDGE_SLOTS)
    last_edge = (jnp.arange(N_MESH) == N_MESH - 1)[:, None]
    upward = jnp.where(last_edge, 0, upward).astype(jnp.int32)
    downward = jnp.where(last_edge, 0, downward).astype(jnp.int32)
    empty_row = jnp.zeros((1, N_SUB), jnp.int32)
    return (upward, downward, empty_row)


def edge_codes(key, first_side, second_side):
    face_codes = jax.random.randint(key, (N_MESH, N_SUB, 2, EDGE_SLOTS), 0, 4 * ELEM_DEV)
    sides = jnp.stack([first_side, second_side], 2)
    slot_index = jnp.arange(EDGE_SLOTS, dtype=jnp.int32)[None, None, None, :]
    live_slot = slot_index < sides[..., None]
    return jnp.where(live_slot, face_codes, -1).astype(jnp.int32).reshape(N_MESH * N_SUB, 2, EDGE_SLOTS)


def draw_edge_send(key, part):
    upward, downward, empty_row = edge_counts(key)
    key = jax.random.fold_in(key, 3)
    to_lower = jnp.concatenate([empty_row, downward[:-1]], 0)
    return edge_codes(key, to_lower, upward)


def draw_edge_recv(key, part):
    upward, downward, empty_row = edge_counts(key)
    key = jax.random.fold_in(key, 4)
    from_lower = jnp.concatenate([empty_row, upward[:-1]], 0)
    return edge_codes(key, from_lower, downward)


def touch_ends(values, rng, low, largest):
    dims = values.shape
    spot = [jax.random.randint(jax.random.fold_in(rng, axis), (), 0, dims[axis]) for axis in range(len(dims))]
    values = values.at[tuple(spot)].set(low)
    longest = dims.index(max(dims))
    spot[longest] = (spot[longest] + 1) % dims[longest]
    return values.at[tuple(spot)].set(largest)


def shard_levels(stream_key, dims, split, least, high):
    factor_of, own = 1.0, jax.random.fold_in(stream_key, 6)
    for dim, blocks in split:
        heights = jnp.exp(jax.random.uniform(jax.random.fold_in(own, dim), (blocks,), jnp.float32, least / len(split), high / len(split)))
        factor_of = factor_of * jnp.repeat(heights, dims[dim] // blocks).reshape([-1 if axis == dim else 1 for axis in range(len(dims))])
    return factor_of


def deal_out(rng, own, number, rows, number_of, top, most, lean):
    sequence = jax.random.permutation(rng, number_of)
    crowded, ordinary = shares(number_of, rows * top, most, lean, True), shares(number_of, rows * top, most, lean, False)
    places = jnp.arange(number_of)

    def named(tallies, turn):
        used = int((tallies > 0).sum())
        fixed = max(1, used // 4)
        passed = fixed + (places - fixed + turn * (used - fixed)) % max(1, number_of - fixed)
        return jnp.zeros((number_of,), jnp.int32).at[sequence[jnp.where(places < fixed, places, passed)]].set(jnp.asarray(tallies, jnp.int32))

    tallies = jnp.where(number % 4 == 0, named(crowded, number // 4), named(ordinary, number - number // 4 - 1))
    mixed = jax.random.permutation(jax.random.fold_in(own, 3), number_of)
    giver, receiver = mixed[0:number_of // 2 * 2:2], mixed[1:number_of // 2 * 2:2]
    slack = jnp.minimum(tallies[giver] - 1, most - tallies[receiver]) // 2
    slack = jnp.where((giver == sequence[0]) | (receiver == sequence[0]) | (tallies[receiver] == 0), 0, jnp.maximum(slack, 0))
    passed = jax.random.randint(jax.random.fold_in(own, 4), (number_of // 2,), 0, 1 << 20) % (slack + 1)
    tallies = tallies.at[giver].add(-passed).at[receiver].add(passed)
    items = jnp.searchsorted(jnp.cumsum(tallies), jnp.arange(rows * top), side="right").astype(jnp.int32)
    grid = items.reshape(top, rows).T
    grid = grid[jax.random.permutation(jax.random.fold_in(own, 1), rows)]
    turn = jax.random.randint(jax.random.fold_in(own, 2), (rows, 1), 0, top)
    return jnp.take_along_axis(grid, (jnp.arange(top)[None, :] + turn) % top, axis=1)


def shares(count, total, most, skew, full):
    loads = [(1 << 20) // math.isqrt(rank ** skew) + 1 for rank in range(1, count + 1)]
    largest = most if full else min(most, max(-(-total // count), total * loads[0] // sum(loads)))
    least = 1 if total - largest >= count - 1 else 0
    given, surplus = [largest] + [least] * (count - 1), total - largest - least * (count - 1)
    while surplus > 0:
        movable = [i for i in range(1, count) if given[i] < largest] or [i for i in range(1, count) if given[i] < most]
        pool, left = sum([loads[i] for i in movable]), surplus
        for i in movable:
            more = min(most - given[i], max(1, left * loads[i] // pool), surplus)
            given[i] = given[i] + more
            surplus = surplus - more
    return np.array(given)


def normal_values(rng, extent, scale, reach, cuts=(), held_as=jnp.bfloat16):
    values = jax.random.normal(rng, extent, jnp.float32) * scale
    if len(cuts) > 0:
        values = shard_levels(rng, extent, cuts, -0.22, 0.18) * values
    return jnp.clip(values, min=-reach, max=reach).astype(held_as)


def setup_inputs(seed: int = 0) -> dict:
    key_list = jax.random.split(jax.random.key(seed), 20)
    state = normal_values(key_list[0], (NBASIS, NQ, ELEMS), 1.0, 6.0, ((2, 768),), jnp.float32)
    scales = jnp.clip(jnp.exp(math.log(2.0) - 1.3862944 * jax.random.uniform(key_list[1], (ELEMS,), jnp.float32) ** shard_levels(key_list[1], (ELEMS,), ((0, 768),), -0.2, 0.2)), 0.5, 2.0)
    stiffness = normal_values(key_list[2], (3, NBASIS, NBASIS), NBASIS ** -0.5, 0.75, (), jnp.float32)
    jacobians = normal_values(key_list[3], (3, NQ, NQ), NQ ** -0.5, 2.0, (), jnp.float32)
    projection = normal_values(key_list[4], (4, NFACEB, NBASIS), NBASIS ** -0.5, 0.75, (), jnp.float32)
    lifting = normal_values(key_list[5], (4, NBASIS, NFACEB), NFACEB ** -0.5, 1.25, (), jnp.float32)
    flux_matrix = normal_values(key_list[6], (NQ, NQ), NQ ** -0.5, 2.0, (), jnp.float32)
    peer_send = draw_peer_send(jax.random.fold_in(key_list[19], 71), 0)
    peer_recv = draw_peer_recv(jax.random.fold_in(key_list[19], 71), 0)
    edge_send = draw_edge_send(jax.random.fold_in(key_list[19], 71), 0)
    edge_recv = draw_edge_recv(jax.random.fold_in(key_list[19], 71), 0)
    uplift_map = normal_values(key_list[11], (NBASIS * NQ, TY), (NBASIS * NQ) ** -0.5, 0.25, (), jnp.float32)
    fault_elem = touch_ends(jax.random.randint(key_list[12], (FAULTS,), 0, ELEM_DEV), jax.random.fold_in(key_list[12], 1), 0, ELEM_DEV - 1).astype(jnp.int32)
    fault_dest_keys = jax.random.split(jax.random.fold_in(key_list[13], 1), FAULTS // FAULT_DEV)
    fault_dest_turns = jax.random.permutation(jax.random.fold_in(key_list[13], 3), FAULTS // FAULT_DEV)
    fault_dest = jax.vmap(lambda own, number: deal_out(jax.random.fold_in(key_list[13], 2), own, number, FAULT_DEV, N_SUB, 1, CAP, 2))(fault_dest_keys, fault_dest_turns).reshape((FAULTS, 1))
    fault_row = touch_ends(jax.random.randint(key_list[14], (FAULTS,), 0, TX), jax.random.fold_in(key_list[14], 1), 0, TX - 1).astype(jnp.int32)
    fault_slip = touch_ends((jax.random.randint(key_list[15], (FAULTS,), 0, 2) < 1).astype(jnp.int32), jax.random.fold_in(key_list[15], 1), 0, 1)
    sea_level = normal_values(key_list[16], (NX, NY), 1.0, 6.0, ((0, 96), (1, 8)), jnp.float32)
    velocity = normal_values(key_list[17], (2, NX, NY), 0.5, 4.0, ((1, 96), (2, 8)), jnp.float32)
    depth = jnp.clip(jnp.exp(math.log(2.0) - 1.3862944 * jax.random.uniform(key_list[18], (NX, NY), jnp.float32) ** shard_levels(key_list[18], (NX, NY), ((0, 96), (1, 8)), -0.2, 0.2)), 0.5, 2.0)
    return {"state": state, "scales": scales, "stiffness": stiffness, "jacobians": jacobians, "projection": projection, "lifting": lifting, "flux_matrix": flux_matrix, "peer_send": peer_send, "peer_recv": peer_recv, "edge_send": edge_send, "edge_recv": edge_recv, "uplift_map": uplift_map, "fault_elem": fault_elem, "fault_dest": fault_dest, "fault_row": fault_row, "fault_slip": fault_slip, "sea_level": sea_level, "velocity": velocity, "depth": depth}


EXACT_PRECISION = lax.Precision.HIGHEST
EARTH_STEP = 0.5
COURANT = 0.45


def derivative(field_in, scales, stiffness, jacobians):
    summed = jnp.zeros(field_in.shape, jnp.float32)
    for direction in range(3):
        basis_mixed = jnp.einsum('cb,bqe->cqe', stiffness[direction], field_in, precision=EXACT_PRECISION)
        summed = summed + jnp.einsum('cpe,pq->cqe', basis_mixed, jacobians[direction], precision=EXACT_PRECISION)
    return summed * scales


def predictor(field_in, scales, stiffness, jacobians):
    factor = EARTH_STEP
    integral = factor * field_in
    current = field_in
    for power in range(1, ORDER):
        current = derivative(current, scales, stiffness, jacobians)
        factor = factor * EARTH_STEP / (power + 1)
        integral = integral + factor * current
    return integral


def face_select(face_codes):
    live_slot = face_codes >= 0
    element = jnp.where(live_slot, face_codes // 4, 0).astype(jnp.int32)
    select = ((face_codes % 4)[None, :] == jnp.arange(4, dtype=jnp.int32)[:, None]) & live_slot[None, :]
    return element, select.astype(jnp.float32)


def traces(integral, face_codes, projection):
    element, select = face_select(face_codes)
    picked = jnp.take(integral, element, axis=2)
    chosen_proj = jnp.einsum('fnb,fm->nbm', projection, select, precision=EXACT_PRECISION)
    return jnp.einsum('nbm,bqm->nqm', chosen_proj, picked, precision=EXACT_PRECISION)


def face_terms(integral, incoming, face_codes, projection, lifting, flux_matrix, element_count):
    element, select = face_select(face_codes)
    own_trace = traces(integral, face_codes, projection)
    face_flux = jnp.einsum('npm,pq->nqm', incoming - own_trace, flux_matrix, precision=EXACT_PRECISION)
    chosen_lift = jnp.einsum('fbn,fm->bnm', lifting, select, precision=EXACT_PRECISION)
    lifted = jnp.einsum('bnm,nqm->bqm', chosen_lift, face_flux, precision=EXACT_PRECISION)
    empty_sum = jnp.zeros((integral.shape[0], integral.shape[1], element_count), jnp.float32)
    return empty_sum.at[:, :, element].add(lifted)


def advance(padded, sea_flow):
    height_pad = padded[0]
    flux_rows = padded[1]
    flux_cols = padded[2]
    divergence = (flux_rows[2:, 1:-1] - flux_rows[:-2, 1:-1]) * 0.5 + (flux_cols[1:-1, 2:] - flux_cols[1:-1, :-2]) * 0.5
    height_cycle = height_pad[1:-1, 1:-1] - COURANT * divergence
    slope_rows = (height_cycle[2:, 1:-1] - height_cycle[:-2, 1:-1]) * 0.5
    slope_cols = (height_cycle[1:-1, 2:] - height_cycle[1:-1, :-2]) * 0.5
    new_flow = sea_flow - COURANT * jnp.stack([slope_rows, slope_cols])
    return height_cycle[1:-1, 1:-1], new_flow


def reference(state, scales, stiffness, jacobians, projection, lifting, flux_matrix, peer_send, peer_recv, edge_send, edge_recv, uplift_map, fault_elem, fault_dest, fault_row, fault_slip, sea_level, velocity, depth):
    state_dev = state.reshape(NBASIS, NQ, DEVICES, ELEM_DEV).transpose(2, 0, 1, 3)
    scale_dev = scales.reshape(DEVICES, ELEM_DEV)

    def element_work(block_pair):
        integral = predictor(block_pair[0], block_pair[1], stiffness, jacobians)
        return integral, derivative(integral, block_pair[1], stiffness, jacobians)

    integral_dev, volume_dev = lax.map(element_work, (state_dev, scale_dev))

    send_codes = jnp.concatenate([peer_send.reshape(DEVICES, -1), edge_send.reshape(DEVICES, -1)], 1)
    recv_codes = jnp.concatenate([peer_recv.reshape(DEVICES, -1), edge_recv.reshape(DEVICES, -1)], 1)
    peer_total = N_SUB * SUB_SLOTS

    sent = lax.map(lambda pair: traces(pair[0], pair[1], projection), (integral_dev, send_codes))
    sent_peer = sent[..., :peer_total].reshape(N_MESH, N_SUB, NFACEB, NQ, N_SUB, SUB_SLOTS)
    got_peer = sent_peer.transpose(0, 4, 2, 3, 1, 5).reshape(DEVICES, NFACEB, NQ, peer_total)
    sent_edge = sent[..., peer_total:].reshape(N_MESH, N_SUB, NFACEB, NQ, 2, EDGE_SLOTS)
    empty_rim = jnp.zeros((1, N_SUB, NFACEB, NQ, EDGE_SLOTS), jnp.float32)
    from_lower = jnp.concatenate([empty_rim, sent_edge[:-1, :, :, :, 1]], 0)
    from_upper = jnp.concatenate([sent_edge[1:, :, :, :, 0], empty_rim], 0)
    got_edge = jnp.stack([from_lower, from_upper], 4).reshape(DEVICES, NFACEB, NQ, 2 * EDGE_SLOTS)
    incoming = jnp.concatenate([got_peer, got_edge], 3)

    face_dev = lax.map(lambda trio: face_terms(trio[0], trio[1], trio[2], projection, lifting, flux_matrix, ELEM_DEV), (integral_dev, incoming, recv_codes))
    new_dev = state_dev + volume_dev + face_dev
    new_state = new_dev.transpose(1, 2, 0, 3).reshape(NBASIS, NQ, ELEMS)

    owner_device = jnp.arange(FAULTS, dtype=jnp.int32) // FAULT_DEV
    columns = jnp.take(new_state, owner_device * ELEM_DEV + fault_elem, axis=2).reshape(NBASIS * NQ, FAULTS)
    weighting = 0.3 + 0.7 * fault_slip.astype(jnp.float32)
    uplift_items = jnp.einsum('kf,kt->ft', columns, uplift_map, precision=EXACT_PRECISION) * weighting[:, None]
    tiles = sea_level.reshape(N_MESH, TX, N_SUB, TY)
    tiles = tiles.at[owner_device // N_SUB, fault_row, fault_dest[:, 0]].add(uplift_items)
    sea_height = tiles.reshape(NX, NY)
    sea_flow = velocity
    for substep in range(SEA_STEPS):
        stacked = jnp.concatenate([sea_height[None], depth[None] * sea_flow], 0)
        padded = jnp.pad(stacked, ((0, 0), (2, 2), (2, 2)))
        sea_height, sea_flow = advance(padded, sea_flow)
    return new_state, sea_height, sea_flow
```

```python
import functools

import jax
import jax.numpy as jnp
from jax import lax
from jax.experimental import pallas as pl
from jax.experimental.pallas import tpu as pltpu
from jax.sharding import PartitionSpec as P

ORDER = 5
CAP = 16
EARTH_STEP = 0.5
COURANT = 0.45
MESH = pl.DeviceIdType.MESH
F32, BF16, I32 = jnp.float32, jnp.bfloat16, jnp.int32
LANES = 128
FACE_ROWS = 24
INFO = 224
RIM = 4
DIRECTIONS = ((1, 0), (-1, 0), (0, 1), (0, -1), (1, 1), (1, -1), (-1, 1), (-1, -1))
WAY = {d: i for i, d in enumerate(DIRECTIONS)}


def split(x):
    high = x.astype(BF16)
    return high, (x - high.astype(F32)).astype(BF16)


def mm(a, b, left=1, right=0):
    return lax.dot_general(a, b, (((left,), (right,)), ((), ())), preferred_element_type=F32)


def iota(shape, axis):
    return lax.broadcasted_iota(I32, shape, axis)


def repeat_rows(rows, count):
    return jnp.concatenate(
        [jnp.broadcast_to(rows[i : i + 1], (count, rows.shape[1])) for i in range(rows.shape[0])], 0
    )


def as_column(rows, first=0):
    count = rows.shape[1] if first == 0 else CAP
    wide = repeat_rows(rows, count)
    mine = (iota(wide.shape, 0) & (count - 1)) == iota(wide.shape, 1) - first
    return jnp.sum(jnp.where(mine, wide, 0.0), axis=1, keepdims=True)


def pack_edge(array, last, base):
    lane = iota((8, LANES), 1)
    start = array.shape[1] - LANES if last else 0
    keep = lane >= LANES - RIM if last else lane < RIM
    packed = jnp.zeros((8, LANES), F32)
    for g in range(array.shape[0] // 8):
        tile = jnp.where(keep, array[8 * g : 8 * g + 8, start : start + LANES], 0.0)
        packed = packed + pltpu.roll(tile, (RIM * (g + 1 if last else g) + base) % LANES, 1)
    return packed


def extend(array, low, high, left, right, corners, base):
    lane, row = iota((8, LANES), 1), iota((8, LANES), 0)
    side = jnp.concatenate(
        [
            jnp.where(
                lane < LANES // 2,
                pltpu.roll(right, (-RIM * g - base) % LANES, 1),
                pltpu.roll(left, (LANES - RIM - RIM * g - base) % LANES, 1),
            )
            for g in range(array.shape[0] // 8)
        ],
        0,
    )
    down_right, down_left, up_right, up_left = corners
    corner = jnp.where(
        row < RIM,
        jnp.where(lane < LANES // 2, down_right, down_left),
        jnp.where(lane < LANES // 2, up_right, up_left),
    )
    bottom = jnp.where(iota(low.shape, 0) < RIM, high, low)
    return jnp.concatenate(
        [jnp.concatenate([array, side], 1), jnp.concatenate([bottom, corner], 1)], 0
    )


def shifted(array, axis):
    size = array.shape[axis]
    return (pltpu.roll(array, size - 1, axis) - pltpu.roll(array, 1, axis)) * 0.5


def kernel(mesh_count, sub_count, *refs):
    (
        state_in, scales_in, stiff_in, jac_in, proj_in, lift_in, flux_in,
        psend_in, precv_in, esend_in, erecv_in, uplift_in,
        felem_in, fdest_in, frow_in, fslip_in, sea_in, vel_in, depth_in,
        new_out, sea_out, flow_out,
        state, scales, stiff, jac, proj, lift, flux,
        psend, precv, esend, erecv, uplift,
        felem, fdest, frow, fslip, sea, vel, depth,
        matrix, matrix_hi, matrix_lo, faces, lifts, traces_out, traces_in, items_out, items_in,
        rows_out, cols_out, rows_in, cols_in, corner_in,
        height, hcols_out, hrows_in, hcols_in, hcorner_in, new, sea_buf, flow_buf,
        load_sem, store_sem, rim_send, rim_recv, trace_send, trace_recv,
        item_send, item_recv, high_send, high_recv,
    ) = refs
    quantities, basis = flux.shape[0], stiff.shape[1]
    width = quantities * basis
    padded = matrix.shape[0]
    elements = state.shape[1]
    slots = psend.shape[1]
    edge_slots = esend.shape[1]
    peer_total = sub_count * slots
    send_total = peer_total + 2 * edge_slots
    me, sub = lax.axis_index("mesh"), lax.axis_index("sub")

    def device(dm, ds):
        return (lax.rem(me + dm + mesh_count, mesh_count), lax.rem(sub + ds + sub_count, sub_count))

    loads = [
        pltpu.make_async_copy(src, dst, load_sem.at[i])
        for i, (src, dst) in enumerate(
            (
                (stiff_in, stiff), (jac_in, jac), (state_in, state), (scales_in, scales),
                (vel_in, vel), (depth_in, depth), (proj_in, proj), (flux_in, flux),
                (psend_in, psend), (precv_in, precv), (esend_in, esend), (erecv_in, erecv),
                (felem_in, felem), (fdest_in, fdest), (frow_in, frow), (fslip_in, fslip),
                (uplift_in, uplift), (lift_in, lift), (sea_in, sea),
            )
        )
    ]
    for load in loads:
        load.start()
    barrier = pltpu.get_barrier_semaphore()
    partners = [(0, k) for k in range(1, sub_count)] + [d for d in DIRECTIONS if d[0] != 0]
    for dm, ds in partners:
        pl.semaphore_signal(barrier, inc=1, device_id=device(dm, ds), device_id_type=MESH)

    def send(src, dst, send_sem, recv_sem, dm, ds):
        copy = pltpu.make_async_remote_copy(
            src_ref=src, dst_ref=dst, send_sem=send_sem, recv_sem=recv_sem,
            device_id=device(dm, ds), device_id_type=MESH,
        )
        copy.start()
        return copy

    lane = iota((1, padded), 1)
    of_quantity = sum((lane >= basis * k).astype(I32) for k in range(1, quantities + 1))
    of_basis = lane - basis * of_quantity
    spread_basis = (iota((basis, padded), 0) == of_basis).astype(F32).astype(BF16)
    spread_quantity = (iota((quantities, padded), 0) == of_quantity).astype(F32)
    loads[0].wait()
    loads[1].wait()
    stiff_hi, stiff_lo = split(stiff[...])
    stiff_wide = mm(stiff_hi, spread_basis) + mm(stiff_lo, spread_basis)
    jac_wide = [
        lax.dot_general(
            jac[:, d, :], spread_quantity, (((0,), (0,)), ((), ())),
            precision=lax.Precision.HIGHEST, preferred_element_type=F32,
        )
        for d in range(3)
    ]
    for q in range(quantities):
        block = stiff_wide[0:basis] * jac_wide[0][q : q + 1]
        for d in (1, 2):
            block = block + stiff_wide[d * basis : (d + 1) * basis] * jac_wide[d][q : q + 1]
        matrix[q * basis : (q + 1) * basis, :] = block
    matrix[width:, :] = jnp.zeros((padded - width, padded), F32)
    high, low = split(matrix[...])
    matrix_hi[...] = high
    matrix_lo[...] = low

    loads[4].wait()
    loads[5].wait()
    tile_rows, tile_cols = depth.shape
    for i, first in enumerate((tile_rows - 8, 0)):
        rows_out[i, 0:2] = vel[:, first : first + 8, :]
        rows_out[i, 2] = depth[first : first + 8, :]
    fields = (vel[0], vel[1], depth[...])
    group = RIM * (tile_rows // 8)
    for i, last in enumerate((True, False)):
        packed = pack_edge(fields[0], last, 0)
        for k in (1, 2):
            packed = packed + pack_edge(fields[k], last, k * group)
        cols_out[i] = packed
    pl.semaphore_wait(barrier, len(partners))

    def corner_of(ds):
        return slice(tile_cols - LANES, tile_cols) if ds > 0 else slice(0, LANES)

    rim_copies = []
    for i, (dm, ds) in enumerate(DIRECTIONS):
        if ds == 0:
            src, dst = rows_out.at[i], rows_in.at[i]
        elif dm == 0:
            src, dst = cols_out.at[i - 2], cols_in.at[i - 2]
        else:
            src = rows_out.at[0 if dm > 0 else 1, :, :, corner_of(ds)]
            dst = corner_in.at[i - 4]
        rim_copies.append(send(src, dst, rim_send.at[i], rim_recv.at[i], dm, ds))

    loads[2].wait()
    loads[3].wait()
    scale = scales[...]

    def derivative(x):
        x_hi, x_lo = split(x)
        both = mm(matrix_hi[...], jnp.concatenate([x_hi, x_lo], 1))
        return (both[:, :elements] + both[:, elements:] + mm(matrix_lo[...], x_hi)) * scale

    start = jnp.concatenate([state[...], jnp.zeros((padded - width, elements), F32)], 0)
    factor = EARTH_STEP
    integral = factor * start
    current = start
    for power in range(1, ORDER):
        current = derivative(current)
        factor = factor * EARTH_STEP / (power + 1)
        integral = integral + factor * current

    for i in (6, 7, 8, 9, 10, 11):
        loads[i].wait()
    codes = jnp.concatenate(
        [as_column(ref[...].astype(F32)) for ref in (psend, esend, precv, erecv)], 0
    )
    face_lane = iota((1, 4 * elements), 1)
    key = (4 * (face_lane & (elements - 1)) + face_lane // elements).astype(F32)
    hot = (codes == key).astype(F32).astype(BF16)

    faces[...] = jnp.zeros(faces.shape, F32)
    for f in range(4):
        faces[f * FACE_ROWS : f * FACE_ROWS + proj.shape[0], :] = proj[:, f, :]
    faces_hi, faces_lo = split(faces[...])
    parts = [integral[p * basis : (p + 1) * basis] for p in range(quantities)]
    mixed = []
    for q in range(quantities):
        total = flux[0, q] * parts[0]
        for p in range(1, quantities):
            total = total + flux[p, q] * parts[p]
        mixed.append(total)
    mixed_hi, mixed_lo = split(jnp.concatenate(mixed, 1))
    every = mm(faces_hi, mixed_hi) + mm(faces_hi, mixed_lo) + mm(faces_lo, mixed_hi)
    face_width = quantities * FACE_ROWS
    trace_rows = traces_out.shape[1]

    def face_block(f, q):
        return every[f * FACE_ROWS : (f + 1) * FACE_ROWS, q * elements : (q + 1) * elements]

    table = jnp.concatenate(
        [jnp.concatenate([face_block(f, q) for q in range(quantities)], 0) for f in range(4)], 1
    )
    table = jnp.concatenate([table, jnp.zeros((trace_rows - face_width, 4 * elements), F32)], 0)
    table_hi, table_lo = split(table)
    picked = mm(hot, table_hi, 1, 1) + mm(hot, table_lo, 1, 1)

    for i in (12, 13, 14, 15):
        loads[i].wait()
    fault_count = fdest.shape[1]
    square = (fault_count, fault_count)
    dest_row = fdest[...].astype(F32)
    dest_col = as_column(dest_row)
    same = dest_col == dest_row
    rank_row = jnp.sum(
        jnp.where(same & (iota(square, 0) < iota(square, 1)), 1.0, 0.0), axis=0, keepdims=True
    )
    rank_col = jnp.sum(
        jnp.where(same & (iota(square, 1) < iota(square, 0)), 1.0, 0.0), axis=1, keepdims=True
    )
    row_numbers = frow[...].astype(F32) + 1.0
    info_left = jnp.where(
        dest_row == (iota((peer_total, fault_count), 0) // slots).astype(F32), row_numbers, 0.0
    )
    info_lane = INFO % LANES
    info_right = (
        rank_col == (iota((fault_count, LANES), 1) - info_lane).astype(F32)
    ).astype(F32)
    info = mm(info_left.astype(BF16), info_right.astype(BF16)) - 1.0
    info_lanes = iota((peer_total, LANES), 1)
    info_here = (info_lanes >= info_lane) & (info_lanes < info_lane + CAP)

    traces_out[:, 0:LANES] = picked[0:send_total, 0:LANES]
    traces_out[0:peer_total, LANES:] = jnp.where(
        info_here, info, picked[0:peer_total, LANES:]
    )
    traces_out[peer_total:, LANES:] = picked[peer_total:send_total, LANES:]
    own_trace = picked[send_total:]

    def peer_block(index, rows):
        return pl.ds(pl.multiple_of(index * rows, rows), rows)

    order = sorted(range(1, sub_count), key=lambda k: -min(k, sub_count - k))
    trace_copies = []
    for k in order:
        _, peer = device(0, k)
        trace_copies.append(
            send(
                traces_out.at[peer_block(peer, slots), :], traces_in.at[peer_block(sub, slots), :],
                trace_send.at[k], trace_recv.at[k], 0, k,
            )
        )
    for i, dm in enumerate((1, -1)):
        source = peer_total + (edge_slots if dm > 0 else 0)
        target = peer_total + (0 if dm > 0 else edge_slots)
        trace_copies.append(
            send(
                traces_out.at[source : source + edge_slots, :],
                traces_in.at[target : target + edge_slots, :],
                trace_send.at[sub_count + i], trace_recv.at[sub_count + i], dm, 0,
            )
        )
    own_block = pltpu.make_async_copy(
        traces_out.at[peer_block(sub, slots), :], traces_in.at[peer_block(sub, slots), :],
        trace_recv.at[0],
    )
    own_block.start()

    base = start + derivative(integral)
    loads[17].wait()
    lifts[...] = jnp.zeros(lifts.shape, F32)
    for f in range(4):
        lifts[f * FACE_ROWS : f * FACE_ROWS + lift.shape[0], :] = lift[:, f, :]
    lift_hi, lift_lo = split(jnp.transpose(lifts[...]))
    hot_in = hot[send_total:]

    loads[16].wait()
    rows_here = iota((padded, 1), 0)
    row_quantity = sum((rows_here >= basis * k).astype(I32) for k in range(1, quantities + 1))
    wanted = (rows_here - basis * row_quantity) * quantities + row_quantity
    wanted = jnp.where(rows_here < width, wanted, -1)
    permute = (iota((padded, width), 1) == wanted).astype(F32).astype(BF16)
    uplift_hi, uplift_lo = split(uplift[...])
    uplift_hi = mm(permute, uplift_hi).astype(BF16)
    uplift_lo = mm(permute, uplift_lo).astype(BF16)

    item_slots = sub_count * CAP
    place = (
        iota((item_slots, fault_count), 0).astype(F32) == dest_row * float(CAP) + rank_row
    ).astype(F32)
    elem_col = as_column(felem[...].astype(F32))
    elem_hot = (elem_col == iota((fault_count, elements), 1).astype(F32)).astype(F32)
    choose = mm(place.astype(BF16), elem_hot.astype(BF16)).astype(BF16)
    weighting = 0.3 + 0.7 * fslip[...].astype(F32)
    weight_col = jnp.sum(place * weighting, axis=1, keepdims=True)

    for copy in rim_copies:
        copy.wait_recv()

    def corners_of(ref, k=None):
        return [
            ref[WAY[way] - 4] if k is None else ref[WAY[way] - 4, k]
            for way in ((-1, -1), (-1, 1), (1, -1), (1, 1))
        ]

    extended = [
        extend(
            fields[k], rows_in[WAY[(1, 0)], k], rows_in[WAY[(-1, 0)], k],
            cols_in[0], cols_in[1], corners_of(corner_in, k), k * group,
        )
        for k in range(3)
    ]
    shape = extended[0].shape
    ext_row, ext_lane = iota(shape, 0), iota(shape, 1)
    inside = (
        ((ext_row < tile_rows) | (ext_row >= tile_rows + RIM) | (me < mesh_count - 1))
        & ((ext_row < tile_rows + RIM) | (me > 0))
        & ((ext_lane < tile_cols) | (ext_lane >= tile_cols + LANES // 2) | (sub < sub_count - 1))
        & ((ext_lane < tile_cols + LANES // 2) | (sub > 0))
    )
    flow = [extended[0], extended[1]]
    deep = jnp.where(inside, extended[2], 0.0)
    change = COURANT * (shifted(deep * flow[0], 0) + shifted(deep * flow[1], 1))

    own_block.wait()
    for copy in trace_copies:
        copy.wait_recv()
    difference = traces_in[...] - own_trace
    diff_hi, diff_lo = split(jnp.transpose(difference))
    scattered = mm(diff_hi, hot_in) + mm(diff_lo, hot_in)
    gathered = jnp.concatenate(
        [
            jnp.concatenate(
                [
                    scattered[q * FACE_ROWS : (q + 1) * FACE_ROWS, f * elements : (f + 1) * elements]
                    for f in range(4)
                ],
                0,
            )
            for q in range(quantities)
        ],
        1,
    )
    gathered_hi, gathered_lo = split(gathered)
    lifted = mm(lift_hi, gathered_hi) + mm(lift_hi, gathered_lo) + mm(lift_lo, gathered_hi)
    face_sum = jnp.concatenate(
        [lifted[:, q * elements : (q + 1) * elements] for q in range(quantities)]
        + [jnp.zeros((padded - width, elements), F32)],
        0,
    )
    new_state = base + face_sum
    new[...] = new_state[0:width]
    new_copy = pltpu.make_async_copy(new, new_out, store_sem.at[0])
    new_copy.start()

    new_hi, new_lo = split(new_state)
    columns = mm(choose, new_hi, 1, 1) + mm(choose, new_lo, 1, 1)
    columns_hi, columns_lo = split(columns)
    items = mm(columns_hi, uplift_hi) + mm(columns_lo, uplift_hi) + mm(columns_hi, uplift_lo)
    items_out[...] = items * weight_col
    item_copies = []
    for k in order:
        _, peer = device(0, k)
        item_copies.append(
            send(
                items_out.at[peer_block(peer, CAP), :], items_in.at[peer_block(sub, CAP), :],
                item_send.at[k], item_recv.at[k], 0, k,
            )
        )
    own_items = pltpu.make_async_copy(
        items_out.at[peer_block(sub, CAP), :], items_in.at[peer_block(sub, CAP), :], item_recv.at[0]
    )
    own_items.start()

    got_info = traces_in[0:peer_total, LANES:]
    first_rows = jnp.concatenate([got_info[s * slots : s * slots + 1] for s in range(sub_count)], 0)
    landing_col = as_column(first_rows, info_lane)
    landing = (landing_col == iota((item_slots, LANES), 1).astype(F32)).astype(F32)
    landing = jnp.transpose(landing)[0:tile_rows].astype(BF16)
    loads[18].wait()

    own_items.wait()
    for copy in item_copies:
        copy.wait_recv()
    got_hi, got_lo = split(items_in[...])
    deposit = mm(landing, got_hi) + mm(landing, got_lo)
    level = sea[...] + deposit
    height[...] = level

    hcols_out[0] = pack_edge(level, True, 0)
    hcols_out[1] = pack_edge(level, False, 0)
    high_copies = []
    for i, (dm, ds) in enumerate(DIRECTIONS):
        rows = slice(tile_rows - 8, tile_rows) if dm > 0 else slice(0, 8)
        if ds == 0:
            src, dst = height.at[rows, :], hrows_in.at[i]
        elif dm == 0:
            src, dst = hcols_out.at[i - 2], hcols_in.at[i - 2]
        else:
            src, dst = height.at[rows, corner_of(ds)], hcorner_in.at[i - 4]
        high_copies.append(send(src, dst, high_send.at[i], high_recv.at[i], dm, ds))
    for copy in high_copies:
        copy.wait_recv()
    level = extend(
        level, hrows_in[WAY[(1, 0)]], hrows_in[WAY[(-1, 0)]], hcols_in[0], hcols_in[1],
        corners_of(hcorner_in), 0,
    )
    level = jnp.where(inside, level, 0.0) - change
    flow = [flow[axis] - COURANT * shifted(level, axis) for axis in (0, 1)]
    level = jnp.where(inside, level, 0.0)
    level = level - COURANT * (shifted(deep * flow[0], 0) + shifted(deep * flow[1], 1))
    flow = [flow[axis] - COURANT * shifted(level, axis) for axis in (0, 1)]
    sea_buf[...] = level[0:tile_rows, 0:tile_cols]
    flow_buf[0] = flow[0][0:tile_rows, 0:tile_cols]
    flow_buf[1] = flow[1][0:tile_rows, 0:tile_cols]
    sea_copy = pltpu.make_async_copy(sea_buf, sea_out, store_sem.at[1])
    flow_copy = pltpu.make_async_copy(flow_buf, flow_out, store_sem.at[2])
    sea_copy.start()
    flow_copy.start()
    for copy in rim_copies + trace_copies + item_copies + high_copies:
        copy.wait_send()
    new_copy.wait()
    sea_copy.wait()
    flow_copy.wait()


def body(mesh_count, sub_count, *arguments):
    (
        state, scales, stiffness, jacobians, projection, lifting, flux_matrix,
        peer_send, peer_recv, edge_send, edge_recv, uplift_map,
        fault_elem, fault_dest, fault_row, fault_slip, sea_level, velocity, depth,
    ) = arguments
    basis, quantities, elements = state.shape
    width = basis * quantities
    faults = fault_elem.shape[0]
    rows, cols = sea_level.shape
    slots, edge_slots = peer_send.shape[2], edge_send.shape[2]
    operands = (
        jnp.transpose(state, (1, 0, 2)).reshape(width, elements),
        scales.reshape(1, elements),
        stiffness.reshape(3 * basis, basis),
        jnp.transpose(jacobians, (1, 0, 2)),
        jnp.transpose(projection, (1, 0, 2)),
        jnp.transpose(lifting, (2, 0, 1)),
        flux_matrix,
        peer_send.reshape(sub_count, slots),
        peer_recv.reshape(sub_count, slots),
        edge_send.reshape(2, edge_slots),
        edge_recv.reshape(2, edge_slots),
        uplift_map,
        fault_elem.reshape(1, faults),
        fault_dest.reshape(1, faults),
        fault_row.reshape(1, faults),
        fault_slip.reshape(1, faults),
        sea_level,
        velocity,
        depth,
    )
    padded = -(-width // LANES) * LANES
    trace_lanes = 2 * LANES
    send_total = sub_count * slots + 2 * edge_slots
    item_slots = sub_count * CAP
    vmem, dma = pltpu.VMEM, pltpu.SemaphoreType.DMA
    held = [
        (pltpu.SMEM if i == 6 else vmem)(x.shape, x.dtype) for i, x in enumerate(operands)
    ]
    scratch = held + [
        vmem((padded, padded), F32),
        vmem((padded, padded), BF16),
        vmem((padded, padded), BF16),
        vmem((4 * FACE_ROWS, basis), F32),
        vmem((4 * FACE_ROWS, basis), F32),
        vmem((send_total, trace_lanes), F32),
        vmem((send_total, trace_lanes), F32),
        vmem((item_slots, cols), F32),
        vmem((item_slots, cols), F32),
        vmem((2, 3, 8, cols), F32),
        vmem((2, 8, LANES), F32),
        vmem((2, 3, 8, cols), F32),
        vmem((2, 8, LANES), F32),
        vmem((4, 3, 8, LANES), F32),
        vmem((rows, cols), F32),
        vmem((2, 8, LANES), F32),
        vmem((2, 8, cols), F32),
        vmem((2, 8, LANES), F32),
        vmem((4, 8, LANES), F32),
        vmem((width, elements), F32),
        vmem((rows, cols), F32),
        vmem((2, rows, cols), F32),
        dma((len(operands),)),
        dma((3,)),
        dma((8,)),
        dma((8,)),
        dma((sub_count + 2,)),
        dma((sub_count + 2,)),
        dma((sub_count,)),
        dma((sub_count,)),
        dma((8,)),
        dma((8,)),
    ]
    hbm = pl.BlockSpec(memory_space=pltpu.HBM)
    new_state, sea_out, flow_out = pl.pallas_call(
        functools.partial(kernel, mesh_count, sub_count),
        out_shape=(
            jax.ShapeDtypeStruct((width, elements), F32),
            jax.ShapeDtypeStruct((rows, cols), F32),
            jax.ShapeDtypeStruct((2, rows, cols), F32),
        ),
        in_specs=[hbm] * len(operands),
        out_specs=(hbm, hbm, hbm),
        scratch_shapes=scratch,
        compiler_params=pltpu.CompilerParams(
            collective_id=0, has_side_effects=True, vmem_limit_bytes=63 * 1024 * 1024
        ),
    )(*operands)
    new_state = jnp.transpose(new_state.reshape(quantities, basis, elements), (1, 0, 2))
    return new_state, sea_out, flow_out


def solution(mesh):
    device = P(("mesh", "sub"))
    return jax.shard_map(
        functools.partial(body, mesh.shape["mesh"], mesh.shape["sub"]),
        mesh=mesh,
        in_specs=(
            P(None, None, ("mesh", "sub")),
            device,
            P(),
            P(),
            P(),
            P(),
            P(),
            P(("mesh", "sub"), None, None),
            P(("mesh", "sub"), None, None),
            P(("mesh", "sub"), None, None),
            P(("mesh", "sub"), None, None),
            P(),
            device,
            P(("mesh", "sub"), None),
            device,
            device,
            P("mesh", "sub"),
            P(None, "mesh", "sub"),
            P("mesh", "sub"),
        ),
        out_specs=(P(None, None, ("mesh", "sub")), P("mesh", "sub"), P(None, "mesh", "sub")),
        check_vma=False,
    )
```

```python
import functools

import jax
import jax.numpy as jnp
from jax import lax
from jax.experimental import pallas as pl
from jax.experimental.pallas import tpu as pltpu
from jax.sharding import PartitionSpec as P

ORDER = 5
CAP = 16
EARTH_STEP = 0.5
COURANT = 0.45
MESH = pl.DeviceIdType.MESH
F32, BF16, I32 = jnp.float32, jnp.bfloat16, jnp.int32
LANES = 128
FACE_ROWS = 24
INFO = 224
RIM = 4
DIRECTIONS = ((1, 0), (-1, 0), (0, 1), (0, -1), (1, 1), (1, -1), (-1, 1), (-1, -1))
WAY = {d: i for i, d in enumerate(DIRECTIONS)}


def split(x):
    high = x.astype(BF16)
    return high, (x - high.astype(F32)).astype(BF16)


def mm(a, b, left=1, right=0):
    return lax.dot_general(a, b, (((left,), (right,)), ((), ())), preferred_element_type=F32)


def iota(shape, axis):
    return lax.broadcasted_iota(I32, shape, axis)


def repeat_rows(rows, count):
    return jnp.concatenate(
        [jnp.broadcast_to(rows[i : i + 1], (count, rows.shape[1])) for i in range(rows.shape[0])], 0
    )


def as_column(rows, first=0):
    count = rows.shape[1] if first == 0 else CAP
    wide = repeat_rows(rows, count)
    mine = (iota(wide.shape, 0) & (count - 1)) == iota(wide.shape, 1) - first
    return jnp.sum(jnp.where(mine, wide, 0.0), axis=1, keepdims=True)


def pack_edge(array, last, base):
    lane = iota((8, LANES), 1)
    start = array.shape[1] - LANES if last else 0
    keep = lane >= LANES - RIM if last else lane < RIM
    packed = jnp.zeros((8, LANES), F32)
    for g in range(array.shape[0] // 8):
        tile = jnp.where(keep, array[8 * g : 8 * g + 8, start : start + LANES], 0.0)
        packed = packed + pltpu.roll(tile, (RIM * (g + 1 if last else g) + base) % LANES, 1)
    return packed


def extend(array, low, high, left, right, corners, base):
    lane, row = iota((8, LANES), 1), iota((8, LANES), 0)
    side = jnp.concatenate(
        [
            jnp.where(
                lane < LANES // 2,
                pltpu.roll(right, (-RIM * g - base) % LANES, 1),
                pltpu.roll(left, (LANES - RIM - RIM * g - base) % LANES, 1),
            )
            for g in range(array.shape[0] // 8)
        ],
        0,
    )
    down_right, down_left, up_right, up_left = corners
    corner = jnp.where(
        row < RIM,
        jnp.where(lane < LANES // 2, down_right, down_left),
        jnp.where(lane < LANES // 2, up_right, up_left),
    )
    bottom = jnp.where(iota(low.shape, 0) < RIM, high, low)
    return jnp.concatenate(
        [jnp.concatenate([array, side], 1), jnp.concatenate([bottom, corner], 1)], 0
    )


def shifted(array, axis):
    size = array.shape[axis]
    return (pltpu.roll(array, size - 1, axis) - pltpu.roll(array, 1, axis)) * 0.5


def kernel(mesh_count, sub_count, *refs):
    (
        state_in, scales_in, stiff_in, jac_in, proj_in, lift_in, flux_in,
        psend_in, precv_in, esend_in, erecv_in, uplift_in,
        felem_in, fdest_in, frow_in, fslip_in, sea_in, vel_in, depth_in,
        new_out, sea_out, flow_out,
        state, scales, stiff, jac, proj, lift, flux,
        psend, precv, esend, erecv, uplift,
        felem, fdest, frow, fslip, sea, vel, depth,
        spread, matrix_hi, matrix_lo, hot, faces, lifts, traces_out, traces_in, items_out, items_in,
        rows_out, cols_out, rows_in, cols_in, corner_in,
        height, hcols_out, hrows_in, hcols_in, hcorner_in,
        load_sem, rim_send, rim_recv, trace_send, trace_recv,
        item_send, item_recv, high_send, high_recv,
    ) = refs
    quantities, basis = flux.shape[0], stiff.shape[1]
    width = quantities * basis
    padded = matrix_hi.shape[0]
    elements = state.shape[1]
    slots = psend.shape[1]
    edge_slots = esend.shape[1]
    peer_total = sub_count * slots
    send_total = peer_total + 2 * edge_slots
    tile_rows, tile_cols = depth.shape
    me, sub = lax.axis_index("mesh"), lax.axis_index("sub")
    neighbour = {1: me < mesh_count - 1, -1: me > 0}

    def device(dm, ds):
        return (me + dm, lax.rem(sub + ds + sub_count, sub_count))

    loads = [
        pltpu.make_async_copy(src, dst, load_sem.at[i])
        for i, (src, dst) in enumerate(
            (
                (stiff_in, stiff), (jac_in, jac), (state_in, state), (scales_in, scales),
                (psend_in, psend), (precv_in, precv), (esend_in, esend), (erecv_in, erecv),
                (proj_in, proj), (felem_in, felem), (fdest_in, fdest), (frow_in, frow),
                (fslip_in, fslip), (flux_in, flux), (lift_in, lift),
                (vel_in, vel), (depth_in, depth), (uplift_in, uplift), (sea_in, sea),
            )
        )
    ]
    for load in loads:
        load.start()
    barrier = pltpu.get_barrier_semaphore()

    def greet(dm, ds):
        pl.semaphore_signal(barrier, inc=1, device_id=device(dm, ds), device_id_type=MESH)

    for k in range(1, sub_count):
        greet(0, k)
    for side in (1, -1):

        @pl.when(neighbour[side])
        def _():
            for ds in (0, 1, -1):
                greet(side, ds)

    def remote(src, dst, send_sem, recv_sem, dm, ds):
        return pltpu.make_async_remote_copy(
            src_ref=src, dst_ref=dst, send_sem=send_sem, recv_sem=recv_sem,
            device_id=device(dm, ds), device_id_type=MESH,
        )

    def each(copies, act):
        for dm, copy in copies:
            if dm == 0:
                act(copy)
        for side in (1, -1):
            some = [copy for dm, copy in copies if dm == side]
            if some:

                @pl.when(neighbour[side])
                def _():
                    for copy in some:
                        act(copy)

    def start_all(copies):
        each(copies, lambda copy: copy.start())

    def sent_all(copies):
        each(copies, lambda copy: copy.wait_send())

    def received_all(copies):
        each([(-dm, copy) for dm, copy in copies], lambda copy: copy.wait_recv())

    def rim_copies(rows_of, cols_ref, rows_ref, cols_got, corner_ref, send_sem, recv_sem):
        copies = []
        for i, (dm, ds) in enumerate(DIRECTIONS):
            if ds == 0:
                src, dst = rows_of(dm, None), rows_ref.at[i]
            elif dm == 0:
                src, dst = cols_ref.at[i - 2], cols_got.at[i - 2]
            else:
                lanes = slice(tile_cols - LANES, tile_cols) if ds > 0 else slice(0, LANES)
                src, dst = rows_of(dm, lanes), corner_ref.at[i - 4]
            copies.append((dm, remote(src, dst, send_sem.at[i], recv_sem.at[i], dm, ds)))
        return copies

    lane = iota((1, padded), 1)
    of_quantity = sum((lane >= basis * k).astype(I32) for k in range(1, quantities + 1))
    of_basis = lane - basis * of_quantity
    spread_basis = (iota((basis, padded), 0) == of_basis).astype(F32).astype(BF16)
    spread_quantity = (iota((quantities, padded), 0) == of_quantity).astype(F32)
    for load in loads[0:15]:
        load.wait()
    stiff_hi, stiff_lo = split(stiff[...])
    spread[...] = mm(stiff_hi, spread_basis) + mm(stiff_lo, spread_basis)
    jac_wide = [
        lax.dot_general(
            jac[:, d, :], spread_quantity, (((0,), (0,)), ((), ())),
            precision=lax.Precision.HIGHEST, preferred_element_type=F32,
        )
        for d in range(3)
    ]

    def matrix_rows(q):
        if q == quantities:
            return jnp.zeros((padded - width, padded), F32)
        block = spread[0:basis, :] * jac_wide[0][q : q + 1]
        for d in (1, 2):
            block = block + spread[d * basis : (d + 1) * basis, :] * jac_wide[d][q : q + 1]
        return block

    at = 0
    for q in range(0, quantities, 2):
        high, low = split(jnp.concatenate([matrix_rows(q), matrix_rows(q + 1)], 0))
        matrix_hi[at : at + high.shape[0], :] = high
        matrix_lo[at : at + high.shape[0], :] = low
        at = at + high.shape[0]

    codes = jnp.concatenate(
        [as_column(ref[...].astype(F32)) for ref in (psend, esend, precv, erecv)], 0
    )
    face_lane = iota((1, 4 * elements), 1)
    key = (4 * (face_lane & (elements - 1)) + face_lane // elements).astype(F32)
    hot[...] = (codes == key).astype(F32).astype(BF16)
    faces[...] = jnp.zeros(faces.shape, F32)
    for f in range(4):
        for half in (0, LANES // 2):
            faces[f * FACE_ROWS : f * FACE_ROWS + proj.shape[0], half : half + basis] = proj[:, f, :]
    faces_hi, faces_lo = split(faces[...])
    faces_lo = faces_lo[:, 0 : LANES // 2]

    fault_count = fdest.shape[1]
    square = (fault_count, fault_count)
    dest_row = fdest[...].astype(F32)
    dest_col = as_column(dest_row)
    same = dest_col == dest_row
    rank_row = jnp.sum(
        jnp.where(same & (iota(square, 0) < iota(square, 1)), 1.0, 0.0), axis=0, keepdims=True
    )
    rank_col = jnp.sum(
        jnp.where(same & (iota(square, 1) < iota(square, 0)), 1.0, 0.0), axis=1, keepdims=True
    )
    row_numbers = frow[...].astype(F32) + 1.0
    info_left = jnp.where(
        dest_row == (iota((peer_total, fault_count), 0) // slots).astype(F32), row_numbers, 0.0
    )
    info_lane = INFO % LANES
    info_right = (
        rank_col == (iota((fault_count, LANES), 1) - info_lane).astype(F32)
    ).astype(F32)
    info = mm(info_left.astype(BF16), info_right.astype(BF16)) - 1.0
    info_lanes = iota((peer_total, LANES), 1)
    info_here = (info_lanes >= info_lane) & (info_lanes < info_lane + CAP)

    scale = scales[...]

    def derivative(x):
        x_hi, x_lo = split(x)
        both = mm(matrix_hi[...], jnp.concatenate([x_hi, x_lo], 1))
        return (both[:, :elements] + both[:, elements:] + mm(matrix_lo[...], x_hi)) * scale

    start = jnp.concatenate([state[...], jnp.zeros((padded - width, elements), F32)], 0)
    factor = EARTH_STEP
    integral = factor * start
    current = start
    for power in range(1, ORDER):
        current = derivative(current)
        factor = factor * EARTH_STEP / (power + 1)
        integral = integral + factor * current

    parts = jnp.concatenate(
        [
            jnp.concatenate(
                [
                    integral[p * basis : (p + 1) * basis],
                    jnp.zeros((LANES // 2 - basis, elements), F32),
                ],
                0,
            )
            for p in range(quantities)
        ],
        1,
    )
    parts_hi, parts_lo = split(parts)
    every = mm(faces_hi, jnp.concatenate([parts_hi, parts_lo], 0)) + mm(faces_lo, parts_hi)
    face_width = quantities * FACE_ROWS
    trace_rows = traces_out.shape[1]

    def face_block(f, q):
        return every[f * FACE_ROWS : (f + 1) * FACE_ROWS, q * elements : (q + 1) * elements]

    table = jnp.concatenate(
        [jnp.concatenate([face_block(f, q) for q in range(quantities)], 0) for f in range(4)], 1
    )
    table = jnp.concatenate([table, jnp.zeros((trace_rows - face_width, 4 * elements), F32)], 0)
    table_hi, table_lo = split(table)
    picked = mm(hot[...], table_hi, 1, 1) + mm(hot[...], table_lo, 1, 1)
    traces_out[:, 0:LANES] = picked[0:send_total, 0:LANES]
    traces_out[0:peer_total, LANES:] = jnp.where(
        info_here, info, picked[0:peer_total, LANES:]
    )
    traces_out[peer_total:, LANES:] = picked[peer_total:send_total, LANES:]
    own_trace = picked[send_total:]

    def peer_block(index, rows):
        return pl.ds(pl.multiple_of(index * rows, rows), rows)

    order = sorted(range(1, sub_count), key=lambda k: -min(k, sub_count - k))
    trace_copies = []
    for k in order:
        _, peer = device(0, k)
        trace_copies.append(
            (
                0,
                remote(
                    traces_out.at[peer_block(peer, slots), :],
                    traces_in.at[peer_block(sub, slots), :],
                    trace_send.at[k], trace_recv.at[k], 0, k,
                ),
            )
        )
    for i, dm in enumerate((1, -1)):
        source = peer_total + (edge_slots if dm > 0 else 0)
        target = peer_total + (0 if dm > 0 else edge_slots)
        trace_copies.append(
            (
                dm,
                remote(
                    traces_out.at[source : source + edge_slots, :],
                    traces_in.at[target : target + edge_slots, :],
                    trace_send.at[sub_count + i], trace_recv.at[sub_count + i], dm, 0,
                ),
            )
        )
    pl.semaphore_wait(
        barrier, sub_count - 1 + 3 * (neighbour[1].astype(I32) + neighbour[-1].astype(I32))
    )
    start_all(trace_copies)
    own_block = pltpu.make_async_copy(
        traces_out.at[peer_block(sub, slots), :], traces_in.at[peer_block(sub, slots), :],
        trace_recv.at[0],
    )
    own_block.start()

    for load in loads[15:]:
        load.wait()
    for i, first in enumerate((tile_rows - 8, 0)):
        rows_out[i, 0:2] = vel[:, first : first + 8, :]
        rows_out[i, 2] = depth[first : first + 8, :]
    fields = (vel[0], vel[1], depth[...])
    group = RIM * (tile_rows // 8)
    for i, last in enumerate((True, False)):
        packed = pack_edge(fields[0], last, 0)
        for k in (1, 2):
            packed = packed + pack_edge(fields[k], last, k * group)
        cols_out[i] = packed

    def rows_of_fields(dm, lanes):
        i = 0 if dm > 0 else 1
        return rows_out.at[i] if lanes is None else rows_out.at[i, :, :, lanes]

    field_copies = rim_copies(
        rows_of_fields, cols_out, rows_in, cols_in, corner_in, rim_send, rim_recv
    )
    start_all(field_copies)

    base = start + derivative(integral)
    lifts[...] = jnp.zeros(lifts.shape, F32)
    for f in range(4):
        lifts[f * FACE_ROWS : f * FACE_ROWS + lift.shape[0], :] = lift[:, f, :]
    lift_hi, lift_lo = split(jnp.transpose(lifts[...]))
    lift_hi = jnp.concatenate([lift_hi, lift_hi], 1)
    hot_in = hot[send_total:, :]
    hot_in = jnp.concatenate([hot_in, hot_in], 0)

    face_col, face_row = iota((trace_rows, 1), 0), iota((1, trace_rows), 1)
    quantity_col = sum((face_col >= FACE_ROWS * k).astype(I32) for k in range(1, quantities + 1))
    quantity_row = sum((face_row >= FACE_ROWS * k).astype(I32) for k in range(1, quantities + 1))
    exact = functools.partial(
        lax.dot_general, precision=lax.Precision.HIGHEST, preferred_element_type=F32
    )
    flux_left = exact(
        (quantity_col == iota((trace_rows, quantities), 1)).astype(F32), flux[...],
        (((1,), (1,)), ((), ())),
    )
    flux_wide = exact(
        flux_left, (quantity_row == iota((quantities, trace_rows), 0)).astype(F32),
        (((1,), (0,)), ((), ())),
    )
    same_face = face_col - FACE_ROWS * quantity_col == face_row - FACE_ROWS * quantity_row
    flux_hi, flux_lo = split(jnp.where(same_face, flux_wide, 0.0))

    rows_here = iota((padded, 1), 0)
    row_quantity = sum((rows_here >= basis * k).astype(I32) for k in range(1, quantities + 1))
    wanted = (rows_here - basis * row_quantity) * quantities + row_quantity
    wanted = jnp.where(rows_here < width, wanted, -1)
    permute = (iota((padded, width), 1) == wanted).astype(F32).astype(BF16)
    uplift_hi, uplift_lo = split(uplift[...])
    uplift_hi = mm(permute, uplift_hi).astype(BF16)
    uplift_lo = mm(permute, uplift_lo).astype(BF16)

    item_slots = sub_count * CAP
    place = (
        iota((item_slots, fault_count), 0).astype(F32) == dest_row * float(CAP) + rank_row
    ).astype(F32)
    elem_col = as_column(felem[...].astype(F32))
    elem_hot = (elem_col == iota((fault_count, elements), 1).astype(F32)).astype(F32)
    choose = mm(place.astype(BF16), elem_hot.astype(BF16)).astype(BF16)
    choose = jnp.concatenate([choose, choose], 1)
    weighting = 0.3 + 0.7 * fslip[...].astype(F32)
    weight_col = jnp.sum(place * weighting, axis=1, keepdims=True)

    own_block.wait()
    received_all(trace_copies)
    slot_col = iota((send_total, 1), 0)
    missing = ((slot_col >= peer_total) & (slot_col < peer_total + edge_slots) & (me == 0)) | (
        (slot_col >= peer_total + edge_slots) & (me == mesh_count - 1)
    )
    difference = jnp.where(missing, 0.0, traces_in[...]) - own_trace
    diff_hi, diff_lo = split(difference)
    mixed = mm(flux_hi, jnp.concatenate([diff_hi, diff_lo], 0), 1, 1)
    mixed = mixed[:, :send_total] + mixed[:, send_total:] + mm(flux_lo, diff_hi, 1, 1)
    scattered = mm(jnp.concatenate(split(mixed), 1), hot_in)
    gathered = jnp.concatenate(
        [
            jnp.concatenate(
                [
                    scattered[q * FACE_ROWS : (q + 1) * FACE_ROWS, f * elements : (f + 1) * elements]
                    for f in range(4)
                ],
                0,
            )
            for q in range(quantities)
        ],
        1,
    )
    gathered_hi, gathered_lo = split(gathered)
    lifted = mm(lift_hi, jnp.concatenate([gathered_hi, gathered_lo], 0)) + mm(lift_lo, gathered_hi)
    face_sum = jnp.concatenate(
        [lifted[:, q * elements : (q + 1) * elements] for q in range(quantities)]
        + [jnp.zeros((padded - width, elements), F32)],
        0,
    )
    new_state = base + face_sum
    new_out[...] = new_state[0:width]

    columns = mm(choose, jnp.concatenate(split(new_state), 1), 1, 1)
    columns_hi, columns_lo = split(columns)
    items = mm(columns_hi, uplift_hi) + mm(columns_lo, uplift_hi) + mm(columns_hi, uplift_lo)
    items_out[...] = items * weight_col
    item_copies = []
    for k in order:
        _, peer = device(0, k)
        item_copies.append(
            (
                0,
                remote(
                    items_out.at[peer_block(peer, CAP), :], items_in.at[peer_block(sub, CAP), :],
                    item_send.at[k], item_recv.at[k], 0, k,
                ),
            )
        )
    start_all(item_copies)
    own_items = pltpu.make_async_copy(
        items_out.at[peer_block(sub, CAP), :], items_in.at[peer_block(sub, CAP), :], item_recv.at[0]
    )
    own_items.start()

    got_info = traces_in[0:peer_total, LANES:]
    first_rows = jnp.concatenate([got_info[s * slots : s * slots + 1] for s in range(sub_count)], 0)
    landing_col = as_column(first_rows, info_lane)
    landing = (landing_col == iota((item_slots, LANES), 1).astype(F32)).astype(F32)
    landing = jnp.transpose(landing)[0:tile_rows].astype(BF16)
    landing = jnp.concatenate([landing, landing], 1)

    received_all(field_copies)

    def corners_of(ref, k=None):
        return [
            ref[WAY[way] - 4] if k is None else ref[WAY[way] - 4, k]
            for way in ((-1, -1), (-1, 1), (1, -1), (1, 1))
        ]

    extended = [
        extend(
            fields[k], rows_in[WAY[(1, 0)], k], rows_in[WAY[(-1, 0)], k],
            cols_in[0], cols_in[1], corners_of(corner_in, k), k * group,
        )
        for k in range(3)
    ]
    shape = extended[0].shape
    ext_row, ext_lane = iota(shape, 0), iota(shape, 1)
    inside = (
        ((ext_row < tile_rows) | (ext_row >= tile_rows + RIM) | neighbour[1])
        & ((ext_row < tile_rows + RIM) | neighbour[-1])
        & ((ext_lane < tile_cols) | (ext_lane >= tile_cols + LANES // 2) | (sub < sub_count - 1))
        & ((ext_lane < tile_cols + LANES // 2) | (sub > 0))
    )
    flow = [jnp.where(inside, extended[axis], 0.0) for axis in (0, 1)]
    deep = jnp.where(inside, extended[2], 0.0)
    change = COURANT * (shifted(deep * flow[0], 0) + shifted(deep * flow[1], 1))

    own_items.wait()
    received_all(item_copies)
    deposit = mm(landing, jnp.concatenate(split(items_in[...]), 0))
    level = sea[...] + deposit
    height[...] = level
    hcols_out[0] = pack_edge(level, True, 0)
    hcols_out[1] = pack_edge(level, False, 0)

    def rows_of_height(dm, lanes):
        rows = slice(tile_rows - 8, tile_rows) if dm > 0 else slice(0, 8)
        return height.at[rows, :] if lanes is None else height.at[rows, lanes]

    high_copies = rim_copies(
        rows_of_height, hcols_out, hrows_in, hcols_in, hcorner_in, high_send, high_recv
    )
    start_all(high_copies)
    for copies in (trace_copies, field_copies, item_copies):
        sent_all(copies)

    received_all(high_copies)
    level = extend(
        level, hrows_in[WAY[(1, 0)]], hrows_in[WAY[(-1, 0)]], hcols_in[0], hcols_in[1],
        corners_of(hcorner_in), 0,
    )
    level = jnp.where(inside, level, 0.0) - change
    flow = [flow[axis] - COURANT * shifted(level, axis) for axis in (0, 1)]
    level = jnp.where(inside, level, 0.0)
    level = level - COURANT * (shifted(deep * flow[0], 0) + shifted(deep * flow[1], 1))
    flow = [flow[axis] - COURANT * shifted(level, axis) for axis in (0, 1)]
    sea_out[...] = level[0:tile_rows, 0:tile_cols]
    flow_out[0] = flow[0][0:tile_rows, 0:tile_cols]
    flow_out[1] = flow[1][0:tile_rows, 0:tile_cols]
    sent_all(high_copies)


def store_kernel(new_in, sea_in, flow_in, new_out, sea_out, flow_out, sems):
    copies = [
        pltpu.make_async_copy(src, dst, sems.at[i])
        for i, (src, dst) in enumerate(
            ((new_in, new_out), (sea_in, sea_out), (flow_in, flow_out))
        )
    ]
    for copy in copies:
        copy.start()
    for copy in copies:
        copy.wait()


def body(mesh_count, sub_count, *arguments):
    (
        state, scales, stiffness, jacobians, projection, lifting, flux_matrix,
        peer_send, peer_recv, edge_send, edge_recv, uplift_map,
        fault_elem, fault_dest, fault_row, fault_slip, sea_level, velocity, depth,
    ) = arguments
    basis, quantities, elements = state.shape
    width = basis * quantities
    faults = fault_elem.shape[0]
    rows, cols = sea_level.shape
    slots, edge_slots = peer_send.shape[2], edge_send.shape[2]
    operands = (
        jnp.transpose(state, (1, 0, 2)).reshape(width, elements),
        scales.reshape(1, elements),
        stiffness.reshape(3 * basis, basis),
        jnp.transpose(jacobians, (1, 0, 2)),
        jnp.transpose(projection, (1, 0, 2)),
        jnp.transpose(lifting, (2, 0, 1)),
        flux_matrix,
        peer_send.reshape(sub_count, slots),
        peer_recv.reshape(sub_count, slots),
        edge_send.reshape(2, edge_slots),
        edge_recv.reshape(2, edge_slots),
        uplift_map,
        fault_elem.reshape(1, faults),
        fault_dest.reshape(1, faults),
        fault_row.reshape(1, faults),
        fault_slip.reshape(1, faults),
        sea_level,
        velocity,
        depth,
    )
    padded = -(-width // LANES) * LANES
    trace_lanes = 2 * LANES
    send_total = sub_count * slots + 2 * edge_slots
    item_slots = sub_count * CAP
    vmem, dma = pltpu.VMEM, pltpu.SemaphoreType.DMA
    held = [vmem(x.shape, x.dtype) for x in operands]
    scratch = held + [
        vmem((3 * basis, padded), F32),
        vmem((padded, padded), BF16),
        vmem((padded, padded), BF16),
        vmem((2 * send_total, 4 * elements), BF16),
        vmem((4 * FACE_ROWS, LANES), F32),
        vmem((4 * FACE_ROWS, basis), F32),
        vmem((send_total, trace_lanes), F32),
        vmem((send_total, trace_lanes), F32),
        vmem((item_slots, cols), F32),
        vmem((item_slots, cols), F32),
        vmem((2, 3, 8, cols), F32),
        vmem((2, 8, LANES), F32),
        vmem((2, 3, 8, cols), F32),
        vmem((2, 8, LANES), F32),
        vmem((4, 3, 8, LANES), F32),
        vmem((rows, cols), F32),
        vmem((2, 8, LANES), F32),
        vmem((2, 8, cols), F32),
        vmem((2, 8, LANES), F32),
        vmem((4, 8, LANES), F32),
        dma((len(operands),)),
        dma((8,)),
        dma((8,)),
        dma((sub_count + 2,)),
        dma((sub_count + 2,)),
        dma((sub_count,)),
        dma((sub_count,)),
        dma((8,)),
        dma((8,)),
    ]
    hbm, local = pl.BlockSpec(memory_space=pltpu.HBM), pl.BlockSpec(memory_space=pltpu.VMEM)
    shapes = ((width, elements), (rows, cols), (2, rows, cols))
    results = pl.pallas_call(
        functools.partial(kernel, mesh_count, sub_count),
        out_shape=tuple(vmem(shape, F32) for shape in shapes),
        in_specs=[hbm] * len(operands),
        out_specs=(local,) * 3,
        scratch_shapes=scratch,
        compiler_params=pltpu.CompilerParams(
            collective_id=0, has_side_effects=True, vmem_limit_bytes=40 * 1024 * 1024
        ),
    )(*[pltpu.with_memory_space_constraint(x, pltpu.HBM) for x in operands])
    new_state, sea_out, flow_out = pl.pallas_call(
        store_kernel,
        out_shape=tuple(pltpu.HBM(shape, F32) for shape in shapes),
        in_specs=[local] * 3,
        out_specs=(hbm,) * 3,
        scratch_shapes=[dma((3,))],
    )(*results)
    new_state = jnp.transpose(new_state.reshape(quantities, basis, elements), (1, 0, 2))
    return new_state, sea_out, flow_out


def solution(mesh):
    device = P(("mesh", "sub"))
    return jax.shard_map(
        functools.partial(body, mesh.shape["mesh"], mesh.shape["sub"]),
        mesh=mesh,
        in_specs=(
            P(None, None, ("mesh", "sub")),
            device,
            P(),
            P(),
            P(),
            P(),
            P(),
            P(("mesh", "sub"), None, None),
            P(("mesh", "sub"), None, None),
            P(("mesh", "sub"), None, None),
            P(("mesh", "sub"), None, None),
            P(),
            device,
            P(("mesh", "sub"), None),
            device,
            device,
            P("mesh", "sub"),
            P(None, "mesh", "sub"),
            P("mesh", "sub"),
        ),
        out_specs=(P(None, None, ("mesh", "sub")), P("mesh", "sub"), P(None, "mesh", "sub")),
        check_vma=False,
    )
```

```python
import functools

import jax
import jax.numpy as jnp
from jax import lax
from jax.experimental import pallas as pl
from jax.experimental.pallas import tpu as pltpu
from jax.sharding import PartitionSpec as P

ORDER = 5
CAP = 16
EARTH_STEP = 0.5
COURANT = 0.45
MESH = pl.DeviceIdType.MESH
F32, BF16, I32 = jnp.float32, jnp.bfloat16, jnp.int32
LANES = 128
FACE_ROWS = 24
INFO = 224
RIM = 4
DIRECTIONS = ((1, 0), (-1, 0), (0, 1), (0, -1), (1, 1), (1, -1), (-1, 1), (-1, -1))
WAY = {d: i for i, d in enumerate(DIRECTIONS)}


def split(x):
    high = x.astype(BF16)
    return high, (x - high.astype(F32)).astype(BF16)


def mm(a, b, left=1, right=0):
    return lax.dot_general(a, b, (((left,), (right,)), ((), ())), preferred_element_type=F32)


def iota(shape, axis):
    return lax.broadcasted_iota(I32, shape, axis)


def repeat_rows(rows, count):
    return jnp.concatenate(
        [jnp.broadcast_to(rows[i : i + 1], (count, rows.shape[1])) for i in range(rows.shape[0])], 0
    )


def as_column(rows, first=0):
    count = rows.shape[1] if first == 0 else CAP
    wide = repeat_rows(rows, count)
    mine = (iota(wide.shape, 0) & (count - 1)) == iota(wide.shape, 1) - first
    return jnp.sum(jnp.where(mine, wide, 0.0), axis=1, keepdims=True)


def pack_edge(array, last, base):
    lane = iota((8, LANES), 1)
    start = array.shape[1] - LANES if last else 0
    keep = lane >= LANES - RIM if last else lane < RIM
    packed = jnp.zeros((8, LANES), F32)
    for g in range(array.shape[0] // 8):
        tile = jnp.where(keep, array[8 * g : 8 * g + 8, start : start + LANES], 0.0)
        packed = packed + pltpu.roll(tile, (RIM * (g + 1 if last else g) + base) % LANES, 1)
    return packed


def extend(array, low, high, left, right, corners, base):
    lane, row = iota((8, LANES), 1), iota((8, LANES), 0)
    side = jnp.concatenate(
        [
            jnp.where(
                lane < LANES // 2,
                pltpu.roll(right, (-RIM * g - base) % LANES, 1),
                pltpu.roll(left, (LANES - RIM - RIM * g - base) % LANES, 1),
            )
            for g in range(array.shape[0] // 8)
        ],
        0,
    )
    down_right, down_left, up_right, up_left = corners
    corner = jnp.where(
        row < RIM,
        jnp.where(lane < LANES // 2, down_right, down_left),
        jnp.where(lane < LANES // 2, up_right, up_left),
    )
    bottom = jnp.where(iota(low.shape, 0) < RIM, high, low)
    return jnp.concatenate(
        [jnp.concatenate([array, side], 1), jnp.concatenate([bottom, corner], 1)], 0
    )


def shifted(array, axis):
    size = array.shape[axis]
    return (pltpu.roll(array, size - 1, axis) - pltpu.roll(array, 1, axis)) * 0.5


def kernel(mesh_count, sub_count, *refs):
    (
        state_in, scales_in, stiff_in, jac_in, proj_in, lift_in, flux_in,
        psend_in, precv_in, esend_in, erecv_in, uplift_in,
        felem_in, fdest_in, frow_in, fslip_in, sea_in, vel_in, depth_in,
        new_out, sea_out, flow_out,
        state, scales, stiff, jac, proj, lift, flux,
        psend, precv, esend, erecv, uplift,
        felem, fdest, frow, fslip, sea, vel, depth,
        spread, matrix_hi, matrix_lo, hot, faces, lifts, traces_out, traces_in, items_out, items_in,
        rows_out, cols_out, rows_in, cols_in, corner_in,
        height, hcols_out, hrows_in, hcols_in, hcorner_in,
        load_sem, rim_send, rim_recv, trace_send, trace_recv,
        item_send, item_recv, high_send, high_recv,
    ) = refs
    quantities, basis = flux.shape[0], stiff.shape[1]
    width = quantities * basis
    padded = matrix_hi.shape[0]
    elements = state.shape[1]
    slots = psend.shape[1]
    edge_slots = esend.shape[1]
    peer_total = sub_count * slots
    send_total = peer_total + 2 * edge_slots
    tile_rows, tile_cols = depth.shape
    me, sub = lax.axis_index("mesh"), lax.axis_index("sub")
    neighbour = {1: me < mesh_count - 1, -1: me > 0}

    def device(dm, ds):
        return (me + dm, lax.rem(sub + ds + sub_count, sub_count))

    loads = [
        pltpu.make_async_copy(src, dst, load_sem.at[i])
        for i, (src, dst) in enumerate(
            (
                (stiff_in, stiff), (jac_in, jac), (state_in, state), (scales_in, scales),
                (psend_in, psend), (precv_in, precv), (esend_in, esend), (erecv_in, erecv),
                (proj_in, proj), (felem_in, felem), (fdest_in, fdest), (frow_in, frow),
                (fslip_in, fslip), (flux_in, flux), (lift_in, lift),
                (vel_in, vel), (depth_in, depth), (uplift_in, uplift), (sea_in, sea),
            )
        )
    ]
    for load in loads:
        load.start()
    barrier = pltpu.get_barrier_semaphore()

    def greet(dm, ds):
        pl.semaphore_signal(barrier, inc=1, device_id=device(dm, ds), device_id_type=MESH)

    for k in range(1, sub_count):
        greet(0, k)
    for side in (1, -1):

        @pl.when(neighbour[side])
        def _():
            for ds in (0, 1, -1):
                greet(side, ds)

    def remote(src, dst, send_sem, recv_sem, dm, ds):
        return pltpu.make_async_remote_copy(
            src_ref=src, dst_ref=dst, send_sem=send_sem, recv_sem=recv_sem,
            device_id=device(dm, ds), device_id_type=MESH,
        )

    def each(copies, act):
        for dm, copy in copies:
            if dm == 0:
                act(copy)
        for side in (1, -1):
            some = [copy for dm, copy in copies if dm == side]
            if some:

                @pl.when(neighbour[side])
                def _():
                    for copy in some:
                        act(copy)

    def start_all(copies):
        each(copies, lambda copy: copy.start())

    def sent_all(copies):
        each(copies, lambda copy: copy.wait_send())

    def received_all(copies):
        each([(-dm, copy) for dm, copy in copies], lambda copy: copy.wait_recv())

    def rim_copies(rows_of, cols_ref, rows_ref, cols_got, corner_ref, send_sem, recv_sem):
        copies = []
        for i, (dm, ds) in enumerate(DIRECTIONS):
            if ds == 0:
                src, dst = rows_of(dm, None), rows_ref.at[i]
            elif dm == 0:
                src, dst = cols_ref.at[i - 2], cols_got.at[i - 2]
            else:
                lanes = slice(tile_cols - LANES, tile_cols) if ds > 0 else slice(0, LANES)
                src, dst = rows_of(dm, lanes), corner_ref.at[i - 4]
            copies.append((dm, remote(src, dst, send_sem.at[i], recv_sem.at[i], dm, ds)))
        return copies

    lane = iota((1, padded), 1)
    of_quantity = sum((lane >= basis * k).astype(I32) for k in range(1, quantities + 1))
    of_basis = lane - basis * of_quantity
    spread_basis = (iota((basis, padded), 0) == of_basis).astype(F32).astype(BF16)
    spread_quantity = (iota((quantities, padded), 0) == of_quantity).astype(F32)
    for load in loads[0:15]:
        load.wait()
    stiff_hi, stiff_lo = split(stiff[...])
    spread[...] = mm(stiff_hi, spread_basis) + mm(stiff_lo, spread_basis)
    jac_wide = [
        lax.dot_general(
            jac[:, d, :], spread_quantity, (((0,), (0,)), ((), ())),
            precision=lax.Precision.HIGHEST, preferred_element_type=F32,
        )
        for d in range(3)
    ]

    def matrix_rows(q):
        if q == quantities:
            return jnp.zeros((padded - width, padded), F32)
        block = spread[0:basis, :] * jac_wide[0][q : q + 1]
        for d in (1, 2):
            block = block + spread[d * basis : (d + 1) * basis, :] * jac_wide[d][q : q + 1]
        return block

    at = 0
    for q in range(0, quantities, 2):
        high, low = split(jnp.concatenate([matrix_rows(q), matrix_rows(q + 1)], 0))
        matrix_hi[at : at + high.shape[0], :] = high
        matrix_lo[at : at + high.shape[0], :] = low
        at = at + high.shape[0]

    codes = jnp.concatenate(
        [as_column(ref[...].astype(F32)) for ref in (psend, esend, precv, erecv)], 0
    )
    face_lane = iota((1, 4 * elements), 1)
    key = (4 * (face_lane & (elements - 1)) + face_lane // elements).astype(F32)
    hot[...] = (codes == key).astype(F32).astype(BF16)
    faces[...] = jnp.zeros(faces.shape, F32)
    for f in range(4):
        for half in (0, LANES // 2):
            faces[f * FACE_ROWS : f * FACE_ROWS + proj.shape[0], half : half + basis] = proj[:, f, :]
    faces_hi, faces_lo = split(faces[...])
    faces_lo = faces_lo[:, 0 : LANES // 2]

    fault_count = fdest.shape[1]
    square = (fault_count, fault_count)
    dest_row = fdest[...].astype(F32)
    dest_col = as_column(dest_row)
    same = dest_col == dest_row
    rank_row = jnp.sum(
        jnp.where(same & (iota(square, 0) < iota(square, 1)), 1.0, 0.0), axis=0, keepdims=True
    )
    rank_col = jnp.sum(
        jnp.where(same & (iota(square, 1) < iota(square, 0)), 1.0, 0.0), axis=1, keepdims=True
    )
    row_numbers = frow[...].astype(F32) + 1.0
    info_left = jnp.where(
        dest_row == (iota((peer_total, fault_count), 0) // slots).astype(F32), row_numbers, 0.0
    )
    info_lane = INFO % LANES
    info_right = (
        rank_col == (iota((fault_count, LANES), 1) - info_lane).astype(F32)
    ).astype(F32)
    info = mm(info_left.astype(BF16), info_right.astype(BF16)) - 1.0
    info_lanes = iota((peer_total, LANES), 1)
    info_here = (info_lanes >= info_lane) & (info_lanes < info_lane + CAP)

    scale = scales[...]

    def derivative(x):
        x_hi, x_lo = split(x)
        both = mm(matrix_hi[...], jnp.concatenate([x_hi, x_lo], 1))
        return (both[:, :elements] + both[:, elements:] + mm(matrix_lo[...], x_hi)) * scale

    start = jnp.concatenate([state[...], jnp.zeros((padded - width, elements), F32)], 0)
    factor = EARTH_STEP
    integral = factor * start
    current = start
    for power in range(1, ORDER):
        current = derivative(current)
        factor = factor * EARTH_STEP / (power + 1)
        integral = integral + factor * current

    parts = jnp.concatenate(
        [
            jnp.concatenate(
                [
                    integral[p * basis : (p + 1) * basis],
                    jnp.zeros((LANES // 2 - basis, elements), F32),
                ],
                0,
            )
            for p in range(quantities)
        ],
        1,
    )
    parts_hi, parts_lo = split(parts)
    every = mm(faces_hi, jnp.concatenate([parts_hi, parts_lo], 0)) + mm(faces_lo, parts_hi)
    face_width = quantities * FACE_ROWS
    trace_rows = traces_out.shape[1]

    def face_block(f, q):
        return every[f * FACE_ROWS : (f + 1) * FACE_ROWS, q * elements : (q + 1) * elements]

    table = jnp.concatenate(
        [jnp.concatenate([face_block(f, q) for q in range(quantities)], 0) for f in range(4)], 1
    )
    table = jnp.concatenate([table, jnp.zeros((trace_rows - face_width, 4 * elements), F32)], 0)
    table_hi, table_lo = split(table)
    picked = mm(hot[...], table_hi, 1, 1) + mm(hot[...], table_lo, 1, 1)
    traces_out[:, 0:LANES] = picked[0:send_total, 0:LANES]
    traces_out[0:peer_total, LANES:] = jnp.where(
        info_here, info, picked[0:peer_total, LANES:]
    )
    traces_out[peer_total:, LANES:] = picked[peer_total:send_total, LANES:]
    own_trace = picked[send_total:]

    def peer_block(index, rows):
        return pl.ds(pl.multiple_of(index * rows, rows), rows)

    order = sorted(range(1, sub_count), key=lambda k: -min(k, sub_count - k))
    trace_copies = []
    for k in order:
        _, peer = device(0, k)
        trace_copies.append(
            (
                0,
                remote(
                    traces_out.at[peer_block(peer, slots), :],
                    traces_in.at[peer_block(sub, slots), :],
                    trace_send.at[k], trace_recv.at[k], 0, k,
                ),
            )
        )
    for i, dm in enumerate((1, -1)):
        source = peer_total + (edge_slots if dm > 0 else 0)
        target = peer_total + (0 if dm > 0 else edge_slots)
        trace_copies.append(
            (
                dm,
                remote(
                    traces_out.at[source : source + edge_slots, :],
                    traces_in.at[target : target + edge_slots, :],
                    trace_send.at[sub_count + i], trace_recv.at[sub_count + i], dm, 0,
                ),
            )
        )
    pl.semaphore_wait(
        barrier, sub_count - 1 + 3 * (neighbour[1].astype(I32) + neighbour[-1].astype(I32))
    )
    start_all(trace_copies)
    own_block = pltpu.make_async_copy(
        traces_out.at[peer_block(sub, slots), :], traces_in.at[peer_block(sub, slots), :],
        trace_recv.at[0],
    )
    own_block.start()

    for load in loads[15:]:
        load.wait()
    for i, first in enumerate((tile_rows - 8, 0)):
        rows_out[i, 0:2] = vel[:, first : first + 8, :]
        rows_out[i, 2] = depth[first : first + 8, :]
    fields = (vel[0], vel[1], depth[...])
    group = RIM * (tile_rows // 8)
    for i, last in enumerate((True, False)):
        packed = pack_edge(fields[0], last, 0)
        for k in (1, 2):
            packed = packed + pack_edge(fields[k], last, k * group)
        cols_out[i] = packed

    def rows_of_fields(dm, lanes):
        i = 0 if dm > 0 else 1
        return rows_out.at[i] if lanes is None else rows_out.at[i, :, :, lanes]

    field_copies = rim_copies(
        rows_of_fields, cols_out, rows_in, cols_in, corner_in, rim_send, rim_recv
    )
    start_all(field_copies)

    base = start + derivative(integral)
    lifts[...] = jnp.zeros(lifts.shape, F32)
    for f in range(4):
        lifts[f * FACE_ROWS : f * FACE_ROWS + lift.shape[0], :] = lift[:, f, :]
    lift_hi, lift_lo = split(jnp.transpose(lifts[...]))
    lift_hi = jnp.concatenate([lift_hi, lift_hi], 1)
    hot_in = hot[send_total:, :]
    hot_in = jnp.concatenate([hot_in, hot_in], 0)

    face_col, face_row = iota((trace_rows, 1), 0), iota((1, trace_rows), 1)
    quantity_col = sum((face_col >= FACE_ROWS * k).astype(I32) for k in range(1, quantities + 1))
    quantity_row = sum((face_row >= FACE_ROWS * k).astype(I32) for k in range(1, quantities + 1))
    exact = functools.partial(
        lax.dot_general, precision=lax.Precision.HIGHEST, preferred_element_type=F32
    )
    flux_left = exact(
        (quantity_col == iota((trace_rows, quantities), 1)).astype(F32), flux[...],
        (((1,), (1,)), ((), ())),
    )
    flux_wide = exact(
        flux_left, (quantity_row == iota((quantities, trace_rows), 0)).astype(F32),
        (((1,), (0,)), ((), ())),
    )
    same_face = face_col - FACE_ROWS * quantity_col == face_row - FACE_ROWS * quantity_row
    flux_hi, flux_lo = split(jnp.where(same_face, flux_wide, 0.0))

    rows_here = iota((padded, 1), 0)
    row_quantity = sum((rows_here >= basis * k).astype(I32) for k in range(1, quantities + 1))
    wanted = (rows_here - basis * row_quantity) * quantities + row_quantity
    wanted = jnp.where(rows_here < width, wanted, -1)
    permute = (iota((padded, width), 1) == wanted).astype(F32).astype(BF16)
    uplift_hi, uplift_lo = split(uplift[...])
    uplift_hi = mm(permute, uplift_hi).astype(BF16)
    uplift_lo = mm(permute, uplift_lo).astype(BF16)

    item_slots = sub_count * CAP
    place = (
        iota((item_slots, fault_count), 0).astype(F32) == dest_row * float(CAP) + rank_row
    ).astype(F32)
    elem_col = as_column(felem[...].astype(F32))
    elem_hot = (elem_col == iota((fault_count, elements), 1).astype(F32)).astype(F32)
    choose = mm(place.astype(BF16), elem_hot.astype(BF16)).astype(BF16)
    choose = jnp.concatenate([choose, choose], 1)
    weighting = 0.3 + 0.7 * fslip[...].astype(F32)
    weight_col = jnp.sum(place * weighting, axis=1, keepdims=True)

    own_block.wait()
    received_all(trace_copies)
    slot_col = iota((send_total, 1), 0)
    missing = ((slot_col >= peer_total) & (slot_col < peer_total + edge_slots) & (me == 0)) | (
        (slot_col >= peer_total + edge_slots) & (me == mesh_count - 1)
    )
    difference = jnp.where(missing, 0.0, traces_in[...]) - own_trace
    diff_hi, diff_lo = split(difference)
    mixed = mm(flux_hi, jnp.concatenate([diff_hi, diff_lo], 0), 1, 1)
    mixed = mixed[:, :send_total] + mixed[:, send_total:] + mm(flux_lo, diff_hi, 1, 1)
    scattered = mm(jnp.concatenate(split(mixed), 1), hot_in)
    gathered = jnp.concatenate(
        [
            jnp.concatenate(
                [
                    scattered[q * FACE_ROWS : (q + 1) * FACE_ROWS, f * elements : (f + 1) * elements]
                    for f in range(4)
                ],
                0,
            )
            for q in range(quantities)
        ],
        1,
    )
    gathered_hi, gathered_lo = split(gathered)
    lifted = mm(lift_hi, jnp.concatenate([gathered_hi, gathered_lo], 0)) + mm(lift_lo, gathered_hi)
    face_sum = jnp.concatenate(
        [lifted[:, q * elements : (q + 1) * elements] for q in range(quantities)]
        + [jnp.zeros((padded - width, elements), F32)],
        0,
    )
    new_state = base + face_sum
    new_out[...] = new_state[0:width]

    columns = mm(choose, jnp.concatenate(split(new_state), 1), 1, 1)
    columns_hi, columns_lo = split(columns)
    items = mm(columns_hi, uplift_hi) + mm(columns_lo, uplift_hi) + mm(columns_hi, uplift_lo)
    items_out[...] = items * weight_col
    item_copies = []
    for k in order:
        _, peer = device(0, k)
        item_copies.append(
            (
                0,
                remote(
                    items_out.at[peer_block(peer, CAP), :], items_in.at[peer_block(sub, CAP), :],
                    item_send.at[k], item_recv.at[k], 0, k,
                ),
            )
        )
    start_all(item_copies)
    own_items = pltpu.make_async_copy(
        items_out.at[peer_block(sub, CAP), :], items_in.at[peer_block(sub, CAP), :], item_recv.at[0]
    )
    own_items.start()

    got_info = traces_in[0:peer_total, LANES:]
    first_rows = jnp.concatenate([got_info[s * slots : s * slots + 1] for s in range(sub_count)], 0)
    landing_col = as_column(first_rows, info_lane)
    landing = (landing_col == iota((item_slots, LANES), 1).astype(F32)).astype(F32)
    landing = jnp.transpose(landing)[0:tile_rows].astype(BF16)
    landing = jnp.concatenate([landing, landing], 1)

    received_all(field_copies)

    def corners_of(ref, k=None):
        return [
            ref[WAY[way] - 4] if k is None else ref[WAY[way] - 4, k]
            for way in ((-1, -1), (-1, 1), (1, -1), (1, 1))
        ]

    extended = [
        extend(
            fields[k], rows_in[WAY[(1, 0)], k], rows_in[WAY[(-1, 0)], k],
            cols_in[0], cols_in[1], corners_of(corner_in, k), k * group,
        )
        for k in range(3)
    ]
    shape = extended[0].shape
    ext_row, ext_lane = iota(shape, 0), iota(shape, 1)
    inside = (
        ((ext_row < tile_rows) | (ext_row >= tile_rows + RIM) | neighbour[1])
        & ((ext_row < tile_rows + RIM) | neighbour[-1])
        & ((ext_lane < tile_cols) | (ext_lane >= tile_cols + LANES // 2) | (sub < sub_count - 1))
        & ((ext_lane < tile_cols + LANES // 2) | (sub > 0))
    )
    flow = [jnp.where(inside, extended[axis], 0.0) for axis in (0, 1)]
    deep = jnp.where(inside, extended[2], 0.0)
    change = COURANT * (shifted(deep * flow[0], 0) + shifted(deep * flow[1], 1))

    own_items.wait()
    received_all(item_copies)
    deposit = mm(landing, jnp.concatenate(split(items_in[...]), 0))
    level = sea[...] + deposit
    height[...] = level
    hcols_out[0] = pack_edge(level, True, 0)
    hcols_out[1] = pack_edge(level, False, 0)

    def rows_of_height(dm, lanes):
        rows = slice(tile_rows - 8, tile_rows) if dm > 0 else slice(0, 8)
        return height.at[rows, :] if lanes is None else height.at[rows, lanes]

    high_copies = rim_copies(
        rows_of_height, hcols_out, hrows_in, hcols_in, hcorner_in, high_send, high_recv
    )
    start_all(high_copies)
    for copies in (trace_copies, field_copies, item_copies):
        sent_all(copies)

    received_all(high_copies)
    level = extend(
        level, hrows_in[WAY[(1, 0)]], hrows_in[WAY[(-1, 0)]], hcols_in[0], hcols_in[1],
        corners_of(hcorner_in), 0,
    )
    level = jnp.where(inside, level, 0.0) - change
    flow = [flow[axis] - COURANT * shifted(level, axis) for axis in (0, 1)]
    level = jnp.where(inside, level, 0.0)
    level = level - COURANT * (shifted(deep * flow[0], 0) + shifted(deep * flow[1], 1))
    flow = [flow[axis] - COURANT * shifted(level, axis) for axis in (0, 1)]
    sea_out[...] = level[0:tile_rows, 0:tile_cols]
    flow_out[0] = flow[0][0:tile_rows, 0:tile_cols]
    flow_out[1] = flow[1][0:tile_rows, 0:tile_cols]
    sent_all(high_copies)


def store_kernel(new_in, sea_in, flow_in, new_out, sea_out, flow_out, sems):
    copies = [
        pltpu.make_async_copy(src, dst, sems.at[i])
        for i, (src, dst) in enumerate(
            ((new_in, new_out), (sea_in, sea_out), (flow_in, flow_out))
        )
    ]
    for copy in copies:
        copy.start()
    for copy in copies:
        copy.wait()


def body(mesh_count, sub_count, *arguments):
    (
        state, scales, stiffness, jacobians, projection, lifting, flux_matrix,
        peer_send, peer_recv, edge_send, edge_recv, uplift_map,
        fault_elem, fault_dest, fault_row, fault_slip, sea_level, velocity, depth,
    ) = arguments
    basis, quantities, elements = state.shape
    width = basis * quantities
    faults = fault_elem.shape[0]
    rows, cols = sea_level.shape
    slots, edge_slots = peer_send.shape[2], edge_send.shape[2]
    operands = (
        jnp.transpose(state, (1, 0, 2)).reshape(width, elements),
        scales.reshape(1, elements),
        stiffness.reshape(3 * basis, basis),
        jnp.transpose(jacobians, (1, 0, 2)),
        jnp.transpose(projection, (1, 0, 2)),
        jnp.transpose(lifting, (2, 0, 1)),
        flux_matrix,
        peer_send.reshape(sub_count, slots),
        peer_recv.reshape(sub_count, slots),
        edge_send.reshape(2, edge_slots),
        edge_recv.reshape(2, edge_slots),
        uplift_map,
        fault_elem.reshape(1, faults),
        fault_dest.reshape(1, faults),
        fault_row.reshape(1, faults),
        fault_slip.reshape(1, faults),
        sea_level,
        velocity,
        depth,
    )
    padded = -(-width // LANES) * LANES
    trace_lanes = 2 * LANES
    send_total = sub_count * slots + 2 * edge_slots
    item_slots = sub_count * CAP
    vmem, dma = pltpu.VMEM, pltpu.SemaphoreType.DMA
    held = [vmem(x.shape, x.dtype) for x in operands]
    scratch = held + [
        vmem((3 * basis, padded), F32),
        vmem((padded, padded), BF16),
        vmem((padded, padded), BF16),
        vmem((2 * send_total, 4 * elements), BF16),
        vmem((4 * FACE_ROWS, LANES), F32),
        vmem((4 * FACE_ROWS, basis), F32),
        vmem((send_total, trace_lanes), F32),
        vmem((send_total, trace_lanes), F32),
        vmem((item_slots, cols), F32),
        vmem((item_slots, cols), F32),
        vmem((2, 3, 8, cols), F32),
        vmem((2, 8, LANES), F32),
        vmem((2, 3, 8, cols), F32),
        vmem((2, 8, LANES), F32),
        vmem((4, 3, 8, LANES), F32),
        vmem((rows, cols), F32),
        vmem((2, 8, LANES), F32),
        vmem((2, 8, cols), F32),
        vmem((2, 8, LANES), F32),
        vmem((4, 8, LANES), F32),
        dma((len(operands),)),
        dma((8,)),
        dma((8,)),
        dma((sub_count + 2,)),
        dma((sub_count + 2,)),
        dma((sub_count,)),
        dma((sub_count,)),
        dma((8,)),
        dma((8,)),
    ]
    hbm, local = pl.BlockSpec(memory_space=pltpu.HBM), pl.BlockSpec(memory_space=pltpu.VMEM)
    shapes = ((width, elements), (rows, cols), (2, rows, cols))
    results = pl.pallas_call(
        functools.partial(kernel, mesh_count, sub_count),
        out_shape=tuple(vmem(shape, F32) for shape in shapes),
        in_specs=[hbm] * len(operands),
        out_specs=(local,) * 3,
        scratch_shapes=scratch,
        compiler_params=pltpu.CompilerParams(
            collective_id=0, has_side_effects=True, vmem_limit_bytes=40 * 1024 * 1024
        ),
    )(*[pltpu.with_memory_space_constraint(x, pltpu.HBM) for x in operands])
    new_state, sea_out, flow_out = pl.pallas_call(
        store_kernel,
        out_shape=tuple(pltpu.HBM(shape, F32) for shape in shapes),
        in_specs=[local] * 3,
        out_specs=(hbm,) * 3,
        scratch_shapes=[dma((3,))],
    )(*[pltpu.with_memory_space_constraint(x, pltpu.VMEM) for x in results])
    new_state = jnp.transpose(new_state.reshape(quantities, basis, elements), (1, 0, 2))
    return new_state, sea_out, flow_out


def solution(mesh):
    device = P(("mesh", "sub"))
    return jax.shard_map(
        functools.partial(body, mesh.shape["mesh"], mesh.shape["sub"]),
        mesh=mesh,
        in_specs=(
            P(None, None, ("mesh", "sub")),
            device,
            P(),
            P(),
            P(),
            P(),
            P(),
            P(("mesh", "sub"), None, None),
            P(("mesh", "sub"), None, None),
            P(("mesh", "sub"), None, None),
            P(("mesh", "sub"), None, None),
            P(),
            device,
            P(("mesh", "sub"), None),
            device,
            device,
            P("mesh", "sub"),
            P(None, "mesh", "sub"),
            P("mesh", "sub"),
        ),
        out_specs=(P(None, None, ("mesh", "sub")), P("mesh", "sub"), P(None, "mesh", "sub")),
        check_vma=False,
    )
```

```python
import functools

import jax
import jax.numpy as jnp
from jax import lax
from jax.experimental import pallas as pl
from jax.experimental.pallas import tpu as pltpu
from jax.sharding import PartitionSpec as P

ORDER = 5
CAP = 16
EARTH_STEP = 0.5
COURANT = 0.45
MESH = pl.DeviceIdType.MESH
F32, BF16, I32 = jnp.float32, jnp.bfloat16, jnp.int32
LANES = 128
FACE_ROWS = 24
INFO = 224
RIM = 4
TURN_LOW, TURN_HIGH = 1, 2
DIRECTIONS = ((1, 0), (-1, 0), (0, 1), (0, -1), (1, 1), (1, -1), (-1, 1), (-1, -1))
WAY = {d: i for i, d in enumerate(DIRECTIONS)}


def split(x):
    high = x.astype(BF16)
    return high, (x - high.astype(F32)).astype(BF16)


def mm(a, b, left=1, right=0):
    return lax.dot_general(a, b, (((left,), (right,)), ((), ())), preferred_element_type=F32)


def iota(shape, axis):
    return lax.broadcasted_iota(I32, shape, axis)


def repeat_rows(rows, count):
    return jnp.concatenate(
        [jnp.broadcast_to(rows[i : i + 1], (count, rows.shape[1])) for i in range(rows.shape[0])], 0
    )


def as_column(rows, first=0, backward=False):
    count = rows.shape[1] if first == 0 else CAP
    wide = repeat_rows(rows, count)
    turn = iota(wide.shape, 0) & (count - 1)
    mine = (count - 1 - turn if backward else turn) == iota(wide.shape, 1) - first
    return jnp.sum(jnp.where(mine, wide, 0.0), axis=1, keepdims=True)


def pack_edge(array, last, base):
    lane = iota((8, LANES), 1)
    start = array.shape[1] - LANES if last else 0
    keep = lane >= LANES - RIM if last else lane < RIM
    packed = jnp.zeros((8, LANES), F32)
    for g in range(array.shape[0] // 8):
        tile = jnp.where(keep, array[8 * g : 8 * g + 8, start : start + LANES], 0.0)
        packed = packed + pltpu.roll(tile, (RIM * (g + 1 if last else g) + base) % LANES, 1)
    return packed


def extend(array, low, high, left, right, corners, base):
    lane, row = iota((8, LANES), 1), iota((8, LANES), 0)
    side = jnp.concatenate(
        [
            jnp.where(
                lane < LANES // 2,
                pltpu.roll(right, (-RIM * g - base) % LANES, 1),
                pltpu.roll(left, (LANES - RIM - RIM * g - base) % LANES, 1),
            )
            for g in range(array.shape[0] // 8)
        ],
        0,
    )
    down_right, down_left, up_right, up_left = corners
    corner = jnp.where(
        row < RIM,
        jnp.where(lane < LANES // 2, down_right, down_left),
        jnp.where(lane < LANES // 2, up_right, up_left),
    )
    bottom = jnp.where(iota(low.shape, 0) < RIM, high, low)
    return jnp.concatenate(
        [jnp.concatenate([array, side], 1), jnp.concatenate([bottom, corner], 1)], 0
    )


def shifted(array, axis):
    size = array.shape[axis]
    return (pltpu.roll(array, size - 1, axis) - pltpu.roll(array, 1, axis)) * 0.5


def kernel(mesh_count, sub_count, *refs):
    (
        state_in, scales_in, stiff_in, jac_in, proj_in, lift_in, flux_in,
        psend_in, precv_in, esend_in, erecv_in, uplift_in,
        felem_in, fdest_in, frow_in, fslip_in, sea_in, vel_in, depth_in,
        new_out, sea_out, flow_out,
        state, scales, stiff, jac, proj, lift, flux,
        psend, precv, esend, erecv, uplift,
        felem, fdest, frow, fslip, sea, vel, depth,
        spread, matrix_hi, matrix_lo, hot, faces, lifts, traces_out, traces_in, items_out, items_in,
        rows_out, cols_out, rows_in, cols_in, corner_in,
        rims_out, rims_in, sides_out, sides_in,
        load_sem, rim_send, rim_recv, trace_send, trace_recv,
        item_send, item_recv, side_send, side_recv, edge_send, edge_recv,
    ) = refs
    quantities, basis = flux.shape[0], stiff.shape[1]
    width = quantities * basis
    padded = matrix_hi.shape[0]
    elements = state.shape[1]
    slots = psend.shape[1]
    edge_slots = esend.shape[1]
    peer_total = sub_count * slots
    send_total = peer_total + 2 * edge_slots
    tile_rows, tile_cols = depth.shape
    me, sub = lax.axis_index("mesh"), lax.axis_index("sub")
    neighbour = {1: me < mesh_count - 1, -1: me > 0}

    def device(dm, ds):
        return (me + dm, lax.rem(sub + ds + sub_count, sub_count))

    loads = [
        pltpu.make_async_copy(src, dst, load_sem.at[i])
        for i, (src, dst) in enumerate(
            (
                (stiff_in, stiff), (jac_in, jac), (state_in, state), (scales_in, scales),
                (psend_in, psend), (precv_in, precv), (esend_in, esend), (erecv_in, erecv),
                (proj_in, proj), (felem_in, felem), (fdest_in, fdest), (frow_in, frow),
                (fslip_in, fslip), (flux_in, flux), (lift_in, lift),
                (vel_in, vel), (depth_in, depth), (uplift_in, uplift), (sea_in, sea),
            )
        )
    ]
    for load in loads:
        load.start()
    barrier = pltpu.get_barrier_semaphore()

    def greet(dm, ds):
        pl.semaphore_signal(barrier, inc=1, device_id=device(dm, ds), device_id_type=MESH)

    for k in range(1, sub_count):
        greet(0, k)
    for side in (1, -1):

        @pl.when(neighbour[side])
        def _():
            for ds in range(sub_count):
                greet(side, ds)

    def remote(src, dst, send_sem, recv_sem, dm, ds):
        return pltpu.make_async_remote_copy(
            src_ref=src, dst_ref=dst, send_sem=send_sem, recv_sem=recv_sem,
            device_id=device(dm, ds), device_id_type=MESH,
        )

    def each(copies, act):
        for dm, copy in copies:
            if dm == 0:
                act(copy)
        for side in (1, -1):
            some = [copy for dm, copy in copies if dm == side]
            if some:

                @pl.when(neighbour[side])
                def _():
                    for copy in some:
                        act(copy)

    def start_all(copies):
        each(copies, lambda copy: copy.start())

    def sent_all(copies):
        each(copies, lambda copy: copy.wait_send())

    def received_all(copies):
        each([(-dm, copy) for dm, copy in copies], lambda copy: copy.wait_recv())

    def rim_copies(rows_of, cols_ref, rows_ref, cols_got, corner_ref, send_sem, recv_sem):
        copies = []
        for i, (dm, ds) in enumerate(DIRECTIONS):
            if ds == 0:
                src, dst = rows_of(dm, None), rows_ref.at[i]
            elif dm == 0:
                src, dst = cols_ref.at[i - 2], cols_got.at[i - 2]
            else:
                lanes = slice(tile_cols - LANES, tile_cols) if ds > 0 else slice(0, LANES)
                src, dst = rows_of(dm, lanes), corner_ref.at[i - 4]
            copies.append((dm, remote(src, dst, send_sem.at[i], recv_sem.at[i], dm, ds)))
        return copies

    lane = iota((1, padded), 1)
    of_quantity = sum((lane >= basis * k).astype(I32) for k in range(1, quantities + 1))
    of_basis = lane - basis * of_quantity
    spread_basis = (iota((basis, padded), 0) == of_basis).astype(F32).astype(BF16)
    spread_quantity = (iota((quantities, padded), 0) == of_quantity).astype(F32)
    for load in loads[0:15]:
        load.wait()
    stiff_hi, stiff_lo = split(stiff[...])
    spread[...] = mm(stiff_hi, spread_basis) + mm(stiff_lo, spread_basis)
    jac_wide = [
        lax.dot_general(
            jac[:, d, :], spread_quantity, (((0,), (0,)), ((), ())),
            precision=lax.Precision.HIGHEST, preferred_element_type=F32,
        )
        for d in range(3)
    ]

    def matrix_rows(q):
        if q == quantities:
            return jnp.zeros((padded - width, padded), F32)
        block = spread[0:basis, :] * jac_wide[0][q : q + 1]
        for d in (1, 2):
            block = block + spread[d * basis : (d + 1) * basis, :] * jac_wide[d][q : q + 1]
        return block

    at = 0
    for q in range(0, quantities, 2):
        high, low = split(jnp.concatenate([matrix_rows(q), matrix_rows(q + 1)], 0))
        matrix_hi[at : at + high.shape[0], :] = high
        matrix_lo[at : at + high.shape[0], :] = low
        at = at + high.shape[0]

    codes = jnp.concatenate(
        [as_column(ref[...].astype(F32)) for ref in (psend, esend, precv, erecv)], 0
    )
    face_lane = iota((1, 4 * elements), 1)
    key = (4 * (face_lane & (elements - 1)) + face_lane // elements).astype(F32)
    hot[...] = (codes == key).astype(F32).astype(BF16)
    faces[...] = jnp.zeros(faces.shape, F32)
    for f in range(4):
        for half in (0, LANES // 2):
            faces[f * FACE_ROWS : f * FACE_ROWS + proj.shape[0], half : half + basis] = proj[:, f, :]
    faces_hi, faces_lo = split(faces[...])
    faces_lo = faces_lo[:, 0 : LANES // 2]

    fault_count = fdest.shape[1]
    square = (fault_count, fault_count)
    dest_row = fdest[...].astype(F32)
    dest_col = as_column(dest_row)
    same = dest_col == dest_row
    rank_row = jnp.sum(
        jnp.where(same & (iota(square, 0) < iota(square, 1)), 1.0, 0.0), axis=0, keepdims=True
    )
    rank_col = jnp.sum(
        jnp.where(same & (iota(square, 1) < iota(square, 0)), 1.0, 0.0), axis=1, keepdims=True
    )
    row_numbers = frow[...].astype(F32) + 1.0
    info_row = iota((peer_total, 1), 0)
    info_turn = info_row & (slots - 1)
    info_dest = info_row // slots + jnp.where(
        info_turn == TURN_LOW, -1, jnp.where(info_turn == TURN_HIGH, 1, 0)
    )
    info_left = jnp.where(dest_row == info_dest.astype(F32), row_numbers, 0.0)
    info_lane = INFO % LANES
    info_right = (
        rank_col == (iota((fault_count, LANES), 1) - info_lane).astype(F32)
    ).astype(F32)
    info = mm(info_left.astype(BF16), info_right.astype(BF16)) - 1.0
    info_lanes = iota((peer_total, LANES), 1)
    info_here = (info_lanes >= info_lane) & (info_lanes < info_lane + CAP)

    scale = scales[...]

    def derivative(x):
        x_hi, x_lo = split(x)
        both = mm(matrix_hi[...], jnp.concatenate([x_hi, x_lo], 1))
        return (both[:, :elements] + both[:, elements:] + mm(matrix_lo[...], x_hi)) * scale

    start = jnp.concatenate([state[...], jnp.zeros((padded - width, elements), F32)], 0)
    factor = EARTH_STEP
    integral = factor * start
    current = start
    for power in range(1, ORDER):
        current = derivative(current)
        factor = factor * EARTH_STEP / (power + 1)
        integral = integral + factor * current

    parts = jnp.concatenate(
        [
            jnp.concatenate(
                [
                    integral[p * basis : (p + 1) * basis],
                    jnp.zeros((LANES // 2 - basis, elements), F32),
                ],
                0,
            )
            for p in range(quantities)
        ],
        1,
    )
    parts_hi, parts_lo = split(parts)
    every = mm(faces_hi, jnp.concatenate([parts_hi, parts_lo], 0)) + mm(faces_lo, parts_hi)
    face_width = quantities * FACE_ROWS
    trace_rows = traces_out.shape[1]

    def face_block(f, q):
        return every[f * FACE_ROWS : (f + 1) * FACE_ROWS, q * elements : (q + 1) * elements]

    table = jnp.concatenate(
        [jnp.concatenate([face_block(f, q) for q in range(quantities)], 0) for f in range(4)], 1
    )
    table = jnp.concatenate([table, jnp.zeros((trace_rows - face_width, 4 * elements), F32)], 0)
    table_hi, table_lo = split(table)
    picked = mm(hot[...], table_hi, 1, 1) + mm(hot[...], table_lo, 1, 1)
    traces_out[:, 0:LANES] = picked[0:send_total, 0:LANES]
    traces_out[0:peer_total, LANES:] = jnp.where(
        info_here, info, picked[0:peer_total, LANES:]
    )
    traces_out[peer_total:, LANES:] = picked[peer_total:send_total, LANES:]
    own_trace = picked[send_total:]

    def peer_block(index, rows):
        return pl.ds(pl.multiple_of(index * rows, rows), rows)

    order = sorted(range(1, sub_count), key=lambda k: -min(k, sub_count - k))
    trace_copies = []
    for k in order:
        _, peer = device(0, k)
        trace_copies.append(
            (
                0,
                remote(
                    traces_out.at[peer_block(peer, slots), :],
                    traces_in.at[peer_block(sub, slots), :],
                    trace_send.at[k], trace_recv.at[k], 0, k,
                ),
            )
        )
    for i, dm in enumerate((1, -1)):
        source = peer_total + (edge_slots if dm > 0 else 0)
        target = peer_total + (0 if dm > 0 else edge_slots)
        trace_copies.append(
            (
                dm,
                remote(
                    traces_out.at[source : source + edge_slots, :],
                    traces_in.at[target : target + edge_slots, :],
                    trace_send.at[sub_count + i], trace_recv.at[sub_count + i], dm, 0,
                ),
            )
        )
    pl.semaphore_wait(
        barrier,
        sub_count - 1 + sub_count * (neighbour[1].astype(I32) + neighbour[-1].astype(I32)),
    )
    start_all(trace_copies)
    own_block = pltpu.make_async_copy(
        traces_out.at[peer_block(sub, slots), :], traces_in.at[peer_block(sub, slots), :],
        trace_recv.at[0],
    )
    own_block.start()

    for load in loads[15:]:
        load.wait()
    for i, first in enumerate((tile_rows - 8, 0)):
        rows_out[i, 0:2] = vel[:, first : first + 8, :]
        rows_out[i, 2] = depth[first : first + 8, :]
        rows_out[i, 3] = sea[first : first + 8, :]
    fields = (vel[0], vel[1], depth[...], sea[...])
    group = RIM * (tile_rows // 8)
    for i, last in enumerate((True, False)):
        packed = pack_edge(fields[0], last, 0)
        for k in (1, 2, 3):
            packed = packed + pack_edge(fields[k], last, k * group)
        cols_out[i] = packed

    def rows_of_fields(dm, lanes):
        i = 0 if dm > 0 else 1
        return rows_out.at[i] if lanes is None else rows_out.at[i, :, :, lanes]

    field_copies = rim_copies(
        rows_of_fields, cols_out, rows_in, cols_in, corner_in, rim_send, rim_recv
    )
    start_all(field_copies)

    base = start + derivative(integral)
    lifts[...] = jnp.zeros(lifts.shape, F32)
    for f in range(4):
        lifts[f * FACE_ROWS : f * FACE_ROWS + lift.shape[0], :] = lift[:, f, :]
    lift_hi, lift_lo = split(jnp.transpose(lifts[...]))
    lift_hi = jnp.concatenate([lift_hi, lift_hi], 1)
    hot_in = hot[send_total:, :]
    hot_in = jnp.concatenate([hot_in, hot_in], 0)

    face_col, face_row = iota((trace_rows, 1), 0), iota((1, trace_rows), 1)
    quantity_col = sum((face_col >= FACE_ROWS * k).astype(I32) for k in range(1, quantities + 1))
    quantity_row = sum((face_row >= FACE_ROWS * k).astype(I32) for k in range(1, quantities + 1))
    exact = functools.partial(
        lax.dot_general, precision=lax.Precision.HIGHEST, preferred_element_type=F32
    )
    flux_left = exact(
        (quantity_col == iota((trace_rows, quantities), 1)).astype(F32), flux[...],
        (((1,), (1,)), ((), ())),
    )
    flux_wide = exact(
        flux_left, (quantity_row == iota((quantities, trace_rows), 0)).astype(F32),
        (((1,), (0,)), ((), ())),
    )
    same_face = face_col - FACE_ROWS * quantity_col == face_row - FACE_ROWS * quantity_row
    flux_hi, flux_lo = split(jnp.where(same_face, flux_wide, 0.0))

    rows_here = iota((padded, 1), 0)
    row_quantity = sum((rows_here >= basis * k).astype(I32) for k in range(1, quantities + 1))
    wanted = (rows_here - basis * row_quantity) * quantities + row_quantity
    wanted = jnp.where(rows_here < width, wanted, -1)
    permute = (iota((padded, width), 1) == wanted).astype(F32).astype(BF16)
    uplift_hi, uplift_lo = split(uplift[...])
    uplift_hi = mm(permute, uplift_hi).astype(BF16)
    uplift_lo = mm(permute, uplift_lo).astype(BF16)

    item_slots = sub_count * CAP
    place = (
        iota((item_slots, fault_count), 0).astype(F32) == dest_row * float(CAP) + rank_row
    ).astype(F32)
    elem_col = as_column(felem[...].astype(F32))
    elem_hot = (elem_col == iota((fault_count, elements), 1).astype(F32)).astype(F32)
    elem_hot = elem_hot.astype(BF16)
    choose = mm(place.astype(BF16), elem_hot).astype(BF16)
    weighting = 0.3 + 0.7 * fslip[...].astype(F32)
    weight_col = jnp.sum(place * weighting, axis=1, keepdims=True)
    rim_total = 2 * sub_count * RIM
    rim_row = iota((rim_total, 1), 0)
    rim_turn = rim_row & (RIM - 1)
    upward = rim_row >= rim_total // 2
    rim_target = jnp.where(
        upward,
        jnp.where(rim_turn > 0, tile_rows - RIM + rim_turn, -1),
        jnp.where(rim_turn < RIM - 1, rim_turn, -1),
    )
    rim_dest = (rim_row & (rim_total // 2 - 1)) // RIM
    rim_weight = jnp.where(
        (dest_row == rim_dest.astype(F32)) & (frow[...] == rim_target), weighting, 0.0
    )
    rim_hi, rim_lo = split(rim_weight)
    rim_hi, rim_lo = split(mm(rim_hi, elem_hot) + mm(rim_lo, elem_hot))
    choose = jnp.concatenate([choose, rim_hi], 0)
    choose = jnp.concatenate([choose, choose], 1)

    own_block.wait()
    received_all(trace_copies)
    slot_col = iota((send_total, 1), 0)
    missing = ((slot_col >= peer_total) & (slot_col < peer_total + edge_slots) & (me == 0)) | (
        (slot_col >= peer_total + edge_slots) & (me == mesh_count - 1)
    )
    difference = jnp.where(missing, 0.0, traces_in[...]) - own_trace
    diff_hi, diff_lo = split(difference)
    mixed = mm(flux_hi, jnp.concatenate([diff_hi, diff_lo], 0), 1, 1)
    mixed = mixed[:, :send_total] + mixed[:, send_total:] + mm(flux_lo, diff_hi, 1, 1)
    scattered = mm(jnp.concatenate(split(mixed), 1), hot_in)
    gathered = jnp.concatenate(
        [
            jnp.concatenate(
                [
                    scattered[q * FACE_ROWS : (q + 1) * FACE_ROWS, f * elements : (f + 1) * elements]
                    for f in range(4)
                ],
                0,
            )
            for q in range(quantities)
        ],
        1,
    )
    gathered_hi, gathered_lo = split(gathered)
    lifted = mm(lift_hi, jnp.concatenate([gathered_hi, gathered_lo], 0)) + mm(lift_lo, gathered_hi)
    face_sum = jnp.concatenate(
        [lifted[:, q * elements : (q + 1) * elements] for q in range(quantities)]
        + [jnp.zeros((padded - width, elements), F32)],
        0,
    )
    new_state = base + face_sum
    new_out[...] = new_state[0:width]

    new_hi, new_lo = split(new_state)
    columns = mm(choose, jnp.concatenate([new_hi, new_lo], 1), 1, 1)
    columns = jnp.concatenate(
        [columns[:item_slots], columns[item_slots:] + mm(rim_lo, new_hi, 1, 1)], 0
    )
    columns_hi, columns_lo = split(columns)
    uplifted = mm(columns_hi, uplift_hi) + mm(columns_lo, uplift_hi) + mm(columns_hi, uplift_lo)
    rims = uplifted[item_slots:]
    half = rim_total // 2
    rim_lane = iota((half, LANES), 1)
    for i, (part, high_shift, low_shift) in enumerate(
        ((rims[:half], -RIM, RIM), (rims[half:], 1 - 2 * RIM, 1))
    ):
        corner = []
        for shift, tile in (
            (high_shift, jnp.where(rim_lane < RIM - 1, part[:, 0:LANES], 0.0)),
            (low_shift, jnp.where(rim_lane > LANES - RIM, part[:, tile_cols - LANES :], 0.0)),
        ):
            tile = pltpu.roll(tile, 0, 1, stride=8, stride_axis=0)
            tile = tile + pltpu.roll(tile, 1, 0)
            tile = tile + pltpu.roll(tile, 2, 0)
            corner.append(pltpu.roll(tile, shift % half, 0))
        free = (iota((half, LANES), 0) & (RIM - 1)) == (0 if i else RIM - 1)
        first = jnp.where(free, corner[0] + corner[1], part[:, 0:LANES])
        for d in range(sub_count):
            rims_out[i, d, :, 0:LANES] = first[d * RIM : (d + 1) * RIM]
            rims_out[i, d, :, LANES:] = part[d * RIM : (d + 1) * RIM, LANES:]

    edge_copies = []
    for k in [*order, 0]:
        _, peer = device(0, k)
        for i, dm in enumerate((-1, 1)):
            edge_copies.append(
                (
                    dm,
                    remote(
                        rims_out.at[i, peer], rims_in.at[i, sub],
                        edge_send.at[i, k], edge_recv.at[i, k], dm, k,
                    ),
                )
            )
    start_all(edge_copies)
    items = uplifted[:item_slots] * weight_col
    items_out[...] = items
    item_copies = []
    for k in order:
        _, peer = device(0, k)
        item_copies.append(
            (
                0,
                remote(
                    items_out.at[peer_block(peer, CAP), :], items_in.at[peer_block(sub, CAP), :],
                    item_send.at[k], item_recv.at[k], 0, k,
                ),
            )
        )
    start_all(item_copies)
    own_items = pltpu.make_async_copy(
        items_out.at[peer_block(sub, CAP), :], items_in.at[peer_block(sub, CAP), :], item_recv.at[0]
    )
    own_items.start()
    side_lane = iota((CAP, LANES), 1)
    firsts, lasts = [], []
    for d in range(sub_count):
        own = items[d * CAP : (d + 1) * CAP]
        first = jnp.where(side_lane < RIM - 1, own[:, 0:LANES], 0.0)
        last = jnp.where(side_lane > LANES - RIM, own[:, tile_cols - LANES :], 0.0)
        first = pltpu.roll(first, 0, 1, stride=RIM, stride_axis=0)
        last = pltpu.roll(last, LANES // 2 + RIM - 1, 1, stride=RIM, stride_axis=0)
        firsts.append(jnp.sum(first, axis=0, keepdims=True))
        lasts.append(jnp.sum(last, axis=0, keepdims=True))
    for d in range(sub_count):
        sides_out[d] = firsts[(d + 1) % sub_count] + lasts[(d - 1) % sub_count]
    side_copies = []
    for k in order:
        _, peer = device(0, k)
        side_copies.append(
            (
                0,
                remote(
                    sides_out.at[peer], sides_in.at[sub], side_send.at[k], side_recv.at[k], 0, k
                ),
            )
        )
    start_all(side_copies)
    own_side = pltpu.make_async_copy(sides_out.at[sub], sides_in.at[sub], side_recv.at[0])
    own_side.start()

    got_info = traces_in[0:peer_total, LANES:]

    def landing(turn, backward=False):
        rows = jnp.concatenate(
            [got_info[s * slots + turn : s * slots + turn + 1] for s in range(sub_count)], 0
        )
        column = as_column(rows, info_lane, backward)
        hits = (column == iota((item_slots, LANES), 1).astype(F32)).astype(F32)
        return jnp.transpose(hits)[0:tile_rows].astype(BF16)

    land = landing(0)
    land = jnp.concatenate([land, land], 1)
    land_high, land_low = landing(TURN_HIGH, True), landing(TURN_LOW, True)
    land_side = jnp.concatenate([land_high, land_low, land_high, land_low], 1)

    received_all(field_copies)

    def corners_of(k):
        return [
            corner_in[WAY[way] - 4, k] for way in ((-1, -1), (-1, 1), (1, -1), (1, 1))
        ]

    extended = [
        extend(
            fields[k], rows_in[WAY[(1, 0)], k], rows_in[WAY[(-1, 0)], k],
            cols_in[0], cols_in[1], corners_of(k), k * group,
        )
        for k in range(4)
    ]
    shape = extended[0].shape
    ext_row, ext_lane = iota(shape, 0), iota(shape, 1)
    inside = (
        ((ext_row < tile_rows) | (ext_row >= tile_rows + RIM) | neighbour[1])
        & ((ext_row < tile_rows + RIM) | neighbour[-1])
        & ((ext_lane < tile_cols) | (ext_lane >= tile_cols + LANES // 2) | (sub < sub_count - 1))
        & ((ext_lane < tile_cols + LANES // 2) | (sub > 0))
    )
    flow = [jnp.where(inside, extended[axis], 0.0) for axis in (0, 1)]
    deep = jnp.where(inside, extended[2], 0.0)
    calm = jnp.where(inside, extended[3], 0.0) - COURANT * (
        shifted(deep * flow[0], 0) + shifted(deep * flow[1], 1)
    )
    for copies in (trace_copies, field_copies):
        sent_all(copies)

    own_side.wait()
    received_all(side_copies)
    beside = []
    last_turn = LANES - RIM * (CAP - 1)
    for shift, keep in (
        (last_turn, side_lane < RIM - 1),
        (last_turn + LANES // 2 - RIM + 1, side_lane > LANES - RIM),
    ):
        for s in range(sub_count):
            wide = jnp.broadcast_to(sides_in[s], (CAP, LANES))
            wide = pltpu.roll(wide, shift % LANES, 1, stride=RIM, stride_axis=0)
            beside.append(jnp.where(keep, wide, 0.0))
    beside_hi, beside_lo = split(jnp.concatenate(beside, 0))
    side = mm(land_side, jnp.concatenate([beside_hi, beside_lo], 0))

    own_items.wait()
    received_all(item_copies)
    received_all(edge_copies)
    deposit = mm(land, jnp.concatenate(split(items_in[...]), 0))
    bottom = []
    for i in (0, 1):
        total = rims_in[i, 0]
        for s in range(1, sub_count):
            total = total + rims_in[i, s]
        bottom.append(total)
    bottom = jnp.concatenate(bottom, 0)
    bottom_lane, bottom_row = iota((8, LANES), 1), iota((8, LANES), 0)
    corner = []
    for free in (RIM - 1, RIM):
        wide = jnp.broadcast_to(bottom[free : free + 1, 0:LANES], (8, LANES))
        around = []
        for turn in (1, -1):
            tile = pltpu.roll(wide, lax.rem(8 * LANES - 8 * RIM * (sub + turn), LANES), 1)
            rows = tile
            for r in range(1, RIM):
                rows = jnp.where(
                    (bottom_row & (RIM - 1)) == r, pltpu.roll(tile, LANES - 8 * r, 1), rows
                )
            around.append(rows)
        corner.append(jnp.where(bottom_lane < LANES // 2, around[0], around[1]))
    corner = jnp.where(bottom_row < RIM, corner[0], corner[1])
    raised = jnp.concatenate(
        [jnp.concatenate([deposit, side], 1), jnp.concatenate([bottom, corner], 1)], 0
    )

    level = calm + jnp.where(inside, raised, 0.0)
    flow = [flow[axis] - COURANT * shifted(level, axis) for axis in (0, 1)]
    level = jnp.where(inside, level, 0.0)
    level = level - COURANT * (shifted(deep * flow[0], 0) + shifted(deep * flow[1], 1))
    flow = [flow[axis] - COURANT * shifted(level, axis) for axis in (0, 1)]
    sea_out[...] = level[0:tile_rows, 0:tile_cols]
    flow_out[0] = flow[0][0:tile_rows, 0:tile_cols]
    flow_out[1] = flow[1][0:tile_rows, 0:tile_cols]
    for copies in (edge_copies, item_copies, side_copies):
        sent_all(copies)


def store_kernel(new_in, sea_in, flow_in, new_out, sea_out, flow_out, sems):
    copies = [
        pltpu.make_async_copy(src, dst, sems.at[i])
        for i, (src, dst) in enumerate(
            ((new_in, new_out), (sea_in, sea_out), (flow_in, flow_out))
        )
    ]
    for copy in copies:
        copy.start()
    for copy in copies:
        copy.wait()


def body(mesh_count, sub_count, *arguments):
    (
        state, scales, stiffness, jacobians, projection, lifting, flux_matrix,
        peer_send, peer_recv, edge_send, edge_recv, uplift_map,
        fault_elem, fault_dest, fault_row, fault_slip, sea_level, velocity, depth,
    ) = arguments
    basis, quantities, elements = state.shape
    width = basis * quantities
    faults = fault_elem.shape[0]
    rows, cols = sea_level.shape
    slots, edge_slots = peer_send.shape[2], edge_send.shape[2]
    operands = (
        jnp.transpose(state, (1, 0, 2)).reshape(width, elements),
        scales.reshape(1, elements),
        stiffness.reshape(3 * basis, basis),
        jnp.transpose(jacobians, (1, 0, 2)),
        jnp.transpose(projection, (1, 0, 2)),
        jnp.transpose(lifting, (2, 0, 1)),
        flux_matrix,
        peer_send.reshape(sub_count, slots),
        peer_recv.reshape(sub_count, slots),
        edge_send.reshape(2, edge_slots),
        edge_recv.reshape(2, edge_slots),
        uplift_map,
        fault_elem.reshape(1, faults),
        fault_dest.reshape(1, faults),
        fault_row.reshape(1, faults),
        fault_slip.reshape(1, faults),
        sea_level,
        velocity,
        depth,
    )
    padded = -(-width // LANES) * LANES
    trace_lanes = 2 * LANES
    send_total = sub_count * slots + 2 * edge_slots
    item_slots = sub_count * CAP
    vmem, dma = pltpu.VMEM, pltpu.SemaphoreType.DMA
    held = [vmem(x.shape, x.dtype) for x in operands]
    scratch = held + [
        vmem((3 * basis, padded), F32),
        vmem((padded, padded), BF16),
        vmem((padded, padded), BF16),
        vmem((2 * send_total, 4 * elements), BF16),
        vmem((4 * FACE_ROWS, LANES), F32),
        vmem((4 * FACE_ROWS, basis), F32),
        vmem((send_total, trace_lanes), F32),
        vmem((send_total, trace_lanes), F32),
        vmem((item_slots, cols), F32),
        vmem((item_slots, cols), F32),
        vmem((2, 4, 8, cols), F32),
        vmem((2, 8, LANES), F32),
        vmem((2, 4, 8, cols), F32),
        vmem((2, 8, LANES), F32),
        vmem((4, 4, 8, LANES), F32),
        vmem((2, sub_count, RIM, cols), F32),
        vmem((2, sub_count, RIM, cols), F32),
        vmem((sub_count, 1, LANES), F32),
        vmem((sub_count, 1, LANES), F32),
        dma((len(operands),)),
        dma((8,)),
        dma((8,)),
        dma((sub_count + 2,)),
        dma((sub_count + 2,)),
        dma((sub_count,)),
        dma((sub_count,)),
        dma((sub_count,)),
        dma((sub_count,)),
        dma((2, sub_count)),
        dma((2, sub_count)),
    ]
    hbm, local = pl.BlockSpec(memory_space=pltpu.HBM), pl.BlockSpec(memory_space=pltpu.VMEM)
    shapes = ((width, elements), (rows, cols), (2, rows, cols))
    results = pl.pallas_call(
        functools.partial(kernel, mesh_count, sub_count),
        out_shape=tuple(vmem(shape, F32) for shape in shapes),
        in_specs=[hbm] * len(operands),
        out_specs=(local,) * 3,
        scratch_shapes=scratch,
        compiler_params=pltpu.CompilerParams(
            collective_id=0, has_side_effects=True, vmem_limit_bytes=40 * 1024 * 1024
        ),
    )(*[pltpu.with_memory_space_constraint(x, pltpu.HBM) for x in operands])
    new_state, sea_out, flow_out = pl.pallas_call(
        store_kernel,
        out_shape=tuple(pltpu.HBM(shape, F32) for shape in shapes),
        in_specs=[local] * 3,
        out_specs=(hbm,) * 3,
        scratch_shapes=[dma((3,))],
    )(*[pltpu.with_memory_space_constraint(x, pltpu.VMEM) for x in results])
    new_state = jnp.transpose(new_state.reshape(quantities, basis, elements), (1, 0, 2))
    return new_state, sea_out, flow_out


def solution(mesh):
    device = P(("mesh", "sub"))
    return jax.shard_map(
        functools.partial(body, mesh.shape["mesh"], mesh.shape["sub"]),
        mesh=mesh,
        in_specs=(
            P(None, None, ("mesh", "sub")),
            device,
            P(),
            P(),
            P(),
            P(),
            P(),
            P(("mesh", "sub"), None, None),
            P(("mesh", "sub"), None, None),
            P(("mesh", "sub"), None, None),
            P(("mesh", "sub"), None, None),
            P(),
            device,
            P(("mesh", "sub"), None),
            device,
            device,
            P("mesh", "sub"),
            P(None, "mesh", "sub"),
            P("mesh", "sub"),
        ),
        out_specs=(P(None, None, ("mesh", "sub")), P("mesh", "sub"), P(None, "mesh", "sub")),
        check_vma=False,
    )
```

```python
import functools

import jax
import jax.numpy as jnp
from jax import lax
from jax.experimental import pallas as pl
from jax.experimental.pallas import tpu as pltpu
from jax.sharding import PartitionSpec as P

ORDER = 5
CAP = 16
EARTH_STEP = 0.5
COURANT = 0.45
MESH = pl.DeviceIdType.MESH
F32, BF16, I32 = jnp.float32, jnp.bfloat16, jnp.int32
LANES = 128
FACE_ROWS = 24
INFO = 224
RIM = 4
TRACES, FIELDS, RIMS, ITEMS, SIDES = range(5)
TURN_LOW, TURN_HIGH = 1, 2
DIRECTIONS = ((1, 0), (-1, 0), (0, 1), (0, -1), (1, 1), (1, -1), (-1, 1), (-1, -1))
WAY = {d: i for i, d in enumerate(DIRECTIONS)}


def split(x):
    high = x.astype(BF16)
    return high, (x - high.astype(F32)).astype(BF16)


def mm(a, b, left=1, right=0):
    return lax.dot_general(a, b, (((left,), (right,)), ((), ())), preferred_element_type=F32)


def iota(shape, axis):
    return lax.broadcasted_iota(I32, shape, axis)


def repeat_rows(rows, count):
    return jnp.concatenate(
        [jnp.broadcast_to(rows[i : i + 1], (count, rows.shape[1])) for i in range(rows.shape[0])], 0
    )


def as_column(rows, first=0, backward=False):
    count = rows.shape[1] if first == 0 else CAP
    wide = repeat_rows(rows, count)
    turn = iota(wide.shape, 0) & (count - 1)
    mine = (count - 1 - turn if backward else turn) == iota(wide.shape, 1) - first
    return jnp.sum(jnp.where(mine, wide, 0.0), axis=1, keepdims=True)


def pack_edge(array, last, base):
    lane = iota((8, LANES), 1)
    start = array.shape[1] - LANES if last else 0
    keep = lane >= LANES - RIM if last else lane < RIM
    packed = jnp.zeros((8, LANES), F32)
    for g in range(array.shape[0] // 8):
        tile = jnp.where(keep, array[8 * g : 8 * g + 8, start : start + LANES], 0.0)
        packed = packed + pltpu.roll(tile, (RIM * (g + 1 if last else g) + base) % LANES, 1)
    return packed


def extend(array, low, high, left, right, corners, base):
    lane, row = iota((8, LANES), 1), iota((8, LANES), 0)
    side = jnp.concatenate(
        [
            jnp.where(
                lane < LANES // 2,
                pltpu.roll(right, (-RIM * g - base) % LANES, 1),
                pltpu.roll(left, (LANES - RIM - RIM * g - base) % LANES, 1),
            )
            for g in range(array.shape[0] // 8)
        ],
        0,
    )
    down_right, down_left, up_right, up_left = corners
    corner = jnp.where(
        row < RIM,
        jnp.where(lane < LANES // 2, down_right, down_left),
        jnp.where(lane < LANES // 2, up_right, up_left),
    )
    bottom = jnp.where(iota(low.shape, 0) < RIM, high, low)
    return jnp.concatenate(
        [jnp.concatenate([array, side], 1), jnp.concatenate([bottom, corner], 1)], 0
    )


def shifted(array, axis):
    size = array.shape[axis]
    return (pltpu.roll(array, size - 1, axis) - pltpu.roll(array, 1, axis)) * 0.5


def kernel(mesh_count, sub_count, *refs):
    (
        state_in, scales_in, stiff_in, jac_in, proj_in, lift_in, flux_in,
        psend_in, precv_in, esend_in, erecv_in, uplift_in,
        felem_in, fdest_in, frow_in, fslip_in, sea_in, vel_in, depth_in,
        new_out, sea_out, flow_out,
        state, scales, stiff, jac, proj, lift, flux,
        psend, precv, esend, erecv, uplift,
        felem, fdest, frow, fslip, sea, vel, depth,
        spread, matrix_hi, matrix_lo, hot, faces, lifts, traces_out, traces_in, items_out, items_in,
        rows_out, cols_out, rows_in, cols_in, corner_in,
        rims_out, rims_in, sides_out, sides_in,
        known, mixing_hi, mixing_lo, load_sem, recv_sem,
    ) = refs
    quantities, basis = flux.shape[0], stiff.shape[1]
    width = quantities * basis
    padded = matrix_hi.shape[0]
    elements = state.shape[1]
    slots = psend.shape[1]
    edge_slots = esend.shape[1]
    peer_total = sub_count * slots
    send_total = peer_total + 2 * edge_slots
    tile_rows, tile_cols = depth.shape
    me, sub = lax.axis_index("mesh"), lax.axis_index("sub")
    neighbour = {1: me < mesh_count - 1, -1: me > 0}

    def device(dm, ds):
        return (me + dm, lax.rem(sub + ds + sub_count, sub_count))

    loads = [
        pltpu.make_async_copy(src, dst, load_sem.at[i])
        for i, (src, dst) in enumerate(
            (
                (stiff_in, stiff), (jac_in, jac), (state_in, state), (scales_in, scales),
                (psend_in, psend), (precv_in, precv), (esend_in, esend), (erecv_in, erecv),
                (proj_in, proj), (felem_in, felem), (fdest_in, fdest), (frow_in, frow),
                (fslip_in, fslip), (flux_in, flux), (lift_in, lift),
                (vel_in, vel), (depth_in, depth), (uplift_in, uplift), (sea_in, sea),
            )
        )
    ]
    for load in loads:
        load.start()
    barrier = pltpu.get_barrier_semaphore()

    def greet(dm, ds):
        pl.semaphore_signal(barrier, inc=1, device_id=device(dm, ds), device_id_type=MESH)

    for k in range(1, sub_count):
        greet(0, k)
    for side in (1, -1):

        @pl.when(neighbour[side])
        def _():
            for ds in range(sub_count):
                greet(side, ds)

    def start(group, copies):
        for side in (0, 1, -1):
            some = [copy for copy in copies if copy[0] == side]

            def go():
                for dm, ds, src, dst in some:
                    pltpu.make_async_remote_copy(
                        src_ref=src, dst_ref=dst,
                        send_sem=load_sem.at[3 * group + side % 3],
                        recv_sem=recv_sem.at[3 * group + side % 3],
                        device_id=device(dm, ds), device_id_type=MESH,
                    ).start()

            if side == 0:
                go()
            elif some:
                pl.when(neighbour[side])(go)

    def await_all(sem, whole):
        pltpu.make_async_copy(whole, whole, sem).wait()

    def sent(group, along, across):
        if along is not None:
            await_all(load_sem.at[3 * group], along)
        for side in (1, -1):
            if across is not None:
                pl.when(neighbour[side])(
                    functools.partial(await_all, load_sem.at[3 * group + side % 3], across)
                )

    def received(group, along, across):
        if along is not None:
            await_all(recv_sem.at[3 * group], along)
        for side in (1, -1):
            if across is not None:
                pl.when(neighbour[-side])(
                    functools.partial(await_all, recv_sem.at[3 * group + side % 3], across)
                )

    def keep_own(group, src, dst):
        pltpu.make_async_copy(src, dst, recv_sem.at[3 * group]).start()

    lane = iota((1, padded), 1)
    of_quantity = sum((lane >= basis * k).astype(I32) for k in range(1, quantities + 1))
    of_basis = lane - basis * of_quantity
    spread_basis = (iota((basis, padded), 0) == of_basis).astype(F32).astype(BF16)
    spread_quantity = (iota((quantities, padded), 0) == of_quantity).astype(F32)
    for load in loads[0:15]:
        load.wait()
    stiff_hi, stiff_lo = split(stiff[...])
    spread[...] = mm(stiff_hi, spread_basis) + mm(stiff_lo, spread_basis)
    jac_wide = [
        lax.dot_general(
            jac[:, d, :], spread_quantity, (((0,), (0,)), ((), ())),
            precision=lax.Precision.HIGHEST, preferred_element_type=F32,
        )
        for d in range(3)
    ]

    def matrix_rows(q):
        if q == quantities:
            return jnp.zeros((padded - width, padded), F32)
        block = spread[0:basis, :] * jac_wide[0][q : q + 1]
        for d in (1, 2):
            block = block + spread[d * basis : (d + 1) * basis, :] * jac_wide[d][q : q + 1]
        return block

    at = 0
    for q in range(0, quantities, 2):
        high, low = split(jnp.concatenate([matrix_rows(q), matrix_rows(q + 1)], 0))
        matrix_hi[at : at + high.shape[0], :] = high
        matrix_lo[at : at + high.shape[0], :] = low
        at = at + high.shape[0]

    scale = scales[...]

    def derivative(x):
        x_hi, x_lo = split(x)
        both = mm(matrix_hi[...], jnp.concatenate([x_hi, x_lo], 1))
        return (both[:, :elements] + both[:, elements:] + mm(matrix_lo[...], x_hi)) * scale

    start_state = jnp.concatenate([state[...], jnp.zeros((padded - width, elements), F32)], 0)
    current = derivative(start_state)
    factor = EARTH_STEP * EARTH_STEP / 2
    integral = EARTH_STEP * start_state + factor * current

    codes = jnp.concatenate(
        [as_column(ref[...].astype(F32)) for ref in (psend, esend, precv, erecv)], 0
    )
    face_lane = iota((1, 4 * elements), 1)
    key = (4 * (face_lane & (elements - 1)) + face_lane // elements).astype(F32)
    hot[...] = (codes == key).astype(F32).astype(BF16)
    faces[...] = jnp.zeros(faces.shape, F32)
    for f in range(4):
        for half in (0, LANES // 2):
            faces[f * FACE_ROWS : f * FACE_ROWS + proj.shape[0], half : half + basis] = proj[:, f, :]
    faces_hi, faces_lo = split(faces[...])
    faces_lo = faces_lo[:, 0 : LANES // 2]

    fault_count = fdest.shape[1]
    square = (fault_count, fault_count)
    dest_row = fdest[...].astype(F32)
    dest_col = as_column(dest_row)
    same = dest_col == dest_row
    rank_row = jnp.sum(
        jnp.where(same & (iota(square, 0) < iota(square, 1)), 1.0, 0.0), axis=0, keepdims=True
    )
    rank_col = jnp.sum(
        jnp.where(same & (iota(square, 1) < iota(square, 0)), 1.0, 0.0), axis=1, keepdims=True
    )
    row_numbers = frow[...].astype(F32) + 1.0
    info_row = iota((peer_total, 1), 0)
    info_turn = info_row & (slots - 1)
    info_dest = info_row // slots + jnp.where(
        info_turn == TURN_LOW, -1, jnp.where(info_turn == TURN_HIGH, 1, 0)
    )
    info_left = jnp.where(dest_row == info_dest.astype(F32), row_numbers, 0.0)
    info_lane = INFO % LANES
    info_right = (
        rank_col == (iota((fault_count, LANES), 1) - info_lane).astype(F32)
    ).astype(F32)
    info = mm(info_left.astype(BF16), info_right.astype(BF16)) - 1.0
    info_lanes = iota((peer_total, LANES), 1)
    info_here = (info_lanes >= info_lane) & (info_lanes < info_lane + CAP)

    for power in range(2, ORDER):
        current = derivative(current)
        factor = factor * EARTH_STEP / (power + 1)
        integral = integral + factor * current

    parts = jnp.concatenate(
        [
            jnp.concatenate(
                [
                    integral[p * basis : (p + 1) * basis],
                    jnp.zeros((LANES // 2 - basis, elements), F32),
                ],
                0,
            )
            for p in range(quantities)
        ],
        1,
    )
    parts_hi, parts_lo = split(parts)
    every = mm(faces_hi, jnp.concatenate([parts_hi, parts_lo], 0)) + mm(faces_lo, parts_hi)
    face_width = quantities * FACE_ROWS
    trace_rows = traces_out.shape[1]

    def face_block(f, q):
        return every[f * FACE_ROWS : (f + 1) * FACE_ROWS, q * elements : (q + 1) * elements]

    table = jnp.concatenate(
        [jnp.concatenate([face_block(f, q) for q in range(quantities)], 0) for f in range(4)], 1
    )
    table = jnp.concatenate([table, jnp.zeros((trace_rows - face_width, 4 * elements), F32)], 0)
    table_hi, table_lo = split(table)
    picked = mm(hot[...], table_hi, 1, 1) + mm(hot[...], table_lo, 1, 1)
    traces_out[:, 0:LANES] = picked[0:send_total, 0:LANES]
    traces_out[0:peer_total, LANES:] = jnp.where(
        info_here, info, picked[0:peer_total, LANES:]
    )
    traces_out[peer_total:, LANES:] = picked[peer_total:send_total, LANES:]
    own_trace = picked[send_total:]

    def peer_block(index, rows):
        return pl.ds(pl.multiple_of(index * rows, rows), rows)

    order = sorted(range(1, sub_count), key=lambda k: -min(k, sub_count - k))
    trace_copies = []
    for k in order:
        _, peer = device(0, k)
        trace_copies.append(
            (
                0, k,
                traces_out.at[peer_block(peer, slots), :], traces_in.at[peer_block(sub, slots), :],
            )
        )
    for dm in (1, -1):
        source = peer_total + (edge_slots if dm > 0 else 0)
        target = peer_total + (0 if dm > 0 else edge_slots)
        trace_copies.append(
            (
                dm, 0,
                traces_out.at[source : source + edge_slots, :],
                traces_in.at[target : target + edge_slots, :],
            )
        )
    pl.semaphore_wait(
        barrier,
        sub_count - 1 + sub_count * (neighbour[1].astype(I32) + neighbour[-1].astype(I32)),
    )
    start(TRACES, trace_copies)
    keep_own(
        TRACES, traces_out.at[peer_block(sub, slots), :], traces_in.at[peer_block(sub, slots), :]
    )

    for load in loads[15:]:
        load.wait()
    for i, first in enumerate((tile_rows - 8, 0)):
        rows_out[i, 0:2] = vel[:, first : first + 8, :]
        rows_out[i, 2] = depth[first : first + 8, :]
        rows_out[i, 3] = sea[first : first + 8, :]
    fields = (vel[0], vel[1], depth[...], sea[...])
    group = RIM * (tile_rows // 8)
    for i, last in enumerate((True, False)):
        packed = pack_edge(fields[0], last, 0)
        for k in (1, 2, 3):
            packed = packed + pack_edge(fields[k], last, k * group)
        cols_out[i] = packed

    rim_copies = []
    for i, (dm, ds) in enumerate(DIRECTIONS):
        if ds == 0:
            src, dst = rows_out.at[i], rows_in.at[i]
        elif dm == 0:
            src, dst = cols_out.at[i - 2], cols_in.at[i - 2]
        else:
            lanes = slice(tile_cols - LANES, tile_cols) if ds > 0 else slice(0, LANES)
            src, dst = rows_out.at[0 if dm > 0 else 1, :, :, lanes], corner_in.at[i - 4]
        rim_copies.append((dm, ds, src, dst))
    start(FIELDS, rim_copies)

    base = start_state + derivative(integral)
    lifts[...] = jnp.zeros(lifts.shape, F32)
    for f in range(4):
        for at in (0, LANES // 2):
            lifts[f * FACE_ROWS : f * FACE_ROWS + lift.shape[0], at : at + basis] = lift[:, f, :]
    lift_hi, lift_lo = split(jnp.transpose(lifts[...])[0:basis])
    lift_hi = jnp.concatenate([lift_hi, lift_hi], 1)
    hot_in = hot[send_total:, :]

    face_col, face_row = iota((trace_rows, 1), 0), iota((1, trace_rows), 1)
    quantity_col = sum((face_col >= FACE_ROWS * k).astype(I32) for k in range(1, quantities + 1))
    quantity_row = sum((face_row >= FACE_ROWS * k).astype(I32) for k in range(1, quantities + 1))
    exact = functools.partial(
        lax.dot_general, precision=lax.Precision.HIGHEST, preferred_element_type=F32
    )
    flux_left = exact(
        (quantity_col == iota((trace_rows, quantities), 1)).astype(F32), flux[...],
        (((1,), (1,)), ((), ())),
    )
    flux_wide = exact(
        flux_left, (quantity_row == iota((quantities, trace_rows), 0)).astype(F32),
        (((1,), (0,)), ((), ())),
    )
    same_face = face_col - FACE_ROWS * quantity_col == face_row - FACE_ROWS * quantity_row
    flux_wide = jnp.where(same_face, flux_wide, 0.0)
    flux_hi, flux_lo = split(flux_wide)

    rows_here = iota((padded, 1), 0)
    row_quantity = sum((rows_here >= basis * k).astype(I32) for k in range(1, quantities + 1))
    wanted = (rows_here - basis * row_quantity) * quantities + row_quantity
    wanted = jnp.where(rows_here < width, wanted, -1)
    permute = (iota((padded, width), 1) == wanted).astype(F32).astype(BF16)
    uplift_hi, uplift_lo = split(uplift[...])
    uplift_hi, uplift_lo = mm(permute, uplift_hi), mm(permute, uplift_lo)
    uplift_all = uplift_hi + uplift_lo
    uplift_hi, uplift_lo = uplift_hi.astype(BF16), uplift_lo.astype(BF16)

    wide_hi, wide_lo = split(
        jnp.concatenate(
            [
                jnp.concatenate(
                    [
                        uplift_all[q * basis : (q + 1) * basis],
                        jnp.zeros((LANES // 2 - basis, tile_cols), F32),
                    ],
                    0,
                )
                for q in range(quantities)
            ],
            1,
        )
    )
    down_hi, down_lo = split(lifts[...])
    faces_up = mm(down_hi, jnp.concatenate([wide_hi, wide_lo], 0))
    faces_up = faces_up + mm(down_lo[:, 0 : LANES // 2], wide_hi)
    back_hi, back_lo = split(jnp.transpose(flux_wide))
    for f in range(4):
        rows = [
            faces_up[f * FACE_ROWS : (f + 1) * FACE_ROWS, q * tile_cols : (q + 1) * tile_cols]
            for q in range(quantities)
        ]
        rows.append(jnp.zeros((trace_rows - face_width, tile_cols), F32))
        rows_hi, rows_lo = split(jnp.concatenate(rows, 0))
        block = mm(back_hi, rows_hi) + mm(back_lo, rows_hi) + mm(back_hi, rows_lo)
        high, low = split(block)
        mixing_hi[f * trace_rows : (f + 1) * trace_rows, :] = high
        mixing_lo[f * trace_rows : (f + 1) * trace_rows, :] = low

    item_slots = sub_count * CAP
    place = (
        iota((item_slots, fault_count), 0).astype(F32) == dest_row * float(CAP) + rank_row
    ).astype(F32)
    elem_col = as_column(felem[...].astype(F32))
    elem_hot = (elem_col == iota((fault_count, elements), 1).astype(F32)).astype(F32)
    elem_hot = elem_hot.astype(BF16)
    choose = mm(place.astype(BF16), elem_hot).astype(BF16)
    weighting = 0.3 + 0.7 * fslip[...].astype(F32)
    weight_col = jnp.sum(place * weighting, axis=1, keepdims=True)
    rim_total = 2 * sub_count * RIM
    rim_row = iota((rim_total, 1), 0)
    rim_turn = rim_row & (RIM - 1)
    upward = rim_row >= rim_total // 2
    rim_target = jnp.where(
        upward,
        jnp.where(rim_turn > 0, tile_rows - RIM + rim_turn, -1),
        jnp.where(rim_turn < RIM - 1, rim_turn, -1),
    )
    rim_dest = (rim_row & (rim_total // 2 - 1)) // RIM
    rim_weight = jnp.where(
        (dest_row == rim_dest.astype(F32)) & (frow[...] == rim_target), weighting, 0.0
    )
    rim_hi, rim_lo = split(rim_weight)
    rim_hi, rim_lo = split(mm(rim_hi, elem_hot) + mm(rim_lo, elem_hot))

    base_hi, base_lo = split(base)
    both = jnp.concatenate([choose, rim_hi], 0)
    columns = mm(jnp.concatenate([both, both], 1), jnp.concatenate([base_hi, base_lo], 1), 1, 1)
    columns = jnp.concatenate(
        [columns[:item_slots], columns[item_slots:] + mm(rim_lo, base_hi, 1, 1)], 0
    )
    columns_hi, columns_lo = split(columns)
    known[...] = mm(columns_hi, uplift_hi) + mm(columns_lo, uplift_hi) + mm(columns_hi, uplift_lo)
    in_codes = codes[send_total:].astype(I32)
    in_elem = jnp.where(in_codes >= 0, in_codes >> 2, -1)
    in_hot = (in_elem == iota((send_total, elements), 1)).astype(F32).astype(BF16)
    touch = mm(choose, in_hot, 1, 1).astype(BF16)
    touch_hi, touch_lo = split(mm(rim_hi, in_hot, 1, 1) + mm(rim_lo, in_hot, 1, 1))
    touch = jnp.concatenate([touch, touch_hi], 0)
    touch = jnp.concatenate([touch, touch], 1)
    turns = [
        jnp.broadcast_to(((in_codes >= 0) & ((in_codes & 3) == f)).astype(F32), own_trace.shape)
        .astype(BF16)
        for f in range(4)
    ]

    received(TRACES, traces_in.at[0:peer_total, :], traces_in.at[0:edge_slots, :])
    slot_col = iota((send_total, 1), 0)
    missing = ((slot_col >= peer_total) & (slot_col < peer_total + edge_slots) & (me == 0)) | (
        (slot_col >= peer_total + edge_slots) & (me == mesh_count - 1)
    )
    difference = jnp.where(missing, 0.0, traces_in[...]) - own_trace
    diff_hi, diff_lo = split(difference)
    turned_hi = jnp.concatenate([diff_hi * turn for turn in turns], 1)
    turned_lo = jnp.concatenate([diff_lo * turn for turn in turns], 1)
    each_hi, each_lo = split(
        mm(turned_hi, mixing_hi[...]) + mm(turned_lo, mixing_hi[...]) + mm(turned_hi, mixing_lo[...])
    )
    uplifted = known[...] + mm(touch, jnp.concatenate([each_hi, each_lo], 0))
    uplifted = jnp.concatenate(
        [uplifted[:item_slots], uplifted[item_slots:] + mm(touch_lo, each_hi)], 0
    )
    rims = uplifted[item_slots:]
    half = rim_total // 2
    rim_lane = iota((half, LANES), 1)
    for i, (part, high_shift, low_shift) in enumerate(
        ((rims[:half], -RIM, RIM), (rims[half:], 1 - 2 * RIM, 1))
    ):
        corner = []
        for shift, tile in (
            (high_shift, jnp.where(rim_lane < RIM - 1, part[:, 0:LANES], 0.0)),
            (low_shift, jnp.where(rim_lane > LANES - RIM, part[:, tile_cols - LANES :], 0.0)),
        ):
            tile = pltpu.roll(tile, 0, 1, stride=8, stride_axis=0)
            tile = tile + pltpu.roll(tile, 1, 0)
            tile = tile + pltpu.roll(tile, 2, 0)
            corner.append(pltpu.roll(tile, shift % half, 0))
        free = (iota((half, LANES), 0) & (RIM - 1)) == (0 if i else RIM - 1)
        first = jnp.where(free, corner[0] + corner[1], part[:, 0:LANES])
        for d in range(sub_count):
            rims_out[i, d, :, 0:LANES] = first[d * RIM : (d + 1) * RIM]
            rims_out[i, d, :, LANES:] = part[d * RIM : (d + 1) * RIM, LANES:]

    rim_copies = []
    for k in [*order, 0]:
        _, peer = device(0, k)
        for i, dm in enumerate((-1, 1)):
            rim_copies.append((dm, k, rims_out.at[i, peer], rims_in.at[i, sub]))
    start(RIMS, rim_copies)
    items = uplifted[:item_slots] * weight_col
    items_out[...] = items
    start(
        ITEMS,
        [
            (
                0, k,
                items_out.at[peer_block(device(0, k)[1], CAP), :],
                items_in.at[peer_block(sub, CAP), :],
            )
            for k in order
        ],
    )
    keep_own(ITEMS, items_out.at[peer_block(sub, CAP), :], items_in.at[peer_block(sub, CAP), :])
    side_lane = iota((CAP, LANES), 1)
    firsts, lasts = [], []
    for d in range(sub_count):
        own = items[d * CAP : (d + 1) * CAP]
        first = jnp.where(side_lane < RIM - 1, own[:, 0:LANES], 0.0)
        last = jnp.where(side_lane > LANES - RIM, own[:, tile_cols - LANES :], 0.0)
        first = pltpu.roll(first, 0, 1, stride=RIM, stride_axis=0)
        last = pltpu.roll(last, LANES // 2 + RIM - 1, 1, stride=RIM, stride_axis=0)
        firsts.append(jnp.sum(first, axis=0, keepdims=True))
        lasts.append(jnp.sum(last, axis=0, keepdims=True))
    for d in range(sub_count):
        sides_out[d] = firsts[(d + 1) % sub_count] + lasts[(d - 1) % sub_count]
    start(
        SIDES, [(0, k, sides_out.at[device(0, k)[1]], sides_in.at[sub]) for k in order]
    )
    keep_own(SIDES, sides_out.at[sub], sides_in.at[sub])

    mixed = mm(flux_hi, jnp.concatenate([diff_hi, diff_lo], 0), 1, 1)
    mixed = mixed[:, :send_total] + mixed[:, send_total:] + mm(flux_lo, diff_hi, 1, 1)
    scattered = mm(jnp.concatenate(split(mixed), 1), jnp.concatenate([hot_in, hot_in], 0))
    gathered = jnp.concatenate(
        [
            jnp.concatenate(
                [
                    scattered[q * FACE_ROWS : (q + 1) * FACE_ROWS, f * elements : (f + 1) * elements]
                    for f in range(4)
                ],
                0,
            )
            for q in range(quantities)
        ],
        1,
    )
    gathered_hi, gathered_lo = split(gathered)
    lifted = mm(lift_hi, jnp.concatenate([gathered_hi, gathered_lo], 0)) + mm(lift_lo, gathered_hi)
    face_sum = jnp.concatenate(
        [lifted[:, q * elements : (q + 1) * elements] for q in range(quantities)]
        + [jnp.zeros((padded - width, elements), F32)],
        0,
    )
    new_out[...] = (base + face_sum)[0:width]

    got_info = traces_in[0:peer_total, LANES:]

    def landing(turn, backward=False):
        rows = jnp.concatenate(
            [got_info[s * slots + turn : s * slots + turn + 1] for s in range(sub_count)], 0
        )
        column = as_column(rows, info_lane, backward)
        hits = (column == iota((item_slots, LANES), 1).astype(F32)).astype(F32)
        return jnp.transpose(hits)[0:tile_rows].astype(BF16)

    land = landing(0)
    land = jnp.concatenate([land, land], 1)
    land_high, land_low = landing(TURN_HIGH, True), landing(TURN_LOW, True)
    land_side = jnp.concatenate([land_high, land_low, land_high, land_low], 1)

    received(FIELDS, cols_in, rows_in)

    def corners_of(k):
        return [
            corner_in[WAY[way] - 4, k] for way in ((-1, -1), (-1, 1), (1, -1), (1, 1))
        ]

    extended = [
        extend(
            fields[k], rows_in[WAY[(1, 0)], k], rows_in[WAY[(-1, 0)], k],
            cols_in[0], cols_in[1], corners_of(k), k * group,
        )
        for k in range(4)
    ]
    shape = extended[0].shape
    ext_row, ext_lane = iota(shape, 0), iota(shape, 1)
    inside = (
        ((ext_row < tile_rows) | (ext_row >= tile_rows + RIM) | neighbour[1])
        & ((ext_row < tile_rows + RIM) | neighbour[-1])
        & ((ext_lane < tile_cols) | (ext_lane >= tile_cols + LANES // 2) | (sub < sub_count - 1))
        & ((ext_lane < tile_cols + LANES // 2) | (sub > 0))
    )
    flow = [jnp.where(inside, extended[axis], 0.0) for axis in (0, 1)]
    deep = jnp.where(inside, extended[2], 0.0)
    calm = jnp.where(inside, extended[3], 0.0) - COURANT * (
        shifted(deep * flow[0], 0) + shifted(deep * flow[1], 1)
    )
    sent(TRACES, traces_out.at[0 : peer_total - slots, :], traces_out.at[0:edge_slots, :])
    sent(FIELDS, cols_out, rows_out)

    received(SIDES, sides_in, None)
    beside = []
    last_turn = LANES - RIM * (CAP - 1)
    for shift, keep in (
        (last_turn, side_lane < RIM - 1),
        (last_turn + LANES // 2 - RIM + 1, side_lane > LANES - RIM),
    ):
        for s in range(sub_count):
            wide = jnp.broadcast_to(sides_in[s], (CAP, LANES))
            wide = pltpu.roll(wide, shift % LANES, 1, stride=RIM, stride_axis=0)
            beside.append(jnp.where(keep, wide, 0.0))
    beside_hi, beside_lo = split(jnp.concatenate(beside, 0))
    side = mm(land_side, jnp.concatenate([beside_hi, beside_lo], 0))

    received(ITEMS, items_in, None)
    received(RIMS, None, rims_in.at[0])
    deposit = mm(land, jnp.concatenate(split(items_in[...]), 0))
    bottom = []
    for i in (0, 1):
        total = rims_in[i, 0]
        for s in range(1, sub_count):
            total = total + rims_in[i, s]
        bottom.append(total)
    bottom = jnp.concatenate(bottom, 0)
    bottom_lane, bottom_row = iota((8, LANES), 1), iota((8, LANES), 0)
    corner = []
    for free in (RIM - 1, RIM):
        wide = jnp.broadcast_to(bottom[free : free + 1, 0:LANES], (8, LANES))
        around = []
        for turn in (1, -1):
            tile = pltpu.roll(wide, lax.rem(8 * LANES - 8 * RIM * (sub + turn), LANES), 1)
            rows = tile
            for r in range(1, RIM):
                rows = jnp.where(
                    (bottom_row & (RIM - 1)) == r, pltpu.roll(tile, LANES - 8 * r, 1), rows
                )
            around.append(rows)
        corner.append(jnp.where(bottom_lane < LANES // 2, around[0], around[1]))
    corner = jnp.where(bottom_row < RIM, corner[0], corner[1])
    raised = jnp.concatenate(
        [jnp.concatenate([deposit, side], 1), jnp.concatenate([bottom, corner], 1)], 0
    )

    level = calm + jnp.where(inside, raised, 0.0)
    flow = [flow[axis] - COURANT * shifted(level, axis) for axis in (0, 1)]
    level = jnp.where(inside, level, 0.0)
    level = level - COURANT * (shifted(deep * flow[0], 0) + shifted(deep * flow[1], 1))
    flow = [flow[axis] - COURANT * shifted(level, axis) for axis in (0, 1)]
    sea_out[...] = level[0:tile_rows, 0:tile_cols]
    flow_out[0] = flow[0][0:tile_rows, 0:tile_cols]
    flow_out[1] = flow[1][0:tile_rows, 0:tile_cols]
    sent(RIMS, None, rims_out.at[0])
    sent(ITEMS, items_out.at[0 : item_slots - CAP, :], None)
    sent(SIDES, sides_out.at[0 : sub_count - 1], None)


def store_kernel(new_in, sea_in, flow_in, new_out, sea_out, flow_out, sems):
    copies = [
        pltpu.make_async_copy(src, dst, sems.at[i])
        for i, (src, dst) in enumerate(
            ((new_in, new_out), (sea_in, sea_out), (flow_in, flow_out))
        )
    ]
    for copy in copies:
        copy.start()
    for copy in copies:
        copy.wait()


def body(mesh_count, sub_count, *arguments):
    (
        state, scales, stiffness, jacobians, projection, lifting, flux_matrix,
        peer_send, peer_recv, edge_send, edge_recv, uplift_map,
        fault_elem, fault_dest, fault_row, fault_slip, sea_level, velocity, depth,
    ) = arguments
    basis, quantities, elements = state.shape
    width = basis * quantities
    faults = fault_elem.shape[0]
    rows, cols = sea_level.shape
    slots, edge_slots = peer_send.shape[2], edge_send.shape[2]
    operands = (
        jnp.transpose(state, (1, 0, 2)).reshape(width, elements),
        scales.reshape(1, elements),
        stiffness.reshape(3 * basis, basis),
        jnp.transpose(jacobians, (1, 0, 2)),
        jnp.transpose(projection, (1, 0, 2)),
        jnp.transpose(lifting, (2, 0, 1)),
        flux_matrix,
        peer_send.reshape(sub_count, slots),
        peer_recv.reshape(sub_count, slots),
        edge_send.reshape(2, edge_slots),
        edge_recv.reshape(2, edge_slots),
        uplift_map,
        fault_elem.reshape(1, faults),
        fault_dest.reshape(1, faults),
        fault_row.reshape(1, faults),
        fault_slip.reshape(1, faults),
        sea_level,
        velocity,
        depth,
    )
    padded = -(-width // LANES) * LANES
    trace_lanes = 2 * LANES
    send_total = sub_count * slots + 2 * edge_slots
    item_slots = sub_count * CAP
    vmem, dma = pltpu.VMEM, pltpu.SemaphoreType.DMA
    held = [vmem(x.shape, x.dtype) for x in operands]
    scratch = held + [
        vmem((3 * basis, padded), F32),
        vmem((padded, padded), BF16),
        vmem((padded, padded), BF16),
        vmem((2 * send_total, 4 * elements), BF16),
        vmem((4 * FACE_ROWS, LANES), F32),
        vmem((4 * FACE_ROWS, LANES), F32),
        vmem((send_total, trace_lanes), F32),
        vmem((send_total, trace_lanes), F32),
        vmem((item_slots, cols), F32),
        vmem((item_slots, cols), F32),
        vmem((2, 4, 8, cols), F32),
        vmem((2, 8, LANES), F32),
        vmem((2, 4, 8, cols), F32),
        vmem((2, 8, LANES), F32),
        vmem((4, 4, 8, LANES), F32),
        vmem((2, sub_count, RIM, cols), F32),
        vmem((2, sub_count, RIM, cols), F32),
        vmem((sub_count, 1, LANES), F32),
        vmem((sub_count, 1, LANES), F32),
        vmem((item_slots + 2 * sub_count * RIM, cols), F32),
        vmem((4 * trace_lanes, cols), BF16),
        vmem((4 * trace_lanes, cols), BF16),
        dma((len(operands),)),
        dma((15,)),
    ]
    hbm, local = pl.BlockSpec(memory_space=pltpu.HBM), pl.BlockSpec(memory_space=pltpu.VMEM)
    shapes = ((width, elements), (rows, cols), (2, rows, cols))
    results = pl.pallas_call(
        functools.partial(kernel, mesh_count, sub_count),
        out_shape=tuple(vmem(shape, F32) for shape in shapes),
        in_specs=[hbm] * len(operands),
        out_specs=(local,) * 3,
        scratch_shapes=scratch,
        compiler_params=pltpu.CompilerParams(
            collective_id=0, has_side_effects=True, vmem_limit_bytes=40 * 1024 * 1024
        ),
    )(*[pltpu.with_memory_space_constraint(x, pltpu.HBM) for x in operands])
    new_state, sea_out, flow_out = pl.pallas_call(
        store_kernel,
        out_shape=tuple(pltpu.HBM(shape, F32) for shape in shapes),
        in_specs=[local] * 3,
        out_specs=(hbm,) * 3,
        scratch_shapes=[dma((3,))],
    )(*[pltpu.with_memory_space_constraint(x, pltpu.VMEM) for x in results])
    new_state = jnp.transpose(new_state.reshape(quantities, basis, elements), (1, 0, 2))
    return new_state, sea_out, flow_out


def solution(mesh):
    device = P(("mesh", "sub"))
    return jax.shard_map(
        functools.partial(body, mesh.shape["mesh"], mesh.shape["sub"]),
        mesh=mesh,
        in_specs=(
            P(None, None, ("mesh", "sub")),
            device,
            P(),
            P(),
            P(),
            P(),
            P(),
            P(("mesh", "sub"), None, None),
            P(("mesh", "sub"), None, None),
            P(("mesh", "sub"), None, None),
            P(("mesh", "sub"), None, None),
            P(),
            device,
            P(("mesh", "sub"), None),
            device,
            device,
            P("mesh", "sub"),
            P(None, "mesh", "sub"),
            P("mesh", "sub"),
        ),
        out_specs=(P(None, None, ("mesh", "sub")), P("mesh", "sub"), P(None, "mesh", "sub")),
        check_vma=False,
    )
```

```python
import functools

import jax
import jax.numpy as jnp
from jax import lax
from jax.experimental import pallas as pl
from jax.experimental.pallas import tpu as pltpu
from jax.sharding import PartitionSpec as P

ORDER = 5
CAP = 16
EARTH_STEP = 0.5
COURANT = 0.45
MESH = pl.DeviceIdType.MESH
F32, BF16, I32 = jnp.float32, jnp.bfloat16, jnp.int32
LANES = 128
FACE_ROWS = 24
INFO = 224
RIM = 4
TRACES, FIELDS, RIMS, SIDES = range(4)
ITEMS = RIMS
TURN_LOW, TURN_HIGH = 1, 2
DIRECTIONS = ((1, 0), (-1, 0), (0, 1), (0, -1), (1, 1), (1, -1), (-1, 1), (-1, -1))
WAY = {d: i for i, d in enumerate(DIRECTIONS)}


def split(x):
    high = x.astype(BF16)
    return high, (x - high.astype(F32)).astype(BF16)


def mm(a, b, left=1, right=0):
    return lax.dot_general(a, b, (((left,), (right,)), ((), ())), preferred_element_type=F32)


def iota(shape, axis):
    return lax.broadcasted_iota(I32, shape, axis)


def repeat_rows(rows, count):
    return jnp.concatenate(
        [jnp.broadcast_to(rows[i : i + 1], (count, rows.shape[1])) for i in range(rows.shape[0])], 0
    )


def as_column(rows, first=0, backward=False):
    count = rows.shape[1] if first == 0 else CAP
    wide = repeat_rows(rows, count)
    turn = iota(wide.shape, 0) & (count - 1)
    mine = (count - 1 - turn if backward else turn) == iota(wide.shape, 1) - first
    return jnp.sum(jnp.where(mine, wide, 0.0), axis=1, keepdims=True)


def pack_edge(array, last, base):
    lane = iota((8, LANES), 1)
    start = array.shape[1] - LANES if last else 0
    keep = lane >= LANES - RIM if last else lane < RIM
    packed = jnp.zeros((8, LANES), F32)
    for g in range(array.shape[0] // 8):
        tile = jnp.where(keep, array[8 * g : 8 * g + 8, start : start + LANES], 0.0)
        packed = packed + pltpu.roll(tile, (RIM * (g + 1 if last else g) + base) % LANES, 1)
    return packed


def extend(array, low, high, left, right, corners, base):
    lane, row = iota((8, LANES), 1), iota((8, LANES), 0)
    side = jnp.concatenate(
        [
            jnp.where(
                lane < LANES // 2,
                pltpu.roll(right, (-RIM * g - base) % LANES, 1),
                pltpu.roll(left, (LANES - RIM - RIM * g - base) % LANES, 1),
            )
            for g in range(array.shape[0] // 8)
        ],
        0,
    )
    down_right, down_left, up_right, up_left = corners
    corner = jnp.where(
        row < RIM,
        jnp.where(lane < LANES // 2, down_right, down_left),
        jnp.where(lane < LANES // 2, up_right, up_left),
    )
    bottom = jnp.where(iota(low.shape, 0) < RIM, high, low)
    return jnp.concatenate(
        [jnp.concatenate([array, side], 1), jnp.concatenate([bottom, corner], 1)], 0
    )


def shifted(array, axis):
    size = array.shape[axis]
    return (pltpu.roll(array, size - 1, axis) - pltpu.roll(array, 1, axis)) * 0.5


def kernel(mesh_count, sub_count, *refs):
    (
        state_in, scales_in, stiff_in, jac_in, proj_in, lift_in, flux_in,
        psend_in, precv_in, esend_in, erecv_in, uplift_in,
        felem_in, fdest_in, frow_in, fslip_in, sea_in, vel_in, depth_in,
        new_out, sea_out, flow_out,
        state, scales, stiff, jac, proj, lift, flux,
        psend, precv, esend, erecv, uplift,
        felem, fdest, frow, fslip, sea, vel, depth,
        spread, matrix_hi, matrix_lo, hot, faces, lifts, traces_out, traces_in, items_out, items_in,
        rows_out, cols_out, rows_in, cols_in, corner_in,
        rims_out, rims_in, sides_out, sides_in,
        known, mixing_hi, mixing_lo, load_sem, recv_sem,
    ) = refs
    quantities, basis = flux.shape[0], stiff.shape[1]
    width = quantities * basis
    padded = matrix_hi.shape[0]
    elements = state.shape[1]
    slots = psend.shape[1]
    edge_slots = esend.shape[1]
    peer_total = sub_count * slots
    send_total = peer_total + 2 * edge_slots
    tile_rows, tile_cols = depth.shape
    me, sub = lax.axis_index("mesh"), lax.axis_index("sub")
    neighbour = {1: me < mesh_count - 1, -1: me > 0}

    def device(dm, ds):
        return (me + dm, lax.rem(sub + ds + sub_count, sub_count))

    def loading(first, pairs):
        return [
            pltpu.make_async_copy(src, dst, load_sem.at[first + i])
            for i, (src, dst) in enumerate(pairs)
        ]

    loads = loading(
        0,
        (
            (stiff_in, stiff), (jac_in, jac), (state_in, state), (scales_in, scales),
            (psend_in, psend), (precv_in, precv), (esend_in, esend), (erecv_in, erecv),
            (proj_in, proj), (fdest_in, fdest), (frow_in, frow),
        ),
    )
    late_loads = loading(
        3,
        (
            (vel_in, vel), (depth_in, depth), (sea_in, sea), (uplift_in, uplift),
            (lift_in, lift), (flux_in, flux), (felem_in, felem), (fslip_in, fslip),
        ),
    )
    barrier = pltpu.get_barrier_semaphore()

    def greet(dm, ds):
        pl.semaphore_signal(barrier, inc=1, device_id=device(dm, ds), device_id_type=MESH)

    order = sorted(range(1, sub_count), key=lambda k: -min(k, sub_count - k))
    for k in order:
        greet(0, k)
    for load in loads[0:4]:
        load.start()
    for side in (1, -1):

        @pl.when(neighbour[side])
        def _():
            for ds in [*order, 0]:
                greet(side, ds)

    for load in loads[4:]:
        load.start()

    def start(group, copies):
        for side in (0, 1, -1):
            some = [copy for copy in copies if copy[0] == side]

            def go():
                for dm, ds, src, dst in some:
                    pltpu.make_async_remote_copy(
                        src_ref=src, dst_ref=dst,
                        send_sem=load_sem.at[3 * group + side % 3],
                        recv_sem=recv_sem.at[3 * group + side % 3],
                        device_id=device(dm, ds), device_id_type=MESH,
                    ).start()

            if side == 0:
                go()
            elif some:
                pl.when(neighbour[side])(go)

    def await_all(sem, whole):
        pltpu.make_async_copy(whole, whole, sem).wait()

    def sent(group, along, across):
        if along is not None:
            await_all(load_sem.at[3 * group], along)
        for side in (1, -1):
            if across is not None:
                pl.when(neighbour[side])(
                    functools.partial(await_all, load_sem.at[3 * group + side % 3], across)
                )

    def received(group, along, across):
        if along is not None:
            await_all(recv_sem.at[3 * group], along)
        for side in (1, -1):
            if across is not None:
                pl.when(neighbour[-side])(
                    functools.partial(await_all, recv_sem.at[3 * group + side % 3], across)
                )

    def keep_own(group, src, dst):
        pltpu.make_async_copy(src, dst, recv_sem.at[3 * group]).start()

    lane = iota((1, padded), 1)
    of_quantity = sum((lane >= basis * k).astype(I32) for k in range(1, quantities + 1))
    of_basis = lane - basis * of_quantity
    half_row = iota((LANES, padded), 0) & (LANES // 2 - 1)
    spread_basis = ((half_row == of_basis) & (lane < width)).astype(F32).astype(BF16)
    spread_quantity = ((iota((48, padded), 0) & 15) == of_quantity).astype(F32).astype(BF16)
    for load in loads:
        load.wait()
    for load in late_loads:
        load.start()
    stiff_hi, stiff_lo = split(
        jnp.concatenate([stiff[...], jnp.zeros((3 * basis, LANES // 2 - basis), F32)], 1)
    )
    spread[...] = mm(
        jnp.concatenate([stiff_hi, stiff_lo], 1), spread_basis
    )
    jac_wide = []
    for d in range(3):
        rest, jac_parts = jnp.concatenate([jac[:, d, :], jnp.zeros((16 - quantities, quantities), F32)], 0), []
        for _ in range(3):
            part = rest.astype(BF16)
            rest = rest - part.astype(F32)
            jac_parts.append(part)
        jac_wide.append(mm(jnp.concatenate(jac_parts, 0), spread_quantity, 0, 0))

    def matrix_rows(q):
        if q == quantities:
            return jnp.zeros((padded - width, padded), F32)
        block = spread[0:basis, :] * jac_wide[0][q : q + 1]
        for d in (1, 2):
            block = block + spread[d * basis : (d + 1) * basis, :] * jac_wide[d][q : q + 1]
        return block

    at = 0
    for q in range(0, quantities, 2):
        high, low = split(jnp.concatenate([matrix_rows(q), matrix_rows(q + 1)], 0))
        matrix_hi[at : at + high.shape[0], :] = high
        matrix_lo[at : at + high.shape[0], :] = low
        at = at + high.shape[0]

    scale = scales[...]

    def derivative(x):
        x_hi, x_lo = split(x)
        both = mm(matrix_hi[...], jnp.concatenate([x_hi, x_lo], 1))
        return (both[:, :elements] + both[:, elements:] + mm(matrix_lo[...], x_hi)) * scale

    start_state = jnp.concatenate([state[...], jnp.zeros((padded - width, elements), F32)], 0)
    current = derivative(start_state)
    factor = EARTH_STEP * EARTH_STEP / 2
    integral = EARTH_STEP * start_state + factor * current

    codes = jnp.concatenate(
        [as_column(ref[...].astype(F32)) for ref in (psend, esend, precv, erecv)], 0
    )
    face_lane = iota((1, 4 * elements), 1)
    key = (4 * (face_lane & (elements - 1)) + face_lane // elements).astype(F32)
    hot[...] = (codes == key).astype(F32).astype(BF16)
    faces[...] = jnp.zeros(faces.shape, F32)
    for f in range(4):
        for half in (0, LANES // 2):
            faces[f * FACE_ROWS : f * FACE_ROWS + proj.shape[0], half : half + basis] = proj[:, f, :]
    faces_hi, faces_lo = split(faces[...])
    faces_lo = faces_lo[:, 0 : LANES // 2]

    fault_count = fdest.shape[1]
    square = (fault_count, fault_count)
    dest_row = fdest[...].astype(F32)
    dest_col = as_column(dest_row)
    same = dest_col == dest_row
    rank_row = jnp.sum(
        jnp.where(same & (iota(square, 0) < iota(square, 1)), 1.0, 0.0), axis=0, keepdims=True
    )
    rank_col = jnp.sum(
        jnp.where(same & (iota(square, 1) < iota(square, 0)), 1.0, 0.0), axis=1, keepdims=True
    )
    row_numbers = frow[...].astype(F32) + 1.0
    info_row = iota((peer_total, 1), 0)
    info_turn = info_row & (slots - 1)
    info_dest = info_row // slots + jnp.where(
        info_turn == TURN_LOW, -1, jnp.where(info_turn == TURN_HIGH, 1, 0)
    )
    info_left = jnp.where(dest_row == info_dest.astype(F32), row_numbers, 0.0)
    info_lane = INFO % LANES
    info_right = (
        rank_col == (iota((fault_count, LANES), 1) - info_lane).astype(F32)
    ).astype(F32)
    info = mm(info_left.astype(BF16), info_right.astype(BF16)) - 1.0
    info_lanes = iota((peer_total, LANES), 1)
    info_here = (info_lanes >= info_lane) & (info_lanes < info_lane + CAP)

    for power in range(2, ORDER):
        current = derivative(current)
        factor = factor * EARTH_STEP / (power + 1)
        integral = integral + factor * current

    parts = jnp.concatenate(
        [
            jnp.concatenate(
                [
                    integral[p * basis : (p + 1) * basis],
                    jnp.zeros((LANES // 2 - basis, elements), F32),
                ],
                0,
            )
            for p in range(quantities)
        ],
        1,
    )
    parts_hi, parts_lo = split(parts)
    every = mm(faces_hi, jnp.concatenate([parts_hi, parts_lo], 0)) + mm(faces_lo, parts_hi)
    face_width = quantities * FACE_ROWS
    trace_rows = traces_out.shape[1]

    def face_block(f, q):
        return every[f * FACE_ROWS : (f + 1) * FACE_ROWS, q * elements : (q + 1) * elements]

    table = jnp.concatenate(
        [jnp.concatenate([face_block(f, q) for q in range(quantities)], 0) for f in range(4)], 1
    )
    table = jnp.concatenate([table, jnp.zeros((trace_rows - face_width, 4 * elements), F32)], 0)
    deep_half = 2 * elements
    tables = [split(table[:, 0:deep_half]), split(table[:, deep_half:])]

    def pick(rows):
        return sum(
            mm(hot[rows, i * deep_half : (i + 1) * deep_half], part, 1, 1)
            for i in (0, 1)
            for part in tables[i]
        )

    picked = pick(slice(0, send_total))
    traces_out[:, 0:LANES] = picked[:, 0:LANES]
    traces_out[0:peer_total, LANES:] = jnp.where(info_here, info, picked[0:peer_total, LANES:])
    traces_out[peer_total:, LANES:] = picked[peer_total:, LANES:]

    def peer_block(index, rows):
        return pl.ds(pl.multiple_of(index * rows, rows), rows)

    trace_copies = []
    for k in order:
        _, peer = device(0, k)
        trace_copies.append(
            (
                0, k,
                traces_out.at[peer_block(peer, slots), :], traces_in.at[peer_block(sub, slots), :],
            )
        )
    for dm in (1, -1):
        source = peer_total + (edge_slots if dm > 0 else 0)
        target = peer_total + (0 if dm > 0 else edge_slots)
        trace_copies.append(
            (
                dm, 0,
                traces_out.at[source : source + edge_slots, :],
                traces_in.at[target : target + edge_slots, :],
            )
        )
    pl.semaphore_wait(
        barrier,
        sub_count - 1 + sub_count * (neighbour[1].astype(I32) + neighbour[-1].astype(I32)),
    )
    start(TRACES, trace_copies)
    keep_own(
        TRACES, traces_out.at[peer_block(sub, slots), :], traces_in.at[peer_block(sub, slots), :]
    )

    own_trace = pick(slice(send_total, 2 * send_total))

    for load in late_loads:
        load.wait()
    for i, first in enumerate((tile_rows - 8, 0)):
        rows_out[i, 0:2] = vel[:, first : first + 8, :]
        rows_out[i, 2] = depth[first : first + 8, :]
        rows_out[i, 3] = sea[first : first + 8, :]
    fields = (vel[0], vel[1], depth[...], sea[...])
    group = RIM * (tile_rows // 8)
    for i, last in enumerate((True, False)):
        packed = pack_edge(fields[0], last, 0)
        for k in (1, 2, 3):
            packed = packed + pack_edge(fields[k], last, k * group)
        cols_out[i] = packed

    rim_copies = []
    for i, (dm, ds) in enumerate(DIRECTIONS):
        if ds == 0:
            src, dst = rows_out.at[i], rows_in.at[i]
        elif dm == 0:
            src, dst = cols_out.at[i - 2], cols_in.at[i - 2]
        else:
            lanes = slice(tile_cols - LANES, tile_cols) if ds > 0 else slice(0, LANES)
            src, dst = rows_out.at[0 if dm > 0 else 1, :, :, lanes], corner_in.at[i - 4]
        rim_copies.append((dm, ds, src, dst))
    start(FIELDS, rim_copies)

    base = start_state + derivative(integral)
    lifts[...] = jnp.zeros(lifts.shape, F32)
    for f in range(4):
        for at in (0, LANES // 2):
            lifts[f * FACE_ROWS : f * FACE_ROWS + lift.shape[0], at : at + basis] = lift[:, f, :]
    lift_hi, lift_lo = split(jnp.transpose(lifts[...])[0:basis])
    lift_hi = jnp.concatenate([lift_hi, lift_hi], 1)
    hot_in = hot[send_total:, :]

    face_col, face_row = iota((trace_rows, 1), 0), iota((1, trace_rows), 1)
    quantity_col = sum((face_col >= FACE_ROWS * k).astype(I32) for k in range(1, quantities + 1))
    quantity_row = sum((face_row >= FACE_ROWS * k).astype(I32) for k in range(1, quantities + 1))
    exact = functools.partial(
        lax.dot_general, precision=lax.Precision.HIGHEST, preferred_element_type=F32
    )
    flux_left = exact(
        (quantity_col == iota((trace_rows, quantities), 1)).astype(F32), flux[...],
        (((1,), (1,)), ((), ())),
    )
    flux_wide = exact(
        flux_left, (quantity_row == iota((quantities, trace_rows), 0)).astype(F32),
        (((1,), (0,)), ((), ())),
    )
    same_face = face_col - FACE_ROWS * quantity_col == face_row - FACE_ROWS * quantity_row
    flux_wide = jnp.where(same_face, flux_wide, 0.0)
    flux_hi, flux_lo = split(flux_wide)

    rows_here = iota((padded, 1), 0)
    row_quantity = sum((rows_here >= basis * k).astype(I32) for k in range(1, quantities + 1))
    wanted = (rows_here - basis * row_quantity) * quantities + row_quantity
    wanted = jnp.where(rows_here < width, wanted, -1)
    permute = (iota((padded, width), 1) == wanted).astype(F32).astype(BF16)
    uplift_hi, uplift_lo = split(uplift[...])
    uplift_hi, uplift_lo = mm(permute, uplift_hi), mm(permute, uplift_lo)
    uplift_all = uplift_hi + uplift_lo
    uplift_hi, uplift_lo = uplift_hi.astype(BF16), uplift_lo.astype(BF16)

    wide_hi, wide_lo = split(
        jnp.concatenate(
            [
                jnp.concatenate(
                    [
                        uplift_all[q * basis : (q + 1) * basis],
                        jnp.zeros((LANES // 2 - basis, tile_cols), F32),
                    ],
                    0,
                )
                for q in range(quantities)
            ],
            1,
        )
    )
    down_hi, down_lo = split(lifts[...])
    faces_up = mm(down_hi, jnp.concatenate([wide_hi, wide_lo], 0))
    faces_up = faces_up + mm(down_lo[:, 0 : LANES // 2], wide_hi)
    back_hi, back_lo = split(jnp.transpose(flux_wide))
    for f in range(4):
        rows = [
            faces_up[f * FACE_ROWS : (f + 1) * FACE_ROWS, q * tile_cols : (q + 1) * tile_cols]
            for q in range(quantities)
        ]
        rows.append(jnp.zeros((trace_rows - face_width, tile_cols), F32))
        rows_hi, rows_lo = split(jnp.concatenate(rows, 0))
        block = mm(back_hi, rows_hi) + mm(back_lo, rows_hi) + mm(back_hi, rows_lo)
        high, low = split(block)
        mixing_hi[f * trace_rows : (f + 1) * trace_rows, :] = high
        mixing_lo[f * trace_rows : (f + 1) * trace_rows, :] = low

    item_slots = sub_count * CAP
    place = (
        iota((item_slots, fault_count), 0).astype(F32) == dest_row * float(CAP) + rank_row
    ).astype(F32)
    elem_col = as_column(felem[...].astype(F32))
    elem_hot = (elem_col == iota((fault_count, elements), 1).astype(F32)).astype(F32)
    elem_hot = elem_hot.astype(BF16)
    choose = mm(place.astype(BF16), elem_hot).astype(BF16)
    weighting = 0.3 + 0.7 * fslip[...].astype(F32)
    weight_col = jnp.sum(place * weighting, axis=1, keepdims=True)
    rim_total = 2 * sub_count * RIM
    rim_row = iota((rim_total, 1), 0)
    rim_turn = rim_row & (RIM - 1)
    upward = rim_row >= rim_total // 2
    rim_target = jnp.where(
        upward,
        jnp.where(rim_turn > 0, tile_rows - RIM + rim_turn, -1),
        jnp.where(rim_turn < RIM - 1, rim_turn, -1),
    )
    rim_dest = (rim_row & (rim_total // 2 - 1)) // RIM
    rim_weight = jnp.where(
        (dest_row == rim_dest.astype(F32)) & (frow[...] == rim_target), weighting, 0.0
    )
    rim_hi, rim_lo = split(rim_weight)
    rim_hi, rim_lo = split(mm(rim_hi, elem_hot) + mm(rim_lo, elem_hot))

    base_hi, base_lo = split(base)
    both = jnp.concatenate([choose, rim_hi], 0)
    columns = mm(jnp.concatenate([both, both], 1), jnp.concatenate([base_hi, base_lo], 1), 1, 1)
    columns = jnp.concatenate(
        [columns[:item_slots], columns[item_slots:] + mm(rim_lo, base_hi, 1, 1)], 0
    )
    columns_hi, columns_lo = split(columns)
    known[...] = mm(columns_hi, uplift_hi) + mm(columns_lo, uplift_hi) + mm(columns_hi, uplift_lo)
    in_codes = codes[send_total:].astype(I32)
    in_elem = jnp.where(in_codes >= 0, in_codes >> 2, -1)
    in_hot = (in_elem == iota((send_total, elements), 1)).astype(F32).astype(BF16)
    touch = mm(choose, in_hot, 1, 1).astype(BF16)
    touch_hi, touch_lo = split(mm(rim_hi, in_hot, 1, 1) + mm(rim_lo, in_hot, 1, 1))
    touch = jnp.concatenate([touch, touch_hi], 0)
    touch = jnp.concatenate([touch, touch], 1)
    turns = [
        jnp.broadcast_to(((in_codes >= 0) & ((in_codes & 3) == f)).astype(F32), own_trace.shape)
        .astype(BF16)
        for f in range(4)
    ]

    received(TRACES, traces_in.at[0:peer_total, :], traces_in.at[0:edge_slots, :])
    slot_col = iota((send_total, 1), 0)
    missing = ((slot_col >= peer_total) & (slot_col < peer_total + edge_slots) & (me == 0)) | (
        (slot_col >= peer_total + edge_slots) & (me == mesh_count - 1)
    )
    difference = jnp.where(missing, 0.0, traces_in[...]) - own_trace
    diff_hi, diff_lo = split(difference)
    turned_hi = jnp.concatenate([diff_hi * turn for turn in turns], 1)
    turned_lo = jnp.concatenate([diff_lo * turn for turn in turns], 1)
    each = mm(jnp.concatenate([turned_hi, turned_lo], 0), mixing_hi[...])
    each = each[:send_total] + each[send_total:] + mm(turned_hi, mixing_lo[...])
    each_hi, each_lo = split(each)
    uplifted = known[...] + mm(touch, jnp.concatenate([each_hi, each_lo], 0))
    uplifted = jnp.concatenate(
        [uplifted[:item_slots], uplifted[item_slots:] + mm(touch_lo, each_hi)], 0
    )
    rims = uplifted[item_slots:]
    half = rim_total // 2
    rim_lane = iota((half, LANES), 1)
    for i, (part, high_shift, low_shift) in enumerate(
        ((rims[:half], -RIM, RIM), (rims[half:], 1 - 2 * RIM, 1))
    ):
        corner = []
        for shift, tile in (
            (high_shift, jnp.where(rim_lane < RIM - 1, part[:, 0:LANES], 0.0)),
            (low_shift, jnp.where(rim_lane > LANES - RIM, part[:, tile_cols - LANES :], 0.0)),
        ):
            tile = pltpu.roll(tile, 0, 1, stride=8, stride_axis=0)
            tile = tile + pltpu.roll(tile, 1, 0)
            tile = tile + pltpu.roll(tile, 2, 0)
            corner.append(pltpu.roll(tile, shift % half, 0))
        free = (iota((half, LANES), 0) & (RIM - 1)) == (0 if i else RIM - 1)
        first = jnp.where(free, corner[0] + corner[1], part[:, 0:LANES])
        for d in range(sub_count):
            rims_out[i, d, :, 0:LANES] = first[d * RIM : (d + 1) * RIM]
            rims_out[i, d, :, LANES:] = part[d * RIM : (d + 1) * RIM, LANES:]

    rim_copies = []
    for k in [*order, 0]:
        _, peer = device(0, k)
        for i, dm in enumerate((-1, 1)):
            rim_copies.append((dm, k, rims_out.at[i, peer], rims_in.at[i, sub]))
    start(RIMS, rim_copies)
    items = uplifted[:item_slots] * weight_col
    items_out[...] = items
    start(
        ITEMS,
        [
            (
                0, k,
                items_out.at[peer_block(device(0, k)[1], CAP), :],
                items_in.at[peer_block(sub, CAP), :],
            )
            for k in order
        ],
    )
    keep_own(ITEMS, items_out.at[peer_block(sub, CAP), :], items_in.at[peer_block(sub, CAP), :])
    side_lane = iota((CAP, LANES), 1)
    firsts, lasts = [], []
    for d in range(sub_count):
        own = items[d * CAP : (d + 1) * CAP]
        first = jnp.where(side_lane < RIM - 1, own[:, 0:LANES], 0.0)
        last = jnp.where(side_lane > LANES - RIM, own[:, tile_cols - LANES :], 0.0)
        first = pltpu.roll(first, 0, 1, stride=RIM, stride_axis=0)
        last = pltpu.roll(last, LANES // 2 + RIM - 1, 1, stride=RIM, stride_axis=0)
        firsts.append(jnp.sum(first, axis=0, keepdims=True))
        lasts.append(jnp.sum(last, axis=0, keepdims=True))
    for d in range(sub_count):
        sides_out[d] = firsts[(d + 1) % sub_count] + lasts[(d - 1) % sub_count]
    start(
        SIDES, [(0, k, sides_out.at[device(0, k)[1]], sides_in.at[sub]) for k in order]
    )
    keep_own(SIDES, sides_out.at[sub], sides_in.at[sub])

    mixed = mm(flux_hi, jnp.concatenate([diff_hi, diff_lo], 0), 1, 1)
    mixed = mixed[:, :send_total] + mixed[:, send_total:] + mm(flux_lo, diff_hi, 1, 1)
    scattered = mm(jnp.concatenate(split(mixed), 1), jnp.concatenate([hot_in, hot_in], 0))
    gathered = jnp.concatenate(
        [
            jnp.concatenate(
                [
                    scattered[q * FACE_ROWS : (q + 1) * FACE_ROWS, f * elements : (f + 1) * elements]
                    for f in range(4)
                ],
                0,
            )
            for q in range(quantities)
        ],
        1,
    )
    gathered_hi, gathered_lo = split(gathered)
    lifted = mm(lift_hi, jnp.concatenate([gathered_hi, gathered_lo], 0)) + mm(lift_lo, gathered_hi)
    face_sum = jnp.concatenate(
        [lifted[:, q * elements : (q + 1) * elements] for q in range(quantities)]
        + [jnp.zeros((padded - width, elements), F32)],
        0,
    )
    new_out[...] = (base + face_sum)[0:width]

    got_info = traces_in[0:peer_total, LANES:]

    def landing(turn, backward=False):
        rows = jnp.concatenate(
            [got_info[s * slots + turn : s * slots + turn + 1] for s in range(sub_count)], 0
        )
        column = as_column(rows, info_lane, backward)
        hits = (column == iota((item_slots, LANES), 1).astype(F32)).astype(F32)
        return jnp.transpose(hits)[0:tile_rows].astype(BF16)

    land = landing(0)
    land = jnp.concatenate([land, land], 1)
    land_high, land_low = landing(TURN_HIGH, True), landing(TURN_LOW, True)
    land_side = jnp.concatenate([land_high, land_low, land_high, land_low], 1)

    received(FIELDS, cols_in, rows_in)

    def corners_of(k):
        return [
            corner_in[WAY[way] - 4, k] for way in ((-1, -1), (-1, 1), (1, -1), (1, 1))
        ]

    extended = [
        extend(
            fields[k], rows_in[WAY[(1, 0)], k], rows_in[WAY[(-1, 0)], k],
            cols_in[0], cols_in[1], corners_of(k), k * group,
        )
        for k in range(4)
    ]
    shape = extended[0].shape
    ext_row, ext_lane = iota(shape, 0), iota(shape, 1)
    inside = (
        ((ext_row < tile_rows) | (ext_row >= tile_rows + RIM) | neighbour[1])
        & ((ext_row < tile_rows + RIM) | neighbour[-1])
        & ((ext_lane < tile_cols) | (ext_lane >= tile_cols + LANES // 2) | (sub < sub_count - 1))
        & ((ext_lane < tile_cols + LANES // 2) | (sub > 0))
    )
    flow = [jnp.where(inside, extended[axis], 0.0) for axis in (0, 1)]
    deep = jnp.where(inside, extended[2], 0.0)
    calm = jnp.where(inside, extended[3], 0.0) - COURANT * (
        shifted(deep * flow[0], 0) + shifted(deep * flow[1], 1)
    )
    sent(TRACES, traces_out.at[0 : peer_total - slots, :], traces_out.at[0:edge_slots, :])
    sent(FIELDS, cols_out, rows_out)

    received(RIMS, None, rims_in.at[0])
    bottom = []
    for i in (0, 1):
        total = rims_in[i, 0]
        for s in range(1, sub_count):
            total = total + rims_in[i, s]
        bottom.append(total)
    bottom = jnp.concatenate(bottom, 0)
    bottom_lane, bottom_row = iota((8, LANES), 1), iota((8, LANES), 0)
    corner = []
    for free in (RIM - 1, RIM):
        wide = jnp.broadcast_to(bottom[free : free + 1, 0:LANES], (8, LANES))
        around = []
        for turn in (1, -1):
            tile = pltpu.roll(wide, lax.rem(8 * LANES - 8 * RIM * (sub + turn), LANES), 1)
            rows = tile
            for r in range(1, RIM):
                rows = jnp.where(
                    (bottom_row & (RIM - 1)) == r, pltpu.roll(tile, LANES - 8 * r, 1), rows
                )
            around.append(rows)
        corner.append(jnp.where(bottom_lane < LANES // 2, around[0], around[1]))
    corner = jnp.where(bottom_row < RIM, corner[0], corner[1])
    received(SIDES, sides_in, None)
    received(ITEMS, items_in, None)
    beside = []
    last_turn = LANES - RIM * (CAP - 1)
    for shift, keep in (
        (last_turn, side_lane < RIM - 1),
        (last_turn + LANES // 2 - RIM + 1, side_lane > LANES - RIM),
    ):
        for s in range(sub_count):
            wide = jnp.broadcast_to(sides_in[s], (CAP, LANES))
            wide = pltpu.roll(wide, shift % LANES, 1, stride=RIM, stride_axis=0)
            beside.append(jnp.where(keep, wide, 0.0))
    beside_hi, beside_lo = split(jnp.concatenate(beside, 0))
    side = mm(land_side, jnp.concatenate([beside_hi, beside_lo], 0))
    deposit = mm(land, jnp.concatenate(split(items_in[...]), 0))
    raised = jnp.concatenate(
        [jnp.concatenate([deposit, side], 1), jnp.concatenate([bottom, corner], 1)], 0
    )

    level = calm + jnp.where(inside, raised, 0.0)
    flow = [flow[axis] - COURANT * shifted(level, axis) for axis in (0, 1)]
    level = jnp.where(inside, level, 0.0)
    level = level - COURANT * (shifted(deep * flow[0], 0) + shifted(deep * flow[1], 1))
    flow = [flow[axis] - COURANT * shifted(level, axis) for axis in (0, 1)]
    sea_out[...] = level[0:tile_rows, 0:tile_cols]
    flow_out[0] = flow[0][0:tile_rows, 0:tile_cols]
    flow_out[1] = flow[1][0:tile_rows, 0:tile_cols]
    sent(RIMS, None, rims_out.at[0])
    sent(ITEMS, items_out.at[0 : item_slots - CAP, :], None)
    sent(SIDES, sides_out.at[0 : sub_count - 1], None)


def store_kernel(new_in, sea_in, flow_in, new_out, sea_out, flow_out, sems):
    copies = [
        pltpu.make_async_copy(src, dst, sems.at[i])
        for i, (src, dst) in enumerate(
            ((new_in, new_out), (sea_in, sea_out), (flow_in, flow_out))
        )
    ]
    for copy in copies:
        copy.start()
    for copy in copies:
        copy.wait()


def body(mesh_count, sub_count, *arguments):
    (
        state, scales, stiffness, jacobians, projection, lifting, flux_matrix,
        peer_send, peer_recv, edge_send, edge_recv, uplift_map,
        fault_elem, fault_dest, fault_row, fault_slip, sea_level, velocity, depth,
    ) = arguments
    basis, quantities, elements = state.shape
    width = basis * quantities
    faults = fault_elem.shape[0]
    rows, cols = sea_level.shape
    slots, edge_slots = peer_send.shape[2], edge_send.shape[2]
    operands = (
        jnp.transpose(state, (1, 0, 2)).reshape(width, elements),
        scales.reshape(1, elements),
        stiffness.reshape(3 * basis, basis),
        jnp.transpose(jacobians, (1, 0, 2)),
        jnp.transpose(projection, (1, 0, 2)),
        jnp.transpose(lifting, (2, 0, 1)),
        flux_matrix,
        peer_send.reshape(sub_count, slots),
        peer_recv.reshape(sub_count, slots),
        edge_send.reshape(2, edge_slots),
        edge_recv.reshape(2, edge_slots),
        uplift_map,
        fault_elem.reshape(1, faults),
        fault_dest.reshape(1, faults),
        fault_row.reshape(1, faults),
        fault_slip.reshape(1, faults),
        sea_level,
        velocity,
        depth,
    )
    padded = -(-width // LANES) * LANES
    trace_lanes = 2 * LANES
    send_total = sub_count * slots + 2 * edge_slots
    item_slots = sub_count * CAP
    vmem, dma = pltpu.VMEM, pltpu.SemaphoreType.DMA
    held = [vmem(x.shape, x.dtype) for x in operands]
    scratch = held + [
        vmem((3 * basis, padded), F32),
        vmem((padded, padded), BF16),
        vmem((padded, padded), BF16),
        vmem((2 * send_total, 4 * elements), BF16),
        vmem((4 * FACE_ROWS, LANES), F32),
        vmem((4 * FACE_ROWS, LANES), F32),
        vmem((send_total, trace_lanes), F32),
        vmem((send_total, trace_lanes), F32),
        vmem((item_slots, cols), F32),
        vmem((item_slots, cols), F32),
        vmem((2, 4, 8, cols), F32),
        vmem((2, 8, LANES), F32),
        vmem((2, 4, 8, cols), F32),
        vmem((2, 8, LANES), F32),
        vmem((4, 4, 8, LANES), F32),
        vmem((2, sub_count, RIM, cols), F32),
        vmem((2, sub_count, RIM, cols), F32),
        vmem((sub_count, 1, LANES), F32),
        vmem((sub_count, 1, LANES), F32),
        vmem((item_slots + 2 * sub_count * RIM, cols), F32),
        vmem((4 * trace_lanes, cols), BF16),
        vmem((4 * trace_lanes, cols), BF16),
        dma((11,)),
        dma((10,)),
    ]
    hbm, local = pl.BlockSpec(memory_space=pltpu.HBM), pl.BlockSpec(memory_space=pltpu.VMEM)
    shapes = ((width, elements), (rows, cols), (2, rows, cols))
    results = pl.pallas_call(
        functools.partial(kernel, mesh_count, sub_count),
        out_shape=tuple(vmem(shape, F32) for shape in shapes),
        in_specs=[hbm] * len(operands),
        out_specs=(local,) * 3,
        scratch_shapes=scratch,
        compiler_params=pltpu.CompilerParams(
            collective_id=0, has_side_effects=True, vmem_limit_bytes=40 * 1024 * 1024
        ),
    )(*[pltpu.with_memory_space_constraint(x, pltpu.HBM) for x in operands])
    new_state, sea_out, flow_out = pl.pallas_call(
        store_kernel,
        out_shape=tuple(pltpu.HBM(shape, F32) for shape in shapes),
        in_specs=[local] * 3,
        out_specs=(hbm,) * 3,
        scratch_shapes=[dma((3,))],
    )(*[pltpu.with_memory_space_constraint(x, pltpu.VMEM) for x in results])
    new_state = jnp.transpose(new_state.reshape(quantities, basis, elements), (1, 0, 2))
    return new_state, sea_out, flow_out


def solution(mesh):
    device = P(("mesh", "sub"))
    return jax.shard_map(
        functools.partial(body, mesh.shape["mesh"], mesh.shape["sub"]),
        mesh=mesh,
        in_specs=(
            P(None, None, ("mesh", "sub")),
            device,
            P(),
            P(),
            P(),
            P(),
            P(),
            P(("mesh", "sub"), None, None),
            P(("mesh", "sub"), None, None),
            P(("mesh", "sub"), None, None),
            P(("mesh", "sub"), None, None),
            P(),
            device,
            P(("mesh", "sub"), None),
            device,
            device,
            P("mesh", "sub"),
            P(None, "mesh", "sub"),
            P("mesh", "sub"),
        ),
        out_specs=(P(None, None, ("mesh", "sub")), P("mesh", "sub"), P(None, "mesh", "sub")),
        check_vma=False,
    )
```
